32 devices in a mesh: stem: 2 (over y), tm: 16 (over z, x, core).
Axes of the slice: x: 2, y: 2, z: 4, core: 2. Of those that a mesh axis runs over, the one named last changes fastest.
Arguments:
- frames: bfloat16 [2, 6144, 1024], P('stem', 'tm'), may hold values from -6 to 6
- timestep: int32 [2], replicated, may hold values from 0 to 49, as said below
- modulation: float32 [50, 6, 1024], replicated, may hold values from -3 to 3
- qkv_self: bfloat16 [1024, 1536], replicated, may hold values from -0.1875 to 0.1875
- out_self: bfloat16 [512, 1024], replicated, may hold values from -0.25 to 0.25
- qk_gain_self: float32 [2, 64], replicated, may hold values from 1.5 to 6
- qkv_cross: bfloat16 [1024, 1536], replicated, may hold values from -0.1875 to 0.1875
- out_cross: bfloat16 [512, 1024], replicated, may hold values from -0.25 to 0.25
- qk_gain_cross: float32 [2, 64], replicated, may hold values from 1.5 to 6
Outputs:
- layer_out: bfloat16 [2, 6144, 1024], P('stem', 'tm')
The draws below stay inside these ranges and needn't reach their ends.
Inputs may be any that keep to these rules, and one draw needn't show every extreme that they name: The stems' timestep indices are distinct, and index 0 and index 49 are always among them.
All inputs are finite; a program needn't handle non-finite values.
Results may differ from the reference program's by a relative error of at most 0.015.
The reference program's roundings to bfloat16 on the way count: a program that leaves them out, or rounds other values in their place, can miss the bound.
Values may be sent and summed in bfloat16 or wider, within the bound.
No kernel may reach another device: no remote copies, remote signals or barrier semaphores. Data moves between devices by JAX's collectives and lax.ppermute only.
A program may use at most 128 MiB of HBM per device.

```python
import math
import jax
import jax.numpy as jnp
from jax import lax

D = 1024
H = 8
HD = 64
HW = 512
HALF = 256
STEPS = 50
STEMS = 2
FRAMES = 6144


def gain_draw(key):
    return jnp.exp(jax.random.uniform(key, (2, HD), jnp.float32, math.log(1.5), math.log(3.5)))


def draw_qk_gain_self(key, part):
    return gain_draw(jax.random.fold_in(key, 11))


def draw_qk_gain_cross(key, part):
    return gain_draw(jax.random.fold_in(key, 23))


def draw_timestep(key, part):
    inner = jax.random.permutation(jax.random.fold_in(key, 37), STEPS - 2)[:STEMS - 2].astype(jnp.int32) + 1
    ends = jnp.array([0, STEPS - 1], dtype=jnp.int32)
    values = jnp.concatenate([ends, inner])
    placing = jax.random.permutation(jax.random.fold_in(key, 41), STEMS)
    return values[placing].astype(jnp.int32)


def shard_levels(stream_key, extent, pieces, low, largest):
    loudness = 1.0
    for axis_at, shards_of in pieces:
        steps = jax.random.uniform(jax.random.fold_in(jax.random.fold_in(stream_key, 6), axis_at), (shards_of,), jnp.float32, low / len(pieces), largest / len(pieces))
        loudness = loudness * jnp.repeat(jnp.exp(steps), extent[axis_at] // shards_of).reshape((-1,) + (1,) * (len(extent) - 1 - axis_at))
    return loudness


def scatter_about(own_key, dims, scale, most, split=(), kind=jnp.bfloat16):
    level = shard_levels(own_key, dims, split, -0.22, 0.18) if split else 1.0
    values = jax.random.normal(own_key, dims, jnp.float32) * scale * level
    return jnp.minimum(jnp.maximum(values, -most), most).astype(kind)


def setup_inputs(seed: int = 0) -> dict:
    seeds = jax.random.split(jax.random.key(seed), 10)
    frames = scatter_about(seeds[0], (STEMS, FRAMES, D), 1.0, 6.0, ((0, 2), (1, 16)))
    timestep = draw_timestep(jax.random.fold_in(seeds[9], 71), 0)
    modulation = scatter_about(seeds[2], (STEPS, 6, D), 0.5, 3.0, (), jnp.float32)
    qkv_self = scatter_about(seeds[3], (D, 3 * HW), D ** -0.5, 0.1875)
    out_self = scatter_about(seeds[4], (HW, D), HW ** -0.5, 0.25)
    qk_gain_self = draw_qk_gain_self(jax.random.fold_in(seeds[9], 71), 0)
    qkv_cross = scatter_about(seeds[6], (D, 3 * HW), D ** -0.5, 0.1875)
    out_cross = scatter_about(seeds[7], (HW, D), HW ** -0.5, 0.25)
    qk_gain_cross = draw_qk_gain_cross(jax.random.fold_in(seeds[9], 71), 0)
    return {"frames": frames, "timestep": timestep, "modulation": modulation, "qkv_self": qkv_self, "out_self": out_self, "qk_gain_self": qk_gain_self, "qkv_cross": qkv_cross, "out_cross": out_cross, "qk_gain_cross": qk_gain_cross}


EPS = 1e-06
NEG = -1e+30

def rounded(values):
    return lax.optimization_barrier(values.astype(jnp.bfloat16))

def layer_norm(values):
    values = values.astype(jnp.float32)
    centred = values - lax.optimization_barrier(jnp.mean(values, axis=-1, keepdims=True))
    return centred * lax.rsqrt(lax.optimization_barrier(jnp.mean(centred * centred, axis=-1, keepdims=True)) + EPS)

def modulate(values, shift, scale):
    return layer_norm(values) * (1.0 + scale) + shift

def head_norm(values, gain):
    shaped = values.reshape(values.shape[:-1] + (H, HD))
    return shaped * lax.rsqrt(lax.optimization_barrier(jnp.mean(shaped * shaped, axis=-1, keepdims=True)) + EPS) * gain

def split_heads(projected, gains):
    width = H * HD
    query = rounded(head_norm(projected[..., :width], gains[0]))
    keyset = rounded(head_norm(projected[..., width:2 * width], gains[1]))
    valueset = rounded(projected[..., 2 * width:].reshape(projected.shape[:-1] + (H, HD)))
    return (query, keyset, valueset)

def window_stem(query, keyset, valueset):
    block = math.gcd(FRAMES, 512)
    edges = ((HALF, HALF), (0, 0), (0, 0))
    keys_pad = jnp.pad(keyset, edges)
    values_pad = jnp.pad(valueset, edges)

    def one_block(index):
        start = index * block
        q_block = lax.dynamic_slice_in_dim(query, start, block, 0).astype(jnp.float32)
        k_block = lax.dynamic_slice_in_dim(keys_pad, start, block + 2 * HALF, 0).astype(jnp.float32)
        v_block = lax.dynamic_slice_in_dim(values_pad, start, block + 2 * HALF, 0).astype(jnp.float32)
        scores = jnp.einsum('qhd,khd->hqk', q_block, k_block) * HD ** (-0.5)
        q_pos = start + jnp.arange(block, dtype=jnp.int32)
        k_pos = start - HALF + jnp.arange(block + 2 * HALF, dtype=jnp.int32)
        keep = (jnp.abs(q_pos[:, None] - k_pos[None, :]) <= HALF) & (k_pos[None, :] >= 0) & (k_pos[None, :] < FRAMES)
        scores = jnp.where(keep[None], scores, NEG)
        weights = rounded(jax.nn.softmax(scores, axis=-1)).astype(jnp.float32)
        return jnp.einsum('hqk,khd->qhd', weights, v_block)
    blocks = lax.map(one_block, jnp.arange(FRAMES // block, dtype=jnp.int32))
    return rounded(blocks.reshape(FRAMES, H * HD))

def reference(frames, timestep, modulation, qkv_self, out_self, qk_gain_self, qkv_cross, out_cross, qk_gain_cross):
    width = H * HD
    modulations = modulation[timestep][:, :, None, :]
    normed_self = rounded(modulate(frames, modulations[:, 0], modulations[:, 1]))
    projected = jnp.dot(normed_self.reshape(-1, D), qkv_self, preferred_element_type=jnp.float32).reshape(STEMS, FRAMES, 3 * width)
    query, keyset, valueset = split_heads(projected, qk_gain_self)
    attended = lax.map(lambda packed: window_stem(packed[0], packed[1], packed[2]), (query, keyset, valueset))
    mixed = jnp.dot(attended.reshape(-1, width), out_self, preferred_element_type=jnp.float32).reshape(STEMS, FRAMES, D)
    first = rounded(frames.astype(jnp.float32) + modulations[:, 2] * mixed)
    normed_cross = rounded(modulate(first, modulations[:, 3], modulations[:, 4]))
    projected_cross = jnp.dot(normed_cross.reshape(-1, D), qkv_cross, preferred_element_type=jnp.float32).reshape(STEMS, FRAMES, 3 * width)
    q_cross, k_cross, v_cross = split_heads(projected_cross, qk_gain_cross)
    scores = jnp.einsum('sfhd,tfhd->fhst', q_cross.astype(jnp.float32), k_cross.astype(jnp.float32)) * HD ** (-0.5)
    weights = rounded(jax.nn.softmax(scores, axis=-1)).astype(jnp.float32)
    attended_cross = rounded(jnp.einsum('fhst,tfhd->sfhd', weights, v_cross.astype(jnp.float32))).reshape(STEMS * FRAMES, width)
    cross_out = rounded(jnp.dot(attended_cross, out_cross, preferred_element_type=jnp.float32)).reshape(STEMS, FRAMES, D)
    return (first.astype(jnp.float32) + modulations[:, 5] * cross_out.astype(jnp.float32)).astype(jnp.bfloat16)
```

```python
import jax
import jax.numpy as jnp
from jax import lax
from jax.experimental import pallas as pl
from jax.experimental.pallas import tpu as pltpu
from jax.sharding import PartitionSpec as P

D = 1024
H = 8
HD = 64
HW = H * HD
HALF = 256
BLOCK = 128
SLAB = 128
WINDOW = BLOCK + 2 * HALF
EPS = 1e-06
NEG = -1e30
F32 = jnp.float32
BF16 = jnp.bfloat16
VMEM = pl.BlockSpec(memory_space=pltpu.VMEM)
SMEM = pl.BlockSpec(memory_space=pltpu.SMEM)
ANY = pl.BlockSpec(memory_space=pl.ANY)
LIMIT = 48 * 1024 * 1024


def params():
    return pltpu.CompilerParams(vmem_limit_bytes=LIMIT)


def shape(*dims, dtype=BF16):
    return jax.ShapeDtypeStruct(dims, dtype)


def dot(a, b, dims=((1,), (0,))):
    return lax.dot_general(a, b, (dims, ((), ())), preferred_element_type=F32)


def modulated(rows, shift, scale):
    values = rows.astype(F32)
    centred = values - jnp.mean(values, axis=-1, keepdims=True)
    spread = jnp.mean(centred * centred, axis=-1, keepdims=True)
    normed = centred * lax.rsqrt(spread + EPS)
    return (normed * (1.0 + scale) + shift).astype(BF16)


def head_ones():
    row = lax.broadcasted_iota(jnp.int32, (2 * SLAB, 2 * SLAB), 0) // HD
    col = lax.broadcasted_iota(jnp.int32, (2 * SLAB, 2 * SLAB), 1) // HD
    return jnp.where(row == col, 1.0, 0.0).astype(BF16)


def head_sums(values, ones):
    high = values.astype(BF16)
    low = (values - high.astype(F32)).astype(BF16)
    parts = []
    for at in range(0, HW, 2 * SLAB):
        cols = slice(at, at + 2 * SLAB)
        parts.append(dot(high[:, cols], ones) + dot(low[:, cols], ones))
    return jnp.concatenate(parts, axis=1)


def head_norm(values, gain, ones):
    mean = head_sums(values * values, ones) * (1.0 / HD)
    return (values * lax.rsqrt(mean + EPS) * gain).astype(BF16)


def wide_gain(gain):
    return jnp.concatenate([gain] * H, axis=1)


def window_bias(first_key, total):
    i = lax.broadcasted_iota(jnp.int32, (BLOCK, WINDOW), 0)
    j = lax.broadcasted_iota(jnp.int32, (BLOCK, WINDOW), 1)
    frame = first_key + j
    keep = (j >= i) & (j <= i + 2 * HALF) & (frame >= 0) & (frame < total)
    return jnp.where(keep, 0.0, NEG)


def window_block(query, keys, values, bias):
    half = lax.broadcasted_iota(jnp.int32, (BLOCK, SLAB), 1) < HD
    ones = jnp.ones((WINDOW, SLAB), BF16)
    outs = []
    for at in range(0, HW, SLAB):
        cols = slice(at, at + SLAB)
        q = query(cols)
        zero = jnp.zeros_like(q)
        pair = jnp.concatenate([jnp.where(half, q, zero), jnp.where(half, zero, q)], axis=0)
        scores = dot(pair, keys(cols), ((1,), (1,)))
        scores = jnp.concatenate([scores[:BLOCK] + bias, scores[BLOCK:] + bias], axis=0)
        top = jnp.max(scores, axis=-1, keepdims=True)
        raised = jnp.exp(scores - top).astype(BF16)
        summed = dot(raised, jnp.concatenate([values(cols), ones], axis=1))
        out = summed[:, :SLAB] / summed[:, SLAB:]
        outs.append(jnp.where(half, out[:BLOCK], out[BLOCK:]).astype(BF16))
    return jnp.concatenate(outs, axis=1)


def cross_attend(query, keys, values, ones):
    query = query.astype(F32)
    scores = [head_sums(query * k.astype(F32), ones) * (HD ** -0.5) for k in keys]
    top = scores[0]
    for s in scores[1:]:
        top = jnp.maximum(top, s)
    raised = [jnp.exp(s - top) for s in scores]
    total = raised[0]
    for r in raised[1:]:
        total = total + r
    scale = 1.0 / total
    out = jnp.zeros_like(query)
    for r, v in zip(raised, values):
        out = out + (r * scale).astype(BF16).astype(F32) * v.astype(F32)
    return out.astype(BF16)


def blocks(rows):
    return [slice(at, min(at + BLOCK, rows)) for at in range(0, rows, BLOCK)]


def mod_copy(timestep, modulation, row, held, sem):
    return pltpu.make_async_copy(modulation.at[timestep[row]], held, sem)


def split_kernel(frames, near, far, sems):
    parity = lax.rem(lax.axis_index("tm"), 2)
    rows = frames.shape[1]
    near_at = pl.multiple_of((1 - parity) * (rows - HALF), BLOCK)
    far_at = pl.multiple_of(parity * (rows - HALF), BLOCK)
    a = pltpu.make_async_copy(frames.at[0, pl.ds(far_at, HALF)], far, sems.at[0])
    b = pltpu.make_async_copy(frames.at[0, pl.ds(near_at, HALF)], near, sems.at[1])
    a.start()
    b.start()
    a.wait()
    b.wait()


def near_kernel(timestep, modulation, frames, near, weight, gains, query, kv, attended, held, sem):
    parity = lax.rem(lax.axis_index("tm"), 2)
    stem = lax.axis_index("stem")
    copy = mod_copy(timestep, modulation, stem, held, sem)
    copy.start()
    copy.wait()
    shift, scale = held[0:1], held[1:2]
    ones = head_ones()
    rows = frames.shape[1]
    q_gain = wide_gain(gains[0:1]) * (HD ** -0.5)
    k_gain = wide_gain(gains[1:2])
    own_at = parity * HALF
    near_at = (1 - parity) * rows

    def keys_values(projected, at, count):
        kv[pl.ds(at, count), :HW] = head_norm(projected[:, :HW], k_gain, ones)
        kv[pl.ds(at, count), HW:] = projected[:, HW:].astype(BF16)

    for part in blocks(rows):
        normed = modulated(frames[0, part], shift, scale)
        projected = dot(normed, weight[...])
        query[part] = head_norm(projected[:, :HW], q_gain, ones)
        keys_values(projected[:, HW:], pl.multiple_of(own_at + part.start, BLOCK), BLOCK)
    for part in blocks(HALF):
        normed = modulated(near[part], shift, scale)
        projected = dot(normed, weight[:, HW:])
        keys_values(projected, pl.multiple_of(near_at + part.start, BLOCK), BLOCK)
    early = pl.multiple_of((1 - parity) * HALF, BLOCK)
    bias = window_bias(HALF, 1 << 30)
    attended[...] = window_block(
        lambda c: query[pl.ds(early, BLOCK), c],
        lambda c: kv[:, c],
        lambda c: kv[:, slice(HW + c.start, HW + c.stop)],
        bias,
    )


def far_kernel(timestep, modulation, far, weight, gains, query, kv, attended, held, full, sem, sem_kv):
    place = lax.axis_index("tm")
    parity = lax.rem(place, 2)
    stem = lax.axis_index("stem")
    copy = mod_copy(timestep, modulation, stem, held, sem)
    copy.start()
    rows = query.shape[0]
    local = rows + HALF
    local_at = pl.multiple_of((1 - parity) * HALF, BLOCK)
    far_at = parity * local
    moved = pltpu.make_async_copy(kv, full.at[pl.ds(local_at, local)], sem_kv)
    moved.start()
    copy.wait()
    shift, scale = held[0:1], held[1:2]
    ones = head_ones()
    k_gain = wide_gain(gains[1:2])
    for part in blocks(HALF):
        at = pl.multiple_of(far_at + part.start, BLOCK)
        normed = modulated(far[part], shift, scale)
        projected = dot(normed, weight[:, HW:])
        full[pl.ds(at, BLOCK), :HW] = head_norm(projected[:, :HW], k_gain, ones)
        full[pl.ds(at, BLOCK), HW:] = projected[:, HW:].astype(BF16)
    moved.wait()
    total = rows * lax.axis_size("tm")
    for part in blocks(HALF):
        at = pl.multiple_of(parity * (rows - HALF) + part.start, BLOCK)
        bias = window_bias(place * rows - HALF + at, total)
        attended[part] = window_block(
            lambda c, at=at: query[pl.ds(at, BLOCK), c],
            lambda c, at=at: full[pl.ds(at, WINDOW), c],
            lambda c, at=at: full[pl.ds(at, WINDOW), slice(HW + c.start, HW + c.stop)],
            bias,
        )


def first_of(frames, attended, weight, gate):
    mixed = dot(attended, weight[...])
    return (frames.astype(F32) + gate * mixed).astype(BF16)


def projected_cross(first, held, weight, gains, ones, with_query):
    normed = modulated(first, held[3:4], held[4:5])
    if with_query:
        projected = dot(normed, weight[...])
        query = head_norm(projected[:, :HW], wide_gain(gains[0:1]), ones)
        projected = projected[:, HW:]
    else:
        projected = dot(normed, weight[:, HW:])
        query = None
    keys = head_norm(projected[:, :HW], wide_gain(gains[1:2]), ones)
    return query, keys, projected[:, HW:].astype(BF16)


def finished(first, attended, weight, gate):
    out = dot(attended, weight[...]).astype(BF16)
    return (first.astype(F32) + gate * out.astype(F32)).astype(BF16)


def mods_of_all(timestep, modulation, held, sems):
    stem = lax.axis_index("stem")
    count = lax.axis_size("stem")
    copies = [
        mod_copy(timestep, modulation, lax.rem(stem + count - k, count), held.at[k], sems.at[k])
        for k in range(count)
    ]
    for copy in copies:
        copy.start()
    for copy in copies:
        copy.wait()


def own_kernel(count, timestep, modulation, frames, early, late, *refs):
    others = refs[: count - 1]
    their_frames = refs[count - 1 : 2 * count - 2]
    out_self, qkv_cross, gains, out_cross, first, qkv, out, held, sems = refs[2 * count - 2 :]
    parity = lax.rem(lax.axis_index("tm"), 2)
    rows = frames.shape[1]
    mods_of_all(timestep, modulation, held, sems)
    ones = head_ones()
    early_at = pl.multiple_of((1 - parity) * HALF, BLOCK)
    late_at = parity * (rows - HALF)
    own = held.at[0]
    for part in blocks(HALF):
        at = pl.multiple_of(late_at + part.start, BLOCK)
        f = first_of(frames[0, pl.ds(at, BLOCK)], late[part], out_self, own[2:3])
        first[part] = f
        q, k, v = projected_cross(f, own, qkv_cross, gains, ones, True)
        qkv[part, :HW] = q
        qkv[part, HW : 2 * HW] = k
        qkv[part, 2 * HW :] = v
    f = first_of(frames[0, pl.ds(early_at, BLOCK)], early[...], out_self, own[2:3])
    q, k, v = projected_cross(f, own, qkv_cross, gains, ones, True)
    keys, values = [k], [v]
    for n, (attended, source) in enumerate(zip(others, their_frames)):
        mods = held.at[n + 1]
        g = first_of(source[0, pl.ds(early_at, BLOCK)], attended[...], out_self, mods[2:3])
        _, k, v = projected_cross(g, mods, qkv_cross, gains, ones, False)
        keys.append(k)
        values.append(v)
    mixed = cross_attend(q, keys, values, ones)
    out[...] = finished(f, mixed, out_cross, own[5:6])


def last_kernel(count, timestep, modulation, first, qkv, early_out, *refs):
    others = refs[: count - 1]
    their_frames = refs[count - 1 : 2 * count - 2]
    out_self, qkv_cross, gains, out_cross, out, held, sems = refs[2 * count - 2 :]
    parity = lax.rem(lax.axis_index("tm"), 2)
    rows = out.shape[1]
    mods_of_all(timestep, modulation, held, sems)
    ones = head_ones()
    early_at = pl.multiple_of((1 - parity) * HALF, BLOCK)
    late_at = parity * (rows - HALF)
    out[0, pl.ds(early_at, rows - HALF)] = early_out[...]
    for part in blocks(HALF):
        at = pl.multiple_of(late_at + part.start, BLOCK)
        keys, values = [qkv[part, HW : 2 * HW]], [qkv[part, 2 * HW :]]
        for n, (attended, source) in enumerate(zip(others, their_frames)):
            mods = held.at[n + 1]
            g = first_of(source[0, pl.ds(at, BLOCK)], attended[part], out_self, mods[2:3])
            _, k, v = projected_cross(g, mods, qkv_cross, gains, ones, False)
            keys.append(k)
            values.append(v)
        mixed = cross_attend(qkv[part, :HW], keys, values, ones)
        out[0, pl.ds(at, BLOCK)] = finished(first[part], mixed, out_cross, held[0, 5:6])


def on_device(
    frames,
    timestep,
    modulation,
    qkv_self,
    out_self,
    qk_gain_self,
    qkv_cross,
    out_cross,
    qk_gain_cross,
):
    stems = lax.axis_size("stem")
    places = lax.axis_size("tm")
    rows = frames.shape[1]
    early = rows - HALF
    assert places % 2 == 0 and early == BLOCK
    inside = [(i, i ^ 1) for i in range(places)]
    across = [(i, i + 1) for i in range(1, places - 1, 2)]
    across += [(b, a) for a, b in across]

    def to_stems(array):
        return [
            lax.ppermute(array, "stem", [(i, (i + k) % stems) for i in range(stems)])
            for k in range(1, stems)
        ]

    near, far = pl.pallas_call(
        split_kernel,
        out_shape=(shape(HALF, D), shape(HALF, D)),
        in_specs=[ANY],
        out_specs=(ANY, ANY),
        scratch_shapes=[pltpu.SemaphoreType.DMA((2,))],
        compiler_params=params(),
        name="split",
    )(frames)
    far = lax.ppermute(far, "tm", across)
    near = lax.ppermute(near, "tm", inside)
    their_frames = to_stems(frames)

    query, kv, attended_early = pl.pallas_call(
        near_kernel,
        out_shape=(shape(rows, HW), shape(rows + HALF, 2 * HW), shape(early, HW)),
        in_specs=[SMEM, ANY, VMEM, VMEM, VMEM, VMEM],
        out_specs=(VMEM, VMEM, VMEM),
        scratch_shapes=[pltpu.VMEM((6, D), F32), pltpu.SemaphoreType.DMA],
        compiler_params=params(),
        name="near",
    )(timestep, modulation, frames, near, qkv_self, qk_gain_self)
    others_early = to_stems(attended_early)

    attended_late = pl.pallas_call(
        far_kernel,
        out_shape=shape(HALF, HW),
        in_specs=[SMEM, ANY, VMEM, VMEM, VMEM, VMEM, ANY],
        out_specs=VMEM,
        scratch_shapes=[
            pltpu.VMEM((6, D), F32),
            pltpu.VMEM((rows + 2 * HALF, 2 * HW), BF16),
            pltpu.SemaphoreType.DMA,
            pltpu.SemaphoreType.DMA,
        ],
        compiler_params=params(),
        name="far",
    )(timestep, modulation, far, qkv_self, qk_gain_self, query, kv)
    others_late = to_stems(attended_late)

    mods = [pltpu.VMEM((stems, 6, D), F32), pltpu.SemaphoreType.DMA((stems,))]
    pairs = 2 * (stems - 1)
    first, qkv, early_out = pl.pallas_call(
        lambda *refs: own_kernel(stems, *refs),
        out_shape=(shape(HALF, D), shape(HALF, 3 * HW), shape(early, D)),
        in_specs=[SMEM, ANY] + [VMEM] * (3 + pairs + 4),
        out_specs=(VMEM, VMEM, VMEM),
        scratch_shapes=mods,
        compiler_params=params(),
        name="own",
    )(
        timestep, modulation, frames, attended_early, attended_late, *others_early, *their_frames,
        out_self, qkv_cross, qk_gain_cross, out_cross,
    )
    return pl.pallas_call(
        lambda *refs: last_kernel(stems, *refs),
        out_shape=shape(1, rows, D),
        in_specs=[SMEM, ANY] + [VMEM] * (3 + pairs + 4),
        out_specs=VMEM,
        scratch_shapes=mods,
        compiler_params=params(),
        name="last",
    )(
        timestep, modulation, first, qkv, early_out, *others_late, *their_frames,
        out_self, qkv_cross, qk_gain_cross, out_cross,
    )


def solution(mesh):
    return jax.shard_map(
        on_device,
        mesh=mesh,
        in_specs=(P("stem", "tm", None), P(), P(), P(), P(), P(), P(), P(), P()),
        out_specs=P("stem", "tm", None),
        check_vma=False,
    )
```

```python
import jax
import jax.numpy as jnp
from jax import lax
from jax.experimental import pallas as pl
from jax.experimental.pallas import tpu as pltpu
from jax.sharding import PartitionSpec as P

D = 1024
H = 8
HD = 64
HW = H * HD
HALF = 256
BLOCK = 128
SLAB = 128
WINDOW = BLOCK + 2 * HALF
EPS = 1e-06
NEG = -1e30
F32 = jnp.float32
BF16 = jnp.bfloat16
VMEM = pl.BlockSpec(memory_space=pltpu.VMEM)
SMEM = pl.BlockSpec(memory_space=pltpu.SMEM)
ANY = pl.BlockSpec(memory_space=pl.ANY)
LIMIT = 16 * 1024 * 1024


def cost(us):
    return pl.CostEstimate(flops=int(us * 1e9), bytes_accessed=int(us * 3e6), transcendentals=0)


def params():
    return pltpu.CompilerParams(vmem_limit_bytes=LIMIT)


def shape(*dims, dtype=BF16):
    return jax.ShapeDtypeStruct(dims, dtype)


def dot(a, b, dims=((1,), (0,))):
    return lax.dot_general(a, b, (dims, ((), ())), preferred_element_type=F32)


def modulated(rows, shift, scale):
    values = rows.astype(F32)
    centred = values - jnp.mean(values, axis=-1, keepdims=True)
    spread = jnp.mean(centred * centred, axis=-1, keepdims=True)
    normed = centred * lax.rsqrt(spread + EPS)
    return (normed * (1.0 + scale) + shift).astype(BF16)


def head_ones():
    row = lax.broadcasted_iota(jnp.int32, (2 * SLAB, 2 * SLAB), 0) // HD
    col = lax.broadcasted_iota(jnp.int32, (2 * SLAB, 2 * SLAB), 1) // HD
    return jnp.where(row == col, 1.0, 0.0).astype(BF16)


def head_sums(values, ones):
    high = values.astype(BF16)
    low = (values - high.astype(F32)).astype(BF16)
    parts = []
    for at in range(0, HW, 2 * SLAB):
        cols = slice(at, at + 2 * SLAB)
        parts.append(dot(high[:, cols], ones) + dot(low[:, cols], ones))
    return jnp.concatenate(parts, axis=1)


def head_norm(values, gain, ones):
    mean = head_sums(values * values, ones) * (1.0 / HD)
    return (values * lax.rsqrt(mean + EPS) * gain).astype(BF16)


def wide_gain(gain):
    return jnp.concatenate([gain] * H, axis=1)


def window_bias(first_key, total):
    i = lax.broadcasted_iota(jnp.int32, (BLOCK, WINDOW), 0)
    j = lax.broadcasted_iota(jnp.int32, (BLOCK, WINDOW), 1)
    frame = first_key + j
    keep = (j >= i) & (j <= i + 2 * HALF) & (frame >= 0) & (frame < total)
    return jnp.where(keep, 0.0, NEG)


def window_block(query, keys, values, bias):
    half = lax.broadcasted_iota(jnp.int32, (BLOCK, SLAB), 1) < HD
    ones = jnp.ones((WINDOW, SLAB), BF16)
    outs = []
    for at in range(0, HW, SLAB):
        cols = slice(at, at + SLAB)
        q = query(cols)
        zero = jnp.zeros_like(q)
        pair = jnp.concatenate([jnp.where(half, q, zero), jnp.where(half, zero, q)], axis=0)
        scores = dot(pair, keys(cols), ((1,), (1,)))
        scores = jnp.concatenate([scores[:BLOCK] + bias, scores[BLOCK:] + bias], axis=0)
        top = jnp.max(scores, axis=-1, keepdims=True)
        raised = jnp.exp(scores - top).astype(BF16)
        summed = dot(raised, jnp.concatenate([values(cols), ones], axis=1))
        out = summed[:, :SLAB] / summed[:, SLAB:]
        outs.append(jnp.where(half, out[:BLOCK], out[BLOCK:]).astype(BF16))
    return jnp.concatenate(outs, axis=1)


def cross_attend(query, keys, values, ones):
    query = query.astype(F32)
    scores = [head_sums(query * k.astype(F32), ones) * (HD ** -0.5) for k in keys]
    top = scores[0]
    for s in scores[1:]:
        top = jnp.maximum(top, s)
    raised = [jnp.exp(s - top) for s in scores]
    total = raised[0]
    for r in raised[1:]:
        total = total + r
    scale = 1.0 / total
    out = jnp.zeros_like(query)
    for r, v in zip(raised, values):
        out = out + (r * scale).astype(BF16).astype(F32) * v.astype(F32)
    return out.astype(BF16)


def blocks(rows):
    return [slice(at, min(at + BLOCK, rows)) for at in range(0, rows, BLOCK)]


def mods_of(timestep, modulation, back):
    count = lax.axis_size("stem")
    step = timestep[lax.rem(lax.axis_index("stem") + count - back, count)]
    return lambda i: modulation[i, pl.ds(step, 1), :]


def split_kernel(frames, near, far, sems):
    parity = lax.rem(lax.axis_index("tm"), 2)
    rows = frames.shape[1]
    near_at = pl.multiple_of((1 - parity) * (rows - HALF), BLOCK)
    far_at = pl.multiple_of(parity * (rows - HALF), BLOCK)
    a = pltpu.make_async_copy(frames.at[0, pl.ds(far_at, HALF)], far, sems.at[0])
    b = pltpu.make_async_copy(frames.at[0, pl.ds(near_at, HALF)], near, sems.at[1])
    a.start()
    b.start()
    a.wait()
    b.wait()


def near_kernel(timestep, modulation, frames, near, weight, gains, query, kv, attended):
    parity = lax.rem(lax.axis_index("tm"), 2)
    mods = mods_of(timestep, modulation, 0)
    shift, scale = mods(0), mods(1)
    ones = head_ones()
    rows = frames.shape[1]
    q_gain = wide_gain(gains[0:1]) * (HD ** -0.5)
    k_gain = wide_gain(gains[1:2])
    own_at = parity * HALF
    near_at = (1 - parity) * rows

    def keys_values(projected, at, count):
        kv[pl.ds(at, count), :HW] = head_norm(projected[:, :HW], k_gain, ones)
        kv[pl.ds(at, count), HW:] = projected[:, HW:].astype(BF16)

    for part in blocks(rows):
        normed = modulated(frames[0, part], shift, scale)
        projected = dot(normed, weight[...])
        query[part] = head_norm(projected[:, :HW], q_gain, ones)
        keys_values(projected[:, HW:], pl.multiple_of(own_at + part.start, BLOCK), BLOCK)
    for part in blocks(HALF):
        normed = modulated(near[part], shift, scale)
        projected = dot(normed, weight[:, HW:])
        keys_values(projected, pl.multiple_of(near_at + part.start, BLOCK), BLOCK)
    early = pl.multiple_of((1 - parity) * HALF, BLOCK)
    bias = window_bias(HALF, 1 << 30)
    attended[...] = window_block(
        lambda c: query[pl.ds(early, BLOCK), c],
        lambda c: kv[:, c],
        lambda c: kv[:, slice(HW + c.start, HW + c.stop)],
        bias,
    )


def far_kernel(timestep, modulation, far, weight, gains, query, kv, attended, full, sem_kv):
    place = lax.axis_index("tm")
    parity = lax.rem(place, 2)
    rows = query.shape[0]
    local = rows + HALF
    local_at = pl.multiple_of((1 - parity) * HALF, BLOCK)
    far_at = parity * local
    moved = pltpu.make_async_copy(kv, full.at[pl.ds(local_at, local)], sem_kv)
    moved.start()
    mods = mods_of(timestep, modulation, 0)
    shift, scale = mods(0), mods(1)
    ones = head_ones()
    k_gain = wide_gain(gains[1:2])
    for part in blocks(HALF):
        at = pl.multiple_of(far_at + part.start, BLOCK)
        normed = modulated(far[part], shift, scale)
        projected = dot(normed, weight[:, HW:])
        full[pl.ds(at, BLOCK), :HW] = head_norm(projected[:, :HW], k_gain, ones)
        full[pl.ds(at, BLOCK), HW:] = projected[:, HW:].astype(BF16)
    moved.wait()
    total = rows * lax.axis_size("tm")
    for part in blocks(HALF):
        at = pl.multiple_of(parity * (rows - HALF) + part.start, BLOCK)
        bias = window_bias(place * rows - HALF + at, total)
        attended[part] = window_block(
            lambda c, at=at: query[pl.ds(at, BLOCK), c],
            lambda c, at=at: full[pl.ds(at, WINDOW), c],
            lambda c, at=at: full[pl.ds(at, WINDOW), slice(HW + c.start, HW + c.stop)],
            bias,
        )


def first_of(frames, attended, weight, gate):
    mixed = dot(attended, weight[...])
    return (frames.astype(F32) + gate * mixed).astype(BF16)


def projected_cross(first, mods, weight, gains, ones, with_query):
    normed = modulated(first, mods(3), mods(4))
    if with_query:
        projected = dot(normed, weight[...])
        query = head_norm(projected[:, :HW], wide_gain(gains[0:1]), ones)
        projected = projected[:, HW:]
    else:
        projected = dot(normed, weight[:, HW:])
        query = None
    keys = head_norm(projected[:, :HW], wide_gain(gains[1:2]), ones)
    return query, keys, projected[:, HW:].astype(BF16)


def finished(first, attended, weight, gate):
    out = dot(attended, weight[...]).astype(BF16)
    return (first.astype(F32) + gate * out.astype(F32)).astype(BF16)


def own_kernel(count, timestep, modulation, frames, early, late, *refs):
    others = refs[: count - 1]
    their_frames = refs[count - 1 : 2 * count - 2]
    out_self, qkv_cross, gains, out_cross, first, qkv, out = refs[2 * count - 2 :]
    parity = lax.rem(lax.axis_index("tm"), 2)
    rows = frames.shape[1]
    all_mods = [mods_of(timestep, modulation, k) for k in range(count)]
    own = all_mods[0]
    ones = head_ones()
    early_at = pl.multiple_of((1 - parity) * HALF, BLOCK)
    late_at = parity * (rows - HALF)
    for part in blocks(HALF):
        at = pl.multiple_of(late_at + part.start, BLOCK)
        f = first_of(frames[0, pl.ds(at, BLOCK)], late[part], out_self, own(2))
        first[part] = f
        q, k, v = projected_cross(f, own, qkv_cross, gains, ones, True)
        qkv[part, :HW] = q
        qkv[part, HW : 2 * HW] = k
        qkv[part, 2 * HW :] = v
    f = first_of(frames[0, pl.ds(early_at, BLOCK)], early[...], out_self, own(2))
    q, k, v = projected_cross(f, own, qkv_cross, gains, ones, True)
    keys, values = [k], [v]
    for n, (attended, source) in enumerate(zip(others, their_frames)):
        mods = all_mods[n + 1]
        g = first_of(source[0, pl.ds(early_at, BLOCK)], attended[...], out_self, mods(2))
        _, k, v = projected_cross(g, mods, qkv_cross, gains, ones, False)
        keys.append(k)
        values.append(v)
    mixed = cross_attend(q, keys, values, ones)
    out[...] = finished(f, mixed, out_cross, own(5))


def last_kernel(count, timestep, modulation, first, qkv, early_out, *refs):
    others = refs[: count - 1]
    their_frames = refs[count - 1 : 2 * count - 2]
    out_self, qkv_cross, gains, out_cross, out = refs[2 * count - 2 :]
    parity = lax.rem(lax.axis_index("tm"), 2)
    rows = out.shape[1]
    all_mods = [mods_of(timestep, modulation, k) for k in range(count)]
    own = all_mods[0]
    ones = head_ones()
    early_at = pl.multiple_of((1 - parity) * HALF, BLOCK)
    late_at = parity * (rows - HALF)
    out[0, pl.ds(early_at, rows - HALF)] = early_out[...]
    for part in blocks(HALF):
        at = pl.multiple_of(late_at + part.start, BLOCK)
        keys, values = [qkv[part, HW : 2 * HW]], [qkv[part, 2 * HW :]]
        for n, (attended, source) in enumerate(zip(others, their_frames)):
            mods = all_mods[n + 1]
            g = first_of(source[0, pl.ds(at, BLOCK)], attended[part], out_self, mods(2))
            _, k, v = projected_cross(g, mods, qkv_cross, gains, ones, False)
            keys.append(k)
            values.append(v)
        mixed = cross_attend(qkv[part, :HW], keys, values, ones)
        out[0, pl.ds(at, BLOCK)] = finished(first[part], mixed, out_cross, own(5))


def on_device(
    frames,
    timestep,
    modulation,
    qkv_self,
    out_self,
    qk_gain_self,
    qkv_cross,
    out_cross,
    qk_gain_cross,
):
    stems = lax.axis_size("stem")
    places = lax.axis_size("tm")
    rows = frames.shape[1]
    modulation = jnp.transpose(modulation, (1, 0, 2))
    early = rows - HALF
    assert places % 2 == 0 and early == BLOCK
    inside = [(i, i ^ 1) for i in range(places)]
    across = [(i, i + 1) for i in range(1, places - 1, 2)]
    across += [(b, a) for a, b in across]

    def to_stems(array):
        return [
            lax.ppermute(array, "stem", [(i, (i + k) % stems) for i in range(stems)])
            for k in range(1, stems)
        ]

    near, far = pl.pallas_call(
        split_kernel,
        out_shape=(shape(HALF, D), shape(HALF, D)),
        in_specs=[ANY],
        out_specs=(ANY, ANY),
        scratch_shapes=[pltpu.SemaphoreType.DMA((2,))],
        compiler_params=params(),
        cost_estimate=cost(4),
        name="split",
    )(frames)
    far = lax.ppermute(far, "tm", across)
    near = lax.ppermute(near, "tm", inside)
    their_frames = to_stems(frames)

    query, kv, attended_early = pl.pallas_call(
        near_kernel,
        out_shape=(shape(rows, HW), shape(rows + HALF, 2 * HW), shape(early, HW)),
        in_specs=[SMEM, VMEM, VMEM, VMEM, VMEM, VMEM],
        out_specs=(VMEM, VMEM, VMEM),
        compiler_params=params(),
        cost_estimate=cost(4),
        name="near",
    )(timestep, modulation, frames, near, qkv_self, qk_gain_self)
    others_early = to_stems(attended_early)

    attended_late = pl.pallas_call(
        far_kernel,
        out_shape=shape(HALF, HW),
        in_specs=[SMEM, VMEM, VMEM, VMEM, VMEM, VMEM, ANY],
        out_specs=VMEM,
        scratch_shapes=[
            pltpu.VMEM((rows + 2 * HALF, 2 * HW), BF16),
            pltpu.SemaphoreType.DMA,
        ],
        compiler_params=params(),
        cost_estimate=cost(4),
        name="far",
    )(timestep, modulation, far, qkv_self, qk_gain_self, query, kv)
    others_late = to_stems(attended_late)

    pairs = 2 * (stems - 1)
    first, qkv, early_out = pl.pallas_call(
        lambda *refs: own_kernel(stems, *refs),
        out_shape=(shape(HALF, D), shape(HALF, 3 * HW), shape(early, D)),
        in_specs=[SMEM, VMEM] + [VMEM] * (3 + pairs + 4),
        out_specs=(VMEM, VMEM, VMEM),
        compiler_params=params(),
        cost_estimate=cost(8),
        name="own",
    )(
        timestep, modulation, frames, attended_early, attended_late, *others_early, *their_frames,
        out_self, qkv_cross, qk_gain_cross, out_cross,
    )
    return pl.pallas_call(
        lambda *refs: last_kernel(stems, *refs),
        out_shape=shape(1, rows, D),
        in_specs=[SMEM, VMEM] + [VMEM] * (3 + pairs + 4),
        out_specs=VMEM,
        compiler_params=params(),
        cost_estimate=cost(7),
        name="last",
    )(
        timestep, modulation, first, qkv, early_out, *others_late, *their_frames,
        out_self, qkv_cross, qk_gain_cross, out_cross,
    )


def solution(mesh):
    return jax.shard_map(
        on_device,
        mesh=mesh,
        in_specs=(P("stem", "tm", None), P(), P(), P(), P(), P(), P(), P(), P()),
        out_specs=P("stem", "tm", None),
        check_vma=False,
    )
```

```python
import jax
import jax.numpy as jnp
from jax import lax
from jax.experimental import pallas as pl
from jax.experimental.pallas import tpu as pltpu
from jax.sharding import PartitionSpec as P

D = 1024
H = 8
HD = 64
HW = H * HD
HALF = 256
BLOCK = 128
SLAB = 128
EPS = 1e-06
NEG = -1e30
F32 = jnp.float32
BF16 = jnp.bfloat16
VMEM = pl.BlockSpec(memory_space=pltpu.VMEM)
SMEM = pl.BlockSpec(memory_space=pltpu.SMEM)
ANY = pl.BlockSpec(memory_space=pl.ANY)
LIMIT = 16 * 1024 * 1024


def cost(us):
    return pl.CostEstimate(flops=int(us * 1e9), bytes_accessed=int(us * 3e6), transcendentals=0)


def params():
    return pltpu.CompilerParams(vmem_limit_bytes=LIMIT)


def shape(*dims, dtype=BF16):
    return jax.ShapeDtypeStruct(dims, dtype)


def dot(a, b, dims=((1,), (0,))):
    return lax.dot_general(a, b, (dims, ((), ())), preferred_element_type=F32)


def modulated(rows, shift, scale):
    values = rows.astype(F32)
    centred = values - jnp.mean(values, axis=-1, keepdims=True)
    spread = jnp.mean(centred * centred, axis=-1, keepdims=True)
    normed = centred * lax.rsqrt(spread + EPS)
    return (normed * (1.0 + scale) + shift).astype(BF16)


def head_ones():
    row = lax.broadcasted_iota(jnp.int32, (2 * SLAB, 2 * SLAB), 0) // HD
    col = lax.broadcasted_iota(jnp.int32, (2 * SLAB, 2 * SLAB), 1) // HD
    return jnp.where(row == col, 1.0, 0.0).astype(BF16)


def head_sums(values, ones):
    parts = [dot(values[:, at : at + 2 * SLAB], ones) for at in range(0, HW, 2 * SLAB)]
    return jnp.concatenate(parts, axis=1)


def exact_head_sums(values, ones):
    high = values.astype(BF16)
    low = (values - high.astype(F32)).astype(BF16)
    return head_sums(high, ones) + head_sums(low, ones)


def head_norm(values, gain, ones):
    mean = head_sums((values * values).astype(BF16), ones) * (1.0 / HD)
    return (values * lax.rsqrt(mean + EPS) * gain).astype(BF16)


def wide_gain(gain):
    return jnp.concatenate([gain] * H, axis=1)


def window_bias(keys, ahead, first_frame=0, total=1 << 30):
    i = lax.broadcasted_iota(jnp.int32, (BLOCK, keys), 0)
    j = lax.broadcasted_iota(jnp.int32, (BLOCK, keys), 1)
    frame = first_frame + j
    keep = (j + ahead >= i) & (j + ahead <= i + 2 * HALF) & (frame >= 0) & (frame < total)
    return jnp.where(keep, 0.0, NEG)


def left_half():
    return lax.broadcasted_iota(jnp.int32, (BLOCK, SLAB), 1) < HD


def by_head(pair):
    return jnp.where(left_half(), pair[:BLOCK], pair[BLOCK:])


def raised_scores(query, keys, bias):
    half, zero = left_half(), jnp.zeros_like(query)
    pair = jnp.concatenate([jnp.where(half, query, zero), jnp.where(half, zero, query)], axis=0)
    scores = dot(pair, keys, ((1,), (1,)))
    scores = jnp.concatenate([scores[:BLOCK] + bias, scores[BLOCK:] + bias], axis=0)
    top = jnp.max(scores, axis=-1, keepdims=True)
    return jnp.exp(scores - top).astype(BF16), top


def weighted(raised, values):
    summed = dot(raised, jnp.concatenate([values, jnp.ones_like(values)], axis=1))
    return by_head(summed[:, :SLAB]), by_head(summed[:, SLAB:])


def cross_attend(query, keys, values, ones):
    query = query.astype(F32)
    base = keys[0].astype(F32)
    scores = [
        exact_head_sums(query * (k.astype(F32) - base), ones) * (HD ** -0.5) for k in keys[1:]
    ]
    top = jnp.zeros_like(query)
    for s in scores:
        top = jnp.maximum(top, s)
    raised = [jnp.exp(-top)] + [jnp.exp(s - top) for s in scores]
    total = raised[0]
    for r in raised[1:]:
        total = total + r
    scale = 1.0 / total
    out = jnp.zeros_like(query)
    for r, v in zip(raised, values):
        out = out + (r * scale).astype(BF16).astype(F32) * v.astype(F32)
    return out.astype(BF16)


def mods_of(timestep, modulation, back):
    count = lax.axis_size("stem")
    step = timestep[lax.rem(lax.axis_index("stem") + count - back, count)]
    return lambda i: modulation[i, pl.ds(step, 1), :]


def places(rows):
    parity = lax.rem(lax.axis_index("tm"), 2)
    outer = pl.multiple_of(parity * HALF, BLOCK)
    early = pl.multiple_of((1 - parity) * HALF, BLOCK)
    return parity, outer, rows - HALF, early


def pending(parity):
    return pl.multiple_of(parity * BLOCK, BLOCK), pl.multiple_of((1 - parity) * BLOCK, BLOCK)


def split_kernel(frames, far, sem):
    parity = lax.rem(lax.axis_index("tm"), 2)
    at = pl.multiple_of(parity * (frames.shape[1] - HALF), BLOCK)
    copy = pltpu.make_async_copy(frames.at[0, pl.ds(at, HALF)], far, sem)
    copy.start()
    copy.wait()


def near_kernel(
    timestep, modulation, frames, near, qkv_self, gains, out_self, qkv_cross, gains_cross,
    query, part_out, part_sum, part_top, first, first_q, first_kv, kv,
):
    rows = frames.shape[1]
    parity, outer, inner, early = places(rows)
    mods = mods_of(timestep, modulation, 0)
    shift, scale = mods(0), mods(1)
    ones = head_ones()
    q_gain = wide_gain(gains[0:1]) * (HD ** -0.5)
    k_gain = wide_gain(gains[1:2])
    own_at = parity * HALF
    near_at = (1 - parity) * rows
    near_from = parity * (rows - HALF)

    sources = [(frames, at, own_at + at) for at in (early, outer, inner)]
    sources += [(near, near_from + at, near_at + at) for at in range(0, HALF, BLOCK)]
    queries = []
    for n, (source, at, to) in enumerate(sources):
        normed = modulated(source[0, pl.ds(pl.multiple_of(at, BLOCK), BLOCK)], shift, scale)
        if n < 3:
            projected = dot(normed, qkv_self[...])
            queries.append(head_norm(projected[:, :HW], q_gain, ones))
            projected = projected[:, HW:]
        else:
            projected = dot(normed, qkv_self[:, HW:])
        to = pl.multiple_of(to, BLOCK)
        kv[pl.ds(to, BLOCK), :HW] = head_norm(projected[:, :HW], k_gain, ones)
        kv[pl.ds(to, BLOCK), HW:] = projected[:, HW:].astype(BF16)
    query[:BLOCK] = queries[1]
    query[BLOCK:] = queries[2]

    window = rows + HALF
    bias = window_bias(window, 0)
    attended = []
    for at in range(0, HW, SLAB):
        raised, _ = raised_scores(queries[0][:, at : at + SLAB], kv[:, at : at + SLAB], bias)
        out, total = weighted(raised, kv[:, HW + at : HW + at + SLAB])
        attended.append((out / total).astype(BF16))
    attended = jnp.concatenate(attended, axis=1)

    f = first_of(frames[0, pl.ds(early, BLOCK)], attended, out_self, mods(2))
    first[...] = f
    first_q[...], first_kv[:, :HW], first_kv[:, HW:] = projected_cross(
        f, mods, qkv_cross, gains_cross, ones, True
    )

    for n, width in ((0, HALF), (1, BLOCK)):
        start = pl.multiple_of(parity * width, BLOCK)
        count = window - width
        bias = window_bias(count, (1 - parity) * width)
        to = slice(n * BLOCK, (n + 1) * BLOCK)
        for at in range(0, HW, SLAB):
            cols = slice(at, at + SLAB)
            raised, top = raised_scores(
                queries[n + 1][:, cols], kv[pl.ds(start, count), cols], bias
            )
            out, total = weighted(raised, kv[pl.ds(start, count), HW + at : HW + at + SLAB])
            part_out[to, cols] = out
            part_sum[to, cols] = total
            part_top[to, cols] = by_head(jnp.broadcast_to(top, (2 * BLOCK, SLAB)))


def far_kernel(
    rows, timestep, modulation, far, qkv_self, gains, query, part_out, part_sum, part_top, attended
):
    parity, _, _, _ = places(rows)
    mods = mods_of(timestep, modulation, 0)
    shift, scale = mods(0), mods(1)
    ones = head_ones()
    k_gain = wide_gain(gains[1:2])
    keys, values = [], []
    for at in range(0, HALF, BLOCK):
        normed = modulated(far[at : at + BLOCK], shift, scale)
        projected = dot(normed, qkv_self[:, HW:])
        keys.append(head_norm(projected[:, :HW], k_gain, ones))
        values.append(projected[:, HW:].astype(BF16))
    keys = jnp.concatenate(keys, axis=0)
    values = jnp.concatenate(values, axis=0)
    place = lax.axis_index("tm")
    total = rows * lax.axis_size("tm")
    first_frame = place * rows + jnp.where(parity == 0, -HALF, rows)
    outer_bias = window_bias(HALF, jnp.where(parity == 0, 0, rows), first_frame, total)
    inner_bias = window_bias(HALF, jnp.where(parity == 0, -BLOCK, rows + BLOCK), first_frame, total)
    for at in range(0, HW, SLAB):
        cols = slice(at, at + SLAB)
        for n, bias in enumerate((outer_bias, inner_bias)):
            to = slice(n * BLOCK, (n + 1) * BLOCK)
            raised, top = raised_scores(query[to, cols], keys[:, cols], bias)
            out, summed = weighted(raised, values[:, cols])
            top = by_head(jnp.broadcast_to(top, (2 * BLOCK, SLAB)))
            both = jnp.maximum(top, part_top[to, cols])
            here = jnp.exp(top - both)
            before = jnp.exp(part_top[to, cols] - both)
            out = out * here + part_out[to, cols] * before
            summed = summed * here + part_sum[to, cols] * before
            attended[to, cols] = (out / summed).astype(BF16)


def first_of(frames, attended, weight, gate):
    mixed = dot(attended, weight[...])
    return (frames.astype(F32) + gate * mixed).astype(BF16)


def projected_cross(first, mods, weight, gains, ones, with_query):
    normed = modulated(first, mods(3), mods(4))
    if with_query:
        projected = dot(normed, weight[...])
        query = head_norm(projected[:, :HW], wide_gain(gains[0:1]), ones)
        projected = projected[:, HW:]
    else:
        projected = dot(normed, weight[:, HW:])
        query = None
    keys = head_norm(projected[:, :HW], wide_gain(gains[1:2]), ones)
    return query, keys, projected[:, HW:].astype(BF16)


def finished(first, attended, weight, gate):
    out = dot(attended, weight[...]).astype(BF16)
    return (first.astype(F32) + gate * out.astype(F32)).astype(BF16)


def own_kernel(
    rows, timestep, modulation, frames, attended, out_self, qkv_cross, gains, first, qkv
):
    mods = mods_of(timestep, modulation, 0)
    ones = head_ones()
    parity, _, _, _ = places(rows)
    for n, at in enumerate(pending(parity)):
        to = slice(n * BLOCK, (n + 1) * BLOCK)
        f = first_of(frames[pl.ds(at, BLOCK)], attended[to], out_self, mods(2))
        first[to] = f
        q, k, v = projected_cross(f, mods, qkv_cross, gains, ones, True)
        qkv[to, :HW] = q
        qkv[to, HW : 2 * HW] = k
        qkv[to, 2 * HW :] = v


def early_kernel(timestep, modulation, first, query, kv, out_cross, *refs):
    others, out = refs[:-1], refs[-1]
    mods = mods_of(timestep, modulation, 0)
    keys = [each[:, :HW] for each in (kv, *others)]
    values = [each[:, HW:] for each in (kv, *others)]
    mixed = cross_attend(query[...], keys, values, head_ones())
    out[...] = finished(first[...], mixed, out_cross, mods(5))


def last_kernel(count, timestep, modulation, first, qkv, early_out, *refs):
    others = refs[: count - 1]
    their_frames = refs[count - 1 : 2 * count - 2]
    out_self, qkv_cross, gains, out_cross, out = refs[2 * count - 2 :]
    rows = out.shape[1]
    own, *mods = [mods_of(timestep, modulation, k) for k in range(count)]
    ones = head_ones()
    parity, outer, inner, early = places(rows)
    out[0, pl.ds(early, BLOCK)] = early_out[...]
    for n, (at, to) in enumerate(zip(pending(parity), (outer, inner))):
        part = slice(n * BLOCK, (n + 1) * BLOCK)
        keys, values = [qkv[part, HW : 2 * HW]], [qkv[part, 2 * HW :]]
        for attended, source, their in zip(others, their_frames, mods):
            g = first_of(source[pl.ds(at, BLOCK)], attended[part], out_self, their(2))
            _, k, v = projected_cross(g, their, qkv_cross, gains, ones, False)
            keys.append(k)
            values.append(v)
        mixed = cross_attend(qkv[part, :HW], keys, values, ones)
        out[0, pl.ds(to, BLOCK)] = finished(first[part], mixed, out_cross, own(5))


def on_device(
    frames,
    timestep,
    modulation,
    qkv_self,
    out_self,
    qk_gain_self,
    qkv_cross,
    out_cross,
    qk_gain_cross,
):
    stems = lax.axis_size("stem")
    count = lax.axis_size("tm")
    rows = frames.shape[1]
    assert count % 2 == 0 and rows == HALF + BLOCK
    modulation = jnp.transpose(modulation, (1, 0, 2))
    inside = [(i, i ^ 1) for i in range(count)]
    across = [(i, i + 1) for i in range(1, count - 1, 2)]
    across += [(b, a) for a, b in across]

    def to_stems(array):
        return [
            lax.ppermute(array, "stem", [(i, (i + k) % stems) for i in range(stems)])
            for k in range(1, stems)
        ]

    near = lax.ppermute(frames, "tm", inside)
    far_own = pl.pallas_call(
        split_kernel,
        out_shape=shape(HALF, D),
        in_specs=[ANY],
        out_specs=ANY,
        scratch_shapes=[pltpu.SemaphoreType.DMA],
        compiler_params=params(),
        cost_estimate=cost(4),
        name="split",
    )(frames)
    far = lax.ppermute(far_own, "tm", across)
    their_frames = to_stems(far_own)

    query, part_out, part_sum, part_top, first_early, q_early, kv_early = pl.pallas_call(
        near_kernel,
        out_shape=(
            shape(HALF, HW),
            shape(HALF, HW, dtype=F32),
            shape(HALF, HW, dtype=F32),
            shape(HALF, HW, dtype=F32),
            shape(BLOCK, D),
            shape(BLOCK, HW),
            shape(BLOCK, 2 * HW),
        ),
        in_specs=[SMEM] + [VMEM] * 8,
        out_specs=(VMEM,) * 7,
        scratch_shapes=[pltpu.VMEM((rows + HALF, 2 * HW), BF16)],
        compiler_params=params(),
        cost_estimate=cost(4),
        name="near",
    )(
        timestep, modulation, frames, near, qkv_self, qk_gain_self, out_self, qkv_cross,
        qk_gain_cross,
    )
    others_early = to_stems(kv_early)

    attended = pl.pallas_call(
        lambda *refs: far_kernel(rows, *refs),
        out_shape=shape(HALF, HW),
        in_specs=[SMEM] + [VMEM] * 8,
        out_specs=VMEM,
        compiler_params=params(),
        cost_estimate=cost(4),
        name="far",
    )(timestep, modulation, far, qkv_self, qk_gain_self, query, part_out, part_sum, part_top)
    others_attended = to_stems(attended)

    first, qkv = pl.pallas_call(
        lambda *refs: own_kernel(rows, *refs),
        out_shape=(shape(HALF, D), shape(HALF, 3 * HW)),
        in_specs=[SMEM] + [VMEM] * 6,
        out_specs=(VMEM, VMEM),
        compiler_params=params(),
        cost_estimate=cost(4),
        name="own",
    )(timestep, modulation, far_own, attended, out_self, qkv_cross, qk_gain_cross)
    early_out = pl.pallas_call(
        early_kernel,
        out_shape=shape(BLOCK, D),
        in_specs=[SMEM] + [VMEM] * (4 + stems),
        out_specs=VMEM,
        compiler_params=params(),
        cost_estimate=cost(2),
        name="early",
    )(timestep, modulation, first_early, q_early, kv_early, out_cross, *others_early)
    return pl.pallas_call(
        lambda *refs: last_kernel(stems, *refs),
        out_shape=shape(1, rows, D),
        in_specs=[SMEM] + [VMEM] * (6 + 2 * stems),
        out_specs=VMEM,
        compiler_params=params(),
        cost_estimate=cost(4),
        name="last",
    )(
        timestep, modulation, first, qkv, early_out, *others_attended, *their_frames,
        out_self, qkv_cross, qk_gain_cross, out_cross,
    )


def solution(mesh):
    return jax.shard_map(
        on_device,
        mesh=mesh,
        in_specs=(P("stem", "tm", None), P(), P(), P(), P(), P(), P(), P(), P()),
        out_specs=P("stem", "tm", None),
        check_vma=False,
    )
```

```python
import jax
import jax.numpy as jnp
from jax import lax
from jax.experimental import pallas as pl
from jax.experimental.pallas import tpu as pltpu
from jax.sharding import PartitionSpec as P

D = 1024
H = 8
HD = 64
HW = H * HD
HALF = 256
BLOCK = 128
SLAB = 128
EPS = 1e-06
NEG = -1e30
F32 = jnp.float32
BF16 = jnp.bfloat16
VMEM = pl.BlockSpec(memory_space=pltpu.VMEM)
SMEM = pl.BlockSpec(memory_space=pltpu.SMEM)
ANY = pl.BlockSpec(memory_space=pl.ANY)
LIMIT = 16 * 1024 * 1024


def cost(us):
    return pl.CostEstimate(flops=int(us * 1e9), bytes_accessed=int(us * 3e6), transcendentals=0)


def params():
    return pltpu.CompilerParams(vmem_limit_bytes=LIMIT)


def shape(*dims, dtype=BF16):
    return jax.ShapeDtypeStruct(dims, dtype)


def dot(a, b, dims=((1,), (0,))):
    return lax.dot_general(a, b, (dims, ((), ())), preferred_element_type=F32)


def modulated(rows, shift, scale):
    values = rows.astype(F32)
    centred = values - jnp.mean(values, axis=-1, keepdims=True)
    spread = jnp.mean(centred * centred, axis=-1, keepdims=True)
    normed = centred * lax.rsqrt(spread + EPS)
    return (normed * (1.0 + scale) + shift).astype(BF16)


def head_ones():
    row = lax.broadcasted_iota(jnp.int32, (2 * SLAB, 2 * SLAB), 0) // HD
    col = lax.broadcasted_iota(jnp.int32, (2 * SLAB, 2 * SLAB), 1) // HD
    return jnp.where(row == col, 1.0, 0.0).astype(BF16)


def head_sums(values, ones):
    parts = [dot(values[:, at : at + 2 * SLAB], ones) for at in range(0, HW, 2 * SLAB)]
    return jnp.concatenate(parts, axis=1)


def exact_head_sums(values, ones):
    high = values.astype(BF16)
    low = (values - high.astype(F32)).astype(BF16)
    return head_sums(high, ones) + head_sums(low, ones)


def head_norm(values, gain, ones):
    mean = head_sums((values * values).astype(BF16), ones) * (1.0 / HD)
    return (values * lax.rsqrt(mean + EPS) * gain).astype(BF16)


def wide_gain(gain):
    return jnp.concatenate([gain] * H, axis=1)


def window_bias(keys, ahead, first_frame=0, total=1 << 30):
    i = lax.broadcasted_iota(jnp.int32, (BLOCK, keys), 0)
    j = lax.broadcasted_iota(jnp.int32, (BLOCK, keys), 1)
    frame = first_frame + j
    keep = (j + ahead >= i) & (j + ahead <= i + 2 * HALF) & (frame >= 0) & (frame < total)
    return jnp.where(keep, 0.0, NEG)


def left_half():
    return lax.broadcasted_iota(jnp.int32, (BLOCK, SLAB), 1) < HD


def by_head(pair):
    return jnp.where(left_half(), pair[:BLOCK], pair[BLOCK:])


def raised_scores(query, keys, bias):
    half, zero = left_half(), jnp.zeros_like(query)
    pair = jnp.concatenate([jnp.where(half, query, zero), jnp.where(half, zero, query)], axis=0)
    scores = dot(pair, keys, ((1,), (1,)))
    scores = jnp.concatenate([scores[:BLOCK] + bias, scores[BLOCK:] + bias], axis=0)
    top = jnp.max(scores, axis=-1, keepdims=True)
    return jnp.exp(scores - top).astype(BF16), top


def weighted(raised, values):
    summed = dot(raised, jnp.concatenate([values, jnp.ones_like(values)], axis=1))
    return by_head(summed[:, :SLAB]), by_head(summed[:, SLAB:])


def cross_attend(query, keys, values, ones):
    query = query.astype(F32)
    base = keys[0].astype(F32)
    scores = [
        exact_head_sums(query * (k.astype(F32) - base), ones) * (HD ** -0.5) for k in keys[1:]
    ]
    top = jnp.zeros_like(query)
    for s in scores:
        top = jnp.maximum(top, s)
    raised = [jnp.exp(-top)] + [jnp.exp(s - top) for s in scores]
    total = raised[0]
    for r in raised[1:]:
        total = total + r
    scale = 1.0 / total
    out = jnp.zeros_like(query)
    for r, v in zip(raised, values):
        out = out + (r * scale).astype(BF16).astype(F32) * v.astype(F32)
    return out.astype(BF16)


def mods_of(timestep, modulation, back):
    count = lax.axis_size("stem")
    step = timestep[lax.rem(lax.axis_index("stem") + count - back, count)]
    return lambda i: modulation[i, pl.ds(step, 1), :]


def mods_held(held, back):
    return lambda i: held[back, i : i + 1]


def places(rows):
    parity = lax.rem(lax.axis_index("tm"), 2)
    outer = pl.multiple_of(parity * HALF, BLOCK)
    early = pl.multiple_of((1 - parity) * HALF, BLOCK)
    return parity, outer, rows - HALF, early


def split_kernel(frames, outer_rows, inner_rows, early_rows, sems):
    copies = [
        pltpu.make_async_copy(frames.at[0, pl.ds(at, BLOCK)], to, sems.at[n])
        for n, (at, to) in enumerate(zip(places(frames.shape[1])[1:], (outer_rows, inner_rows, early_rows)))
    ]
    for copy in copies:
        copy.start()
    for copy in copies:
        copy.wait()


def join_kernel(outer_rows, inner_rows, both):
    both[:BLOCK] = outer_rows[...]
    both[BLOCK:] = inner_rows[...]


def near_kernel(
    timestep, modulation, early_rows, late_rows, near, qkv_self, gains, out_self, qkv_cross, gains_cross,
    query, part_out, part_sum, part_top, first, first_q, first_kv, held, kv,
):
    rows = near.shape[1]
    for k in range(held.shape[0]):
        row = mods_of(timestep, modulation, k)
        for i in range(6):
            held[k, i : i + 1] = row(i)
    parity, outer, inner, early = places(rows)
    mods = mods_of(timestep, modulation, 0)
    shift, scale = mods(0), mods(1)
    ones = head_ones()
    q_gain = wide_gain(gains[0:1]) * (HD ** -0.5)
    k_gain = wide_gain(gains[1:2])
    own_at = parity * HALF
    near_at = (1 - parity) * rows
    near_from = parity * (rows - HALF)

    sources = [(early_rows[...], own_at + early)]
    sources += [(late_rows[:BLOCK], own_at + outer), (late_rows[BLOCK:], own_at + inner)]
    sources += [
        (near[0, pl.ds(pl.multiple_of(near_from + at, BLOCK), BLOCK)], near_at + at)
        for at in range(0, HALF, BLOCK)
    ]
    queries = []
    for n, (source, to) in enumerate(sources):
        normed = modulated(source, shift, scale)
        if n < 3:
            projected = dot(normed, qkv_self[...])
            queries.append(head_norm(projected[:, :HW], q_gain, ones))
            projected = projected[:, HW:]
        else:
            projected = dot(normed, qkv_self[:, HW:])
        to = pl.multiple_of(to, BLOCK)
        kv[pl.ds(to, BLOCK), :HW] = head_norm(projected[:, :HW], k_gain, ones)
        kv[pl.ds(to, BLOCK), HW:] = projected[:, HW:].astype(BF16)
    query[:BLOCK] = queries[1]
    query[BLOCK:] = queries[2]

    window = rows + HALF
    bias = window_bias(window, 0)
    attended = []
    for at in range(0, HW, SLAB):
        raised, _ = raised_scores(queries[0][:, at : at + SLAB], kv[:, at : at + SLAB], bias)
        out, total = weighted(raised, kv[:, HW + at : HW + at + SLAB])
        attended.append((out / total).astype(BF16))
    attended = jnp.concatenate(attended, axis=1)

    f = first_of(early_rows[...], attended, out_self, mods(2))
    first[...] = f
    first_q[...], first_kv[:, :HW], first_kv[:, HW:] = projected_cross(
        f, mods, qkv_cross, gains_cross, ones, True
    )

    for n, width in ((0, HALF), (1, BLOCK)):
        start = pl.multiple_of(parity * width, BLOCK)
        count = window - width
        bias = window_bias(count, (1 - parity) * width)
        to = slice(n * BLOCK, (n + 1) * BLOCK)
        for at in range(0, HW, SLAB):
            cols = slice(at, at + SLAB)
            raised, top = raised_scores(
                queries[n + 1][:, cols], kv[pl.ds(start, count), cols], bias
            )
            out, total = weighted(raised, kv[pl.ds(start, count), HW + at : HW + at + SLAB])
            part_out[to, cols] = out
            part_sum[to, cols] = total
            part_top[to, cols] = by_head(jnp.broadcast_to(top, (2 * BLOCK, SLAB)))


def far_kernel(
    outermost, rows, held, far, qkv_self, gains, query, part_out, part_sum, part_top, *outs
):
    parity = lax.rem(lax.axis_index("tm"), 2)
    mods = mods_held(held, 0)
    ones = head_ones()
    normed = modulated(far[...], mods(0), mods(1))
    keys = dot(normed, qkv_self[:, HW : 2 * HW])
    values = dot(normed, qkv_self[:, 2 * HW :]).astype(BF16)
    keys = head_norm(keys, wide_gain(gains[1:2]), ones)
    start = jnp.where(parity == 0, -2 * BLOCK if outermost else -BLOCK, rows + (BLOCK if outermost else 0))
    place = lax.axis_index("tm")
    total = rows * lax.axis_size("tm")

    def attend(block, block_start):
        bias = window_bias(BLOCK, start - block_start + HALF, place * rows + start, total)
        to = slice(block * BLOCK, (block + 1) * BLOCK)
        for at in range(0, HW, SLAB):
            cols = slice(at, at + SLAB)
            raised, top = raised_scores(query[to, cols], keys[:, cols], bias)
            out, summed = weighted(raised, values[:, cols])
            top = by_head(jnp.broadcast_to(top, (2 * BLOCK, SLAB)))
            both = jnp.maximum(top, part_top[to, cols])
            here = jnp.exp(top - both)
            before = jnp.exp(part_top[to, cols] - both)
            out = out * here + part_out[to, cols] * before
            summed = summed * here + part_sum[to, cols] * before
            yield cols, out, summed, both

    if outermost:
        for cols, out, summed, _ in attend(0, parity * HALF):
            outs[0][:, cols] = (out / summed).astype(BF16)
    else:
        for cols, out, summed, _ in attend(1, rows - HALF):
            outs[0][:, cols] = (out / summed).astype(BF16)
        for cols, out, summed, top in attend(0, parity * HALF):
            outs[1][:, cols], outs[2][:, cols], outs[3][:, cols] = out, summed, top


def first_of(frames, attended, weight, gate):
    mixed = dot(attended, weight[...])
    return (frames.astype(F32) + gate * mixed).astype(BF16)


def projected_cross(first, mods, weight, gains, ones, with_query):
    normed = modulated(first, mods(3), mods(4))
    raw = [dot(normed, weight[:, at : at + HW]) for at in range(0 if with_query else HW, 3 * HW, HW)]
    query = head_norm(raw[0], wide_gain(gains[0:1]), ones) if with_query else None
    keys = head_norm(raw[-2], wide_gain(gains[1:2]), ones)
    return query, keys, raw[-1].astype(BF16)


def finished(first, attended, weight, gate):
    out = dot(attended, weight[...]).astype(BF16)
    return (first.astype(F32) + gate * out.astype(F32)).astype(BF16)


def own_kernel(held, frames, attended, out_self, qkv_cross, gains, first, query, kv):
    mods = mods_held(held, 0)
    f = first_of(frames[...], attended[...], out_self, mods(2))
    first[...] = f
    query[...], kv[:, :HW], kv[:, HW:] = projected_cross(
        f, mods, qkv_cross, gains, head_ones(), True
    )


def early_kernel(held, first, query, kv, out_cross, *refs):
    others, out = refs[:-1], refs[-1]
    keys = [each[:, :HW] for each in (kv, *others)]
    values = [each[:, HW:] for each in (kv, *others)]
    mixed = cross_attend(query[...], keys, values, head_ones())
    out[...] = finished(first[...], mixed, out_cross, mods_held(held, 0)(5))


def late_block(block, held, first, query, kv, others, their_frames, out_self, qkv_cross, gains, out_cross):
    ones = head_ones()
    part = slice(block * BLOCK, (block + 1) * BLOCK)
    keys, values = [kv[:, :HW]], [kv[:, HW:]]
    for n, (attended, source) in enumerate(zip(others, their_frames)):
        mods = mods_held(held, n + 1)
        g = first_of(source[part], attended[...], out_self, mods(2))
        _, k, v = projected_cross(g, mods, qkv_cross, gains, ones, False)
        keys.append(k)
        values.append(v)
    mixed = cross_attend(query[...], keys, values, ones)
    return finished(first[...], mixed, out_cross, mods_held(held, 0)(5))


def inner_kernel(count, _, held, first, query, kv, *refs):
    others, their_frames = refs[: count - 1], refs[count - 1 : 2 * count - 2]
    *weights, out = refs[2 * count - 2 :]
    out[...] = late_block(1, held, first, query, kv, others, their_frames, *weights)


def outer_kernel(count, held, first, query, kv, early_out, inner_out, *refs):
    others, their_frames = refs[: count - 1], refs[count - 1 : 2 * count - 2]
    *weights, out, outer_out, sems = refs[2 * count - 2 :]
    _, outer, inner, early = places(out.shape[1])
    copies = [
        pltpu.make_async_copy(source, out.at[0, pl.ds(at, BLOCK)], sems.at[n])
        for n, (source, at) in enumerate(((early_out, early), (inner_out, inner), (outer_out, outer)))
    ]
    copies[0].start()
    copies[1].start()
    outer_out[...] = late_block(0, held, first, query, kv, others, their_frames, *weights)
    copies[2].start()
    for copy in copies:
        copy.wait()


def on_device(
    frames,
    timestep,
    modulation,
    qkv_self,
    out_self,
    qk_gain_self,
    qkv_cross,
    out_cross,
    qk_gain_cross,
):
    stems = lax.axis_size("stem")
    count = lax.axis_size("tm")
    rows = frames.shape[1]
    assert count % 2 == 0 and rows == HALF + BLOCK
    modulation = jnp.transpose(modulation, (1, 0, 2))
    inside = [(i, i ^ 1) for i in range(count)]
    across = [(i, i + 1) for i in range(1, count - 1, 2)]
    across += [(b, a) for a, b in across]

    def to_stems(array):
        return [
            lax.ppermute(array, "stem", [(i, (i + k) % stems) for i in range(stems)])
            for k in range(1, stems)
        ]

    def call(kernel, name, us, outs, *args, scratch=(), in_specs=None, out_specs=None):
        out_specs = out_specs or jax.tree.map(lambda _: VMEM, outs)
        return pl.pallas_call(
            kernel,
            out_shape=outs,
            in_specs=in_specs or [VMEM] * len(args),
            out_specs=out_specs,
            scratch_shapes=list(scratch),
            compiler_params=params(),
            cost_estimate=cost(us),
            name=name,
        )(*args)

    half = shape(BLOCK, D)
    outer_rows, inner_rows, early_rows = call(
        split_kernel, "split", 4, (half, half, half), frames,
        scratch=[pltpu.SemaphoreType.DMA((3,))], in_specs=[ANY], out_specs=(ANY, ANY, ANY),
    )
    far_inner = lax.ppermute(outer_rows, "tm", across)
    far_outer = lax.ppermute(inner_rows, "tm", across)
    after, _ = lax.optimization_barrier((frames, outer_rows))
    near = lax.ppermute(after, "tm", inside)
    late_rows = call(join_kernel, "join", 0.1, shape(HALF, D), outer_rows, inner_rows)
    their_frames = to_stems(late_rows)

    part = shape(HALF, HW, dtype=F32)
    query, part_out, part_sum, part_top, first_early, q_early, kv_early, held = call(
        near_kernel, "near", 4,
        (shape(HALF, HW), part, part, part, half, shape(BLOCK, HW), half, shape(stems, 8, D, dtype=F32)),
        timestep, modulation, early_rows, late_rows, near, qkv_self, qk_gain_self, out_self, qkv_cross, qk_gain_cross,
        scratch=[pltpu.VMEM((rows + HALF, 2 * HW), BF16)], in_specs=[SMEM] + [VMEM] * 9,
    )
    others_early = to_stems(kv_early)

    block, part = shape(BLOCK, HW), shape(BLOCK, HW, dtype=F32)
    att_inner, *parts = call(
        lambda *refs: far_kernel(False, rows, *refs), "far_inner", 1, (block, part, part, part),
        held, far_inner, qkv_self, qk_gain_self, query, part_out, part_sum, part_top,
    )
    others_inner = to_stems(att_inner)
    att_outer = call(
        lambda *refs: far_kernel(True, rows, *refs), "far_outer", 1, block,
        held, far_outer, qkv_self, qk_gain_self, query, *parts,
    )
    others_outer = to_stems(att_outer)

    weights = (out_self, qkv_cross, qk_gain_cross)
    own_inner = call(
        own_kernel, "own_inner", 0.3, (half, block, half), held, inner_rows, att_inner, *weights
    )
    own_outer = call(
        own_kernel, "own_outer", 0.3, (half, block, half), held, outer_rows, att_outer, *weights
    )
    early_out = call(
        early_kernel, "early", 0.3, half, held, first_early, q_early, kv_early, out_cross, *others_early
    )
    inner_out = call(
        lambda *refs: inner_kernel(stems, *refs), "inner", 0.5, half,
        early_out, held, *own_inner, *others_inner, *their_frames, *weights, out_cross,
        in_specs=[ANY] + [VMEM] * (6 + 2 * stems),
    )
    return call(
        lambda *refs: outer_kernel(stems, *refs), "outer", 2, shape(1, rows, D),
        held, *own_outer, early_out, inner_out, *others_outer, *their_frames, *weights, out_cross,
        scratch=[pltpu.VMEM((BLOCK, D), BF16), pltpu.SemaphoreType.DMA((3,))], out_specs=ANY,
    )


def solution(mesh):
    return jax.shard_map(
        on_device,
        mesh=mesh,
        in_specs=(P("stem", "tm", None), P(), P(), P(), P(), P(), P(), P(), P()),
        out_specs=P("stem", "tm", None),
        check_vma=False,
    )
```

```python
import jax
import jax.numpy as jnp
from jax import lax
from jax.experimental import pallas as pl
from jax.experimental.pallas import tpu as pltpu
from jax.sharding import PartitionSpec as P

D = 1024
H = 8
HD = 64
HW = H * HD
HALF = 256
BLOCK = 128
SLAB = 128
EPS = 1e-06
NEG = -1e30
F32 = jnp.float32
BF16 = jnp.bfloat16
VMEM = pl.BlockSpec(memory_space=pltpu.VMEM)
SMEM = pl.BlockSpec(memory_space=pltpu.SMEM)
ANY = pl.BlockSpec(memory_space=pl.ANY)
LIMIT = 16 * 1024 * 1024


def cost(us):
    return pl.CostEstimate(flops=int(us * 1e9), bytes_accessed=int(us * 3e6), transcendentals=0)


def params():
    return pltpu.CompilerParams(vmem_limit_bytes=LIMIT)


def shape(*dims, dtype=BF16):
    return jax.ShapeDtypeStruct(dims, dtype)


def dot(a, b, dims=((1,), (0,))):
    return lax.dot_general(a, b, (dims, ((), ())), preferred_element_type=F32)


def modulated(rows, shift, scale):
    values = rows.astype(F32)
    centred = values - jnp.mean(values, axis=-1, keepdims=True)
    spread = jnp.mean(centred * centred, axis=-1, keepdims=True)
    normed = centred * lax.rsqrt(spread + EPS)
    return (normed * (1.0 + scale) + shift).astype(BF16)


def head_ones():
    row = lax.broadcasted_iota(jnp.int32, (2 * SLAB, 2 * SLAB), 0) // HD
    col = lax.broadcasted_iota(jnp.int32, (2 * SLAB, 2 * SLAB), 1) // HD
    return jnp.where(row == col, 1.0, 0.0).astype(BF16)


def head_sums(values, ones):
    parts = [dot(values[:, at : at + 2 * SLAB], ones) for at in range(0, HW, 2 * SLAB)]
    return jnp.concatenate(parts, axis=1)


def exact_head_sums(values, ones):
    high = values.astype(BF16)
    low = (values - high.astype(F32)).astype(BF16)
    return head_sums(high, ones) + head_sums(low, ones)


def head_norm(values, gain, ones):
    mean = head_sums((values * values).astype(BF16), ones) * (1.0 / HD)
    return (values * lax.rsqrt(mean + EPS) * gain).astype(BF16)


def wide_gain(gain):
    return jnp.concatenate([gain] * H, axis=1)


def window_bias(keys, ahead, first_frame=0, total=1 << 30):
    i = lax.broadcasted_iota(jnp.int32, (BLOCK, keys), 0)
    j = lax.broadcasted_iota(jnp.int32, (BLOCK, keys), 1)
    frame = first_frame + j
    keep = (j + ahead >= i) & (j + ahead <= i + 2 * HALF) & (frame >= 0) & (frame < total)
    return jnp.where(keep, 0.0, NEG)


def left_half():
    return lax.broadcasted_iota(jnp.int32, (BLOCK, SLAB), 1) < HD


def by_head(pair):
    return jnp.where(left_half(), pair[:BLOCK], pair[BLOCK:])


def raised_scores(query, keys, bias):
    half, zero = left_half(), jnp.zeros_like(query)
    pair = jnp.concatenate([jnp.where(half, query, zero), jnp.where(half, zero, query)], axis=0)
    scores = dot(pair, keys, ((1,), (1,)))
    scores = jnp.concatenate([scores[:BLOCK] + bias, scores[BLOCK:] + bias], axis=0)
    top = jnp.max(scores, axis=-1, keepdims=True)
    return jnp.exp(scores - top).astype(BF16), top


def weighted(raised, values):
    summed = dot(raised, jnp.concatenate([values, jnp.ones_like(values)], axis=1))
    return by_head(summed[:, :SLAB]), by_head(summed[:, SLAB:])


def cross_attend(query, keys, values, ones):
    query = query.astype(F32)
    base = keys[0].astype(F32)
    scores = [
        exact_head_sums(query * (k.astype(F32) - base), ones) * (HD ** -0.5) for k in keys[1:]
    ]
    top = jnp.zeros_like(query)
    for s in scores:
        top = jnp.maximum(top, s)
    raised = [jnp.exp(-top)] + [jnp.exp(s - top) for s in scores]
    total = raised[0]
    for r in raised[1:]:
        total = total + r
    scale = 1.0 / total
    out = jnp.zeros_like(query)
    for r, v in zip(raised, values):
        out = out + (r * scale).astype(BF16).astype(F32) * v.astype(F32)
    return out.astype(BF16)


def mods_of(timestep, modulation, back):
    count = lax.axis_size("stem")
    step = timestep[lax.rem(lax.axis_index("stem") + count - back, count)]
    return lambda i: modulation[i, pl.ds(step, 1), :]


def mods_held(held, back):
    return lambda i: held[back, i : i + 1]


def places(rows):
    parity = lax.rem(lax.axis_index("tm"), 2)
    outer = pl.multiple_of(parity * HALF, BLOCK)
    early = pl.multiple_of((1 - parity) * HALF, BLOCK)
    return parity, outer, rows - HALF, early


def split_kernel(frames, late_rows, early_rows, sems):
    _, outer, inner, early = places(frames.shape[1])
    targets = (late_rows.at[pl.ds(0, BLOCK)], late_rows.at[pl.ds(BLOCK, BLOCK)], early_rows)
    copies = [
        pltpu.make_async_copy(frames.at[0, pl.ds(at, BLOCK)], to, sems.at[n])
        for n, (at, to) in enumerate(zip((outer, inner, early), targets))
    ]
    for copy in copies:
        copy.start()
    for copy in copies:
        copy.wait()


def near_kernel(
    timestep, modulation, early_rows, late_rows, near, qkv_self, gains, out_self, qkv_cross, gains_cross,
    query, kv, first, first_q, first_kv, held,
):
    rows = near.shape[1]
    for k in range(held.shape[0]):
        row = mods_of(timestep, modulation, k)
        for i in range(6):
            held[k, i : i + 1] = row(i)
    parity, outer, inner, early = places(rows)
    mods = mods_of(timestep, modulation, 0)
    shift, scale = mods(0), mods(1)
    ones = head_ones()
    q_gain = wide_gain(gains[0:1]) * (HD ** -0.5)
    k_gain = wide_gain(gains[1:2])
    own_at = parity * HALF
    near_at = (1 - parity) * rows
    near_from = parity * (rows - HALF)

    sources = [(early_rows[...], own_at + early)]
    sources += [(late_rows[:BLOCK], own_at + outer), (late_rows[BLOCK:], own_at + inner)]
    sources += [
        (near[0, pl.ds(pl.multiple_of(near_from + at, BLOCK), BLOCK)], near_at + at)
        for at in range(0, HALF, BLOCK)
    ]
    queries = []
    for n, (source, to) in enumerate(sources):
        normed = modulated(source, shift, scale)
        if n < 3:
            projected = dot(normed, qkv_self[...])
            queries.append(head_norm(projected[:, :HW], q_gain, ones))
            projected = projected[:, HW:]
        else:
            projected = dot(normed, qkv_self[:, HW:])
        to = pl.multiple_of(to, BLOCK)
        kv[pl.ds(to, BLOCK), :HW] = head_norm(projected[:, :HW], k_gain, ones)
        kv[pl.ds(to, BLOCK), HW:] = projected[:, HW:].astype(BF16)
    query[:BLOCK] = queries[1]
    query[BLOCK:] = queries[2]

    window = rows + HALF
    bias = window_bias(window, 0)
    attended = []
    for at in range(0, HW, SLAB):
        raised, _ = raised_scores(queries[0][:, at : at + SLAB], kv[:, at : at + SLAB], bias)
        out, total = weighted(raised, kv[:, HW + at : HW + at + SLAB])
        attended.append((out / total).astype(BF16))
    attended = jnp.concatenate(attended, axis=1)

    f = first_of(early_rows[...], attended, out_self, mods(2))
    first[...] = f
    first_q[...], first_kv[:, :HW], first_kv[:, HW:] = projected_cross(
        f, mods, qkv_cross, gains_cross, ones, True
    )


def part_kernel(query, kv, part_out, part_sum, part_top):
    parity = lax.rem(lax.axis_index("tm"), 2)
    for n, width in ((0, HALF), (1, BLOCK)):
        start = pl.multiple_of(parity * width, BLOCK)
        count = kv.shape[0] - width
        bias = window_bias(count, (1 - parity) * width)
        to = slice(n * BLOCK, (n + 1) * BLOCK)
        for at in range(0, HW, SLAB):
            cols = slice(at, at + SLAB)
            raised, top = raised_scores(
                query[to, cols], kv[pl.ds(start, count), cols], bias
            )
            out, total = weighted(raised, kv[pl.ds(start, count), HW + at : HW + at + SLAB])
            part_out[to, cols] = out
            part_sum[to, cols] = total
            part_top[to, cols] = by_head(jnp.broadcast_to(top, (2 * BLOCK, SLAB)))


def far_keys(rows, held, qkv_self, gains):
    mods = mods_held(held, 0)
    normed = modulated(rows, mods(0), mods(1))
    keys = dot(normed, qkv_self[:, HW : 2 * HW])
    values = dot(normed, qkv_self[:, 2 * HW :]).astype(BF16)
    return head_norm(keys, wide_gain(gains[1:2]), head_ones()), values


def far_bias(rows, block_start, outermost):
    place = lax.axis_index("tm")
    below = -2 * BLOCK if outermost else -BLOCK
    start = jnp.where(lax.rem(place, 2) == 0, below, rows + (BLOCK if outermost else 0))
    total = rows * lax.axis_size("tm")
    return window_bias(BLOCK, start - block_start + HALF, place * rows + start, total)


def far_attend(block, bias, query, keys, values, part_out, part_sum, part_top, attended):
    to = slice(block * BLOCK, (block + 1) * BLOCK)
    for at in range(0, HW, SLAB):
        cols = slice(at, at + SLAB)
        raised, top = raised_scores(query[to, cols], keys[:, cols], bias)
        out, summed = weighted(raised, values[:, cols])
        top = by_head(jnp.broadcast_to(top, (2 * BLOCK, SLAB)))
        both = jnp.maximum(top, part_top[to, cols])
        here = jnp.exp(top - both)
        before = jnp.exp(part_top[to, cols] - both)
        out = out * here + part_out[to, cols] * before
        summed = summed * here + part_sum[to, cols] * before
        attended[:, cols] = (out / summed).astype(BF16)


def far_inner_kernel(rows, held, far, qkv_self, gains, query, *refs):
    *parts, attended, kv = refs
    keys, values = far_keys(far[:BLOCK], held, qkv_self, gains)
    far_attend(1, far_bias(rows, rows - HALF, False), query, keys, values, *parts, attended)
    kv[:, :HW], kv[:, HW:] = keys, values


def far_outer_kernel(rows, held, far, qkv_self, gains, query, *refs):
    *parts, kv, attended = refs
    keys, values = far_keys(far[BLOCK:], held, qkv_self, gains)
    keys = jnp.concatenate([kv[:, :HW], keys], axis=0)
    values = jnp.concatenate([kv[:, HW:], values], axis=0)
    start = lax.rem(lax.axis_index("tm"), 2) * HALF
    bias = [far_bias(rows, start, outermost) for outermost in (False, True)]
    far_attend(0, jnp.concatenate(bias, axis=1), query, keys, values, *parts, attended)


def first_of(frames, attended, weight, gate):
    mixed = dot(attended, weight[...])
    return (frames.astype(F32) + gate * mixed).astype(BF16)


def projected_cross(first, mods, weight, gains, ones, with_query):
    normed = modulated(first, mods(3), mods(4))
    raw = [dot(normed, weight[:, at : at + HW]) for at in range(0 if with_query else HW, 3 * HW, HW)]
    query = head_norm(raw[0], wide_gain(gains[0:1]), ones) if with_query else None
    keys = head_norm(raw[-2], wide_gain(gains[1:2]), ones)
    return query, keys, raw[-1].astype(BF16)


def finished(first, attended, weight, gate):
    out = dot(attended, weight[...]).astype(BF16)
    return (first.astype(F32) + gate * out.astype(F32)).astype(BF16)


def own_kernel(held, frames, inner, outer, out_self, qkv_cross, gains, first, query, kv):
    mods = mods_held(held, 0)
    ones = head_ones()
    parts = [slice(0, BLOCK), slice(BLOCK, HALF)]
    mixed = [dot(attended[...], out_self[...]) for attended in (outer, inner)]
    gains = [wide_gain(gains[i : i + 1]) for i in range(2)]

    def normed(n):
        f = (frames[parts[n]].astype(F32) + mods(2) * mixed[n]).astype(BF16)
        first[parts[n]] = f
        return modulated(f, mods(3), mods(4))

    rows = normed(0)
    for n, part in enumerate(parts):
        raw = [dot(rows, qkv_cross[:, at : at + HW]) for at in (2 * HW, 0, HW)]
        if n + 1 < len(parts):
            rows = normed(n + 1)
        kv[part, HW:] = raw[0].astype(BF16)
        query[part] = head_norm(raw[1], gains[0], ones)
        kv[part, :HW] = head_norm(raw[2], gains[1], ones)


def early_kernel(held, first, query, kv, out_cross, *refs):
    others, out = refs[:-1], refs[-1]
    keys = [each[:, :HW] for each in (kv, *others)]
    values = [each[:, HW:] for each in (kv, *others)]
    mixed = cross_attend(query[...], keys, values, head_ones())
    out[...] = finished(first[...], mixed, out_cross, mods_held(held, 0)(5))


def late_block(block, held, first, query, kv, others, their_frames, out_self, qkv_cross, gains, out_cross):
    ones = head_ones()
    part = slice(block * BLOCK, (block + 1) * BLOCK)
    keys, values = [kv[part, :HW]], [kv[part, HW:]]
    for n, (attended, source) in enumerate(zip(others, their_frames)):
        mods = mods_held(held, n + 1)
        g = first_of(source[part], attended[...], out_self, mods(2))
        _, k, v = projected_cross(g, mods, qkv_cross, gains, ones, False)
        keys.append(k)
        values.append(v)
    mixed = cross_attend(query[part], keys, values, ones)
    return finished(first[part], mixed, out_cross, mods_held(held, 0)(5))


def inner_kernel(count, _, held, first, query, kv, *refs):
    others, their_frames = refs[: count - 1], refs[count - 1 : 2 * count - 2]
    *weights, out = refs[2 * count - 2 :]
    out[...] = late_block(1, held, first, query, kv, others, their_frames, *weights)


def outer_kernel(count, held, first, query, kv, early_out, inner_out, *refs):
    others, their_frames = refs[: count - 1], refs[count - 1 : 2 * count - 2]
    *weights, out, outer_out, sems = refs[2 * count - 2 :]
    _, outer, inner, early = places(out.shape[1])
    copies = [
        pltpu.make_async_copy(source, out.at[0, pl.ds(at, BLOCK)], sems.at[n])
        for n, (source, at) in enumerate(((early_out, early), (inner_out, inner), (outer_out, outer)))
    ]
    copies[0].start()
    copies[1].start()
    outer_out[...] = late_block(0, held, first, query, kv, others, their_frames, *weights)
    copies[2].start()
    for copy in copies:
        copy.wait()


def on_device(
    frames,
    timestep,
    modulation,
    qkv_self,
    out_self,
    qk_gain_self,
    qkv_cross,
    out_cross,
    qk_gain_cross,
):
    stems = lax.axis_size("stem")
    count = lax.axis_size("tm")
    rows = frames.shape[1]
    assert count % 2 == 0 and rows == HALF + BLOCK
    modulation = jnp.transpose(modulation, (1, 0, 2))
    inside = [(i, i ^ 1) for i in range(count)]
    across = [(i, i + 1) for i in range(1, count - 1, 2)]
    across += [(b, a) for a, b in across]

    def to_stems(array):
        return [
            lax.ppermute(array, "stem", [(i, (i + k) % stems) for i in range(stems)])
            for k in range(1, stems)
        ]

    def call(kernel, name, us, outs, *args, scratch=(), in_specs=None, out_specs=None):
        out_specs = out_specs or jax.tree.map(lambda _: VMEM, outs)
        return pl.pallas_call(
            kernel,
            out_shape=outs,
            in_specs=in_specs or [VMEM] * len(args),
            out_specs=out_specs,
            scratch_shapes=list(scratch),
            compiler_params=params(),
            cost_estimate=cost(us),
            name=name,
        )(*args)

    half = shape(BLOCK, D)
    late_rows, early_rows = call(
        split_kernel, "split", 6, (shape(HALF, D), half), frames,
        scratch=[pltpu.SemaphoreType.DMA((3,))], in_specs=[ANY], out_specs=(ANY, ANY),
    )
    their_frames = to_stems(late_rows)
    far = lax.ppermute(late_rows, "tm", across)
    after, _ = lax.optimization_barrier((frames, late_rows))
    near = lax.ppermute(after, "tm", inside)

    late, block, part = shape(HALF, HW), shape(BLOCK, HW), shape(HALF, HW, dtype=F32)
    query, kv, first_early, q_early, kv_early, held = call(
        near_kernel, "near", 2,
        (late, shape(rows + HALF, 2 * HW), half, block, half, shape(stems, 8, D, dtype=F32)),
        timestep, modulation, early_rows, late_rows, near, qkv_self, qk_gain_self, out_self, qkv_cross, qk_gain_cross,
        in_specs=[SMEM] + [VMEM] * 9,
    )
    others_early = to_stems(kv_early)
    parts = call(part_kernel, "part", 0.3, (part, part, part), query, kv)

    self_weights = (qkv_self, qk_gain_self)
    att_inner, far_kv = call(
        lambda *refs: far_inner_kernel(rows, *refs), "far_inner", 2, (block, half),
        held, far, *self_weights, query, *parts,
    )
    others_inner = to_stems(att_inner)
    att_outer = call(
        lambda *refs: far_outer_kernel(rows, *refs), "far_outer", 0.3, block,
        held, far, *self_weights, query, *parts, far_kv,
    )
    others_outer = to_stems(att_outer)

    weights = (out_self, qkv_cross, qk_gain_cross)
    own = call(
        own_kernel, "own", 0.3, (shape(HALF, D), late, shape(HALF, D)),
        held, late_rows, att_inner, att_outer, *weights,
    )
    early_out = call(
        early_kernel, "early", 0.3, half, held, first_early, q_early, kv_early, out_cross, *others_early
    )
    inner_out = call(
        lambda *refs: inner_kernel(stems, *refs), "inner", 0.6, half,
        early_out, held, *own, *others_inner, *their_frames, *weights, out_cross,
        in_specs=[ANY] + [VMEM] * (6 + 2 * stems),
    )
    return call(
        lambda *refs: outer_kernel(stems, *refs), "outer", 0.3, shape(1, rows, D),
        held, *own, early_out, inner_out, *others_outer, *their_frames, *weights, out_cross,
        scratch=[pltpu.VMEM((BLOCK, D), BF16), pltpu.SemaphoreType.DMA((3,))], out_specs=ANY,
    )


def solution(mesh):
    return jax.shard_map(
        on_device,
        mesh=mesh,
        in_specs=(P("stem", "tm", None), P(), P(), P(), P(), P(), P(), P(), P()),
        out_specs=P("stem", "tm", None),
        check_vma=False,
    )
```

```python
import jax
import jax.numpy as jnp
from jax import lax
from jax.experimental import pallas as pl
from jax.experimental.pallas import tpu as pltpu
from jax.sharding import PartitionSpec as P

D = 1024
H = 8
HD = 64
HW = H * HD
HALF = 256
BLOCK = 128
SLAB = 128
EPS = 1e-06
NEG = -1e30
F32 = jnp.float32
BF16 = jnp.bfloat16
VMEM = pl.BlockSpec(memory_space=pltpu.VMEM)
SMEM = pl.BlockSpec(memory_space=pltpu.SMEM)
ANY = pl.BlockSpec(memory_space=pl.ANY)
LIMIT = 16 * 1024 * 1024


def cost(us):
    return pl.CostEstimate(flops=int(us * 1e9), bytes_accessed=int(us * 3e6), transcendentals=0)


def params():
    return pltpu.CompilerParams(vmem_limit_bytes=LIMIT)


def shape(*dims, dtype=BF16):
    return jax.ShapeDtypeStruct(dims, dtype)


def dot(a, b, dims=((1,), (0,))):
    return lax.dot_general(a, b, (dims, ((), ())), preferred_element_type=F32)


def modulated(rows, shift, scale):
    values = rows.astype(F32)
    centred = values - jnp.mean(values, axis=-1, keepdims=True)
    spread = jnp.mean(centred * centred, axis=-1, keepdims=True)
    normed = centred * lax.rsqrt(spread + EPS)
    return (normed * (1.0 + scale) + shift).astype(BF16)


def head_ones():
    row = lax.broadcasted_iota(jnp.int32, (2 * SLAB, 2 * SLAB), 0) // HD
    col = lax.broadcasted_iota(jnp.int32, (2 * SLAB, 2 * SLAB), 1) // HD
    return jnp.where(row == col, 1.0, 0.0).astype(BF16)


def head_sums(values, ones):
    parts = [dot(values[:, at : at + 2 * SLAB], ones) for at in range(0, HW, 2 * SLAB)]
    return jnp.concatenate(parts, axis=1)


def exact_head_sums(values, ones):
    high = values.astype(BF16)
    low = (values - high.astype(F32)).astype(BF16)
    return head_sums(high, ones) + head_sums(low, ones)


def head_norm(values, gain, ones):
    mean = head_sums((values * values).astype(BF16), ones) * (1.0 / HD)
    return (values * lax.rsqrt(mean + EPS) * gain).astype(BF16)


def wide_gain(gain):
    return jnp.concatenate([gain] * H, axis=1)


def window_bias(keys, ahead, first_frame=0, total=1 << 30):
    i = lax.broadcasted_iota(jnp.int32, (BLOCK, keys), 0)
    j = lax.broadcasted_iota(jnp.int32, (BLOCK, keys), 1)
    frame = first_frame + j
    keep = (j + ahead >= i) & (j + ahead <= i + 2 * HALF) & (frame >= 0) & (frame < total)
    return jnp.where(keep, 0.0, NEG)


def left_half():
    return lax.broadcasted_iota(jnp.int32, (BLOCK, SLAB), 1) < HD


def by_head(pair):
    return jnp.where(left_half(), pair[:BLOCK], pair[BLOCK:])


def raised_scores(query, keys, bias):
    half, zero = left_half(), jnp.zeros_like(query)
    pair = jnp.concatenate([jnp.where(half, query, zero), jnp.where(half, zero, query)], axis=0)
    scores = dot(pair, keys, ((1,), (1,)))
    scores = jnp.concatenate([scores[:BLOCK] + bias, scores[BLOCK:] + bias], axis=0)
    top = jnp.max(scores, axis=-1, keepdims=True)
    return jnp.exp(scores - top).astype(BF16), top


def weighted(raised, values):
    summed = dot(raised, jnp.concatenate([values, jnp.ones_like(values)], axis=1))
    return by_head(summed[:, :SLAB]), by_head(summed[:, SLAB:])


def cross_attend(query, keys, values, ones):
    query = query.astype(F32)
    base = keys[0].astype(F32)
    scores = [
        exact_head_sums(query * (k.astype(F32) - base), ones) * (HD ** -0.5) for k in keys[1:]
    ]
    top = jnp.zeros_like(query)
    for s in scores:
        top = jnp.maximum(top, s)
    raised = [jnp.exp(-top)] + [jnp.exp(s - top) for s in scores]
    total = raised[0]
    for r in raised[1:]:
        total = total + r
    scale = 1.0 / total
    out = jnp.zeros_like(query)
    for r, v in zip(raised, values):
        out = out + (r * scale).astype(BF16).astype(F32) * v.astype(F32)
    return out.astype(BF16)


def mods_of(timestep, modulation, back):
    count = lax.axis_size("stem")
    step = timestep[lax.rem(lax.axis_index("stem") + count - back, count)]
    return lambda i: modulation[i, pl.ds(step, 1), :]


def mods_held(held, back):
    return lambda i: held[back, i : i + 1]


def places(rows):
    parity = lax.rem(lax.axis_index("tm"), 2)
    outer = pl.multiple_of(parity * HALF, BLOCK)
    early = pl.multiple_of((1 - parity) * HALF, BLOCK)
    return parity, outer, rows - HALF, early


def split_kernel(frames, late_rows, early_rows, sems):
    _, outer, inner, early = places(frames.shape[1])
    targets = (late_rows.at[pl.ds(0, BLOCK)], late_rows.at[pl.ds(BLOCK, BLOCK)], early_rows)
    copies = [
        pltpu.make_async_copy(frames.at[0, pl.ds(at, BLOCK)], to, sems.at[n])
        for n, (at, to) in enumerate(zip((outer, inner, early), targets))
    ]
    for copy in copies:
        copy.start()
    for copy in copies:
        copy.wait()


def mate_kernel(mate, rows):
    _, _, inner, outer = places(mate.shape[1])
    rows[:BLOCK] = mate[0, pl.ds(outer, BLOCK)]
    rows[BLOCK:] = mate[0, inner : inner + BLOCK]


def near_kernel(
    timestep, modulation, early_rows, late_rows, near, qkv_self, gains, out_self, qkv_cross, gains_cross,
    query, kv, first, first_q, first_kv, held,
):
    rows = near.shape[1]
    for k in range(held.shape[0]):
        row = mods_of(timestep, modulation, k)
        for i in range(6):
            held[k, i : i + 1] = row(i)
    parity, outer, inner, early = places(rows)
    mods = mods_of(timestep, modulation, 0)
    shift, scale = mods(0), mods(1)
    ones = head_ones()
    q_gain = wide_gain(gains[0:1]) * (HD ** -0.5)
    k_gain = wide_gain(gains[1:2])
    own_at = parity * HALF
    near_at = (1 - parity) * rows
    near_from = parity * (rows - HALF)

    sources = [(early_rows[...], own_at + early)]
    sources += [(late_rows[:BLOCK], own_at + outer), (late_rows[BLOCK:], own_at + inner)]
    sources += [
        (near[0, pl.ds(pl.multiple_of(near_from + at, BLOCK), BLOCK)], near_at + at)
        for at in range(0, HALF, BLOCK)
    ]
    queries = []
    for n, (source, to) in enumerate(sources):
        normed = modulated(source, shift, scale)
        if n < 3:
            projected = dot(normed, qkv_self[...])
            queries.append(head_norm(projected[:, :HW], q_gain, ones))
            projected = projected[:, HW:]
        else:
            projected = dot(normed, qkv_self[:, HW:])
        to = pl.multiple_of(to, BLOCK)
        kv[pl.ds(to, BLOCK), :HW] = head_norm(projected[:, :HW], k_gain, ones)
        kv[pl.ds(to, BLOCK), HW:] = projected[:, HW:].astype(BF16)
    query[:BLOCK] = queries[1]
    query[BLOCK:] = queries[2]

    window = rows + HALF
    bias = window_bias(window, 0)
    attended = []
    for at in range(0, HW, SLAB):
        raised, _ = raised_scores(queries[0][:, at : at + SLAB], kv[:, at : at + SLAB], bias)
        out, total = weighted(raised, kv[:, HW + at : HW + at + SLAB])
        attended.append((out / total).astype(BF16))
    attended = jnp.concatenate(attended, axis=1)

    f = first_of(early_rows[...], attended, out_self, mods(2))
    first[...] = f
    first_q[...], first_kv[:, :HW], first_kv[:, HW:] = projected_cross(
        f, mods, qkv_cross, gains_cross, ones, True
    )


def part_kernel(query, kv, part_out, part_sum, part_top):
    parity = lax.rem(lax.axis_index("tm"), 2)
    for n, width in ((0, HALF), (1, BLOCK)):
        start = pl.multiple_of(parity * width, BLOCK)
        count = kv.shape[0] - width
        bias = window_bias(count, (1 - parity) * width)
        to = slice(n * BLOCK, (n + 1) * BLOCK)
        for at in range(0, HW, SLAB):
            cols = slice(at, at + SLAB)
            raised, top = raised_scores(
                query[to, cols], kv[pl.ds(start, count), cols], bias
            )
            out, total = weighted(raised, kv[pl.ds(start, count), HW + at : HW + at + SLAB])
            part_out[to, cols] = out
            part_sum[to, cols] = total
            part_top[to, cols] = by_head(jnp.broadcast_to(top, (2 * BLOCK, SLAB)))


def far_keys(rows, held, qkv_self, gains):
    mods = mods_held(held, 0)
    normed = modulated(rows, mods(0), mods(1))
    keys = dot(normed, qkv_self[:, HW : 2 * HW])
    values = dot(normed, qkv_self[:, 2 * HW :]).astype(BF16)
    return head_norm(keys, wide_gain(gains[1:2]), head_ones()), values


def far_bias(rows, block_start, outermost):
    place = lax.axis_index("tm")
    below = -2 * BLOCK if outermost else -BLOCK
    start = jnp.where(lax.rem(place, 2) == 0, below, rows + (BLOCK if outermost else 0))
    total = rows * lax.axis_size("tm")
    return window_bias(BLOCK, start - block_start + HALF, place * rows + start, total)


def far_attend(block, bias, query, keys, values, part_out, part_sum, part_top, attended):
    to = slice(block * BLOCK, (block + 1) * BLOCK)
    for at in range(0, HW, SLAB):
        cols = slice(at, at + SLAB)
        raised, top = raised_scores(query[to, cols], keys[:, cols], bias)
        out, summed = weighted(raised, values[:, cols])
        top = by_head(jnp.broadcast_to(top, (2 * BLOCK, SLAB)))
        both = jnp.maximum(top, part_top[to, cols])
        here = jnp.exp(top - both)
        before = jnp.exp(part_top[to, cols] - both)
        out = out * here + part_out[to, cols] * before
        summed = summed * here + part_sum[to, cols] * before
        attended[:, cols] = (out / summed).astype(BF16)


def far_inner_kernel(rows, held, far, qkv_self, gains, query, *refs):
    parts, (attended, kv) = refs[:3], refs[-2:]
    keys, values = far_keys(far[:BLOCK], held, qkv_self, gains)
    far_attend(1, far_bias(rows, rows - HALF, False), query, keys, values, *parts, attended)
    kv[:, :HW], kv[:, HW:] = keys, values


def far_outer_kernel(rows, held, far, qkv_self, gains, query, *refs):
    *parts, kv, attended = refs
    keys, values = far_keys(far[BLOCK:], held, qkv_self, gains)
    keys = jnp.concatenate([kv[:, :HW], keys], axis=0)
    values = jnp.concatenate([kv[:, HW:], values], axis=0)
    start = lax.rem(lax.axis_index("tm"), 2) * HALF
    bias = [far_bias(rows, start, outermost) for outermost in (False, True)]
    far_attend(0, jnp.concatenate(bias, axis=1), query, keys, values, *parts, attended)


def first_of(frames, attended, weight, gate):
    mixed = dot(attended, weight[...])
    return (frames.astype(F32) + gate * mixed).astype(BF16)


def projected_cross(first, mods, weight, gains, ones, with_query):
    normed = modulated(first, mods(3), mods(4))
    raw = [dot(normed, weight[:, at : at + HW]) for at in range(0 if with_query else HW, 3 * HW, HW)]
    query = head_norm(raw[0], wide_gain(gains[0:1]), ones) if with_query else None
    keys = head_norm(raw[-2], wide_gain(gains[1:2]), ones)
    return query, keys, raw[-1].astype(BF16)


def finished(first, attended, weight, gate):
    out = dot(attended, weight[...]).astype(BF16)
    return (first.astype(F32) + gate * out.astype(F32)).astype(BF16)


def own_kernel(held, frames, inner, outer, out_self, qkv_cross, gains, first, query, kv):
    mods = mods_held(held, 0)
    ones = head_ones()
    parts = [slice(0, BLOCK), slice(BLOCK, HALF)]
    mixed = [dot(attended[...], out_self[...]) for attended in (outer, inner)]
    gains = [wide_gain(gains[i : i + 1]) for i in range(2)]

    def normed(n):
        f = (frames[parts[n]].astype(F32) + mods(2) * mixed[n]).astype(BF16)
        first[parts[n]] = f
        return modulated(f, mods(3), mods(4))

    rows = normed(0)
    for n, part in enumerate(parts):
        raw = [dot(rows, qkv_cross[:, at : at + HW]) for at in (2 * HW, 0, HW)]
        if n + 1 < len(parts):
            rows = normed(n + 1)
        kv[part, HW:] = raw[0].astype(BF16)
        query[part] = head_norm(raw[1], gains[0], ones)
        kv[part, :HW] = head_norm(raw[2], gains[1], ones)


def early_kernel(_, held, first, query, kv, out_cross, *refs):
    others, out = refs[:-1], refs[-1]
    keys = [each[:, :HW] for each in (kv, *others)]
    values = [each[:, HW:] for each in (kv, *others)]
    mixed = cross_attend(query[...], keys, values, head_ones())
    out[...] = finished(first[...], mixed, out_cross, mods_held(held, 0)(5))


def late_block(block, held, first, query, kv, others, their_frames, out_self, qkv_cross, gains, out_cross):
    ones = head_ones()
    part = slice(block * BLOCK, (block + 1) * BLOCK)
    keys, values = [kv[part, :HW]], [kv[part, HW:]]
    for n, (attended, source) in enumerate(zip(others, their_frames)):
        mods = mods_held(held, n + 1)
        g = first_of(source[part], attended[...], out_self, mods(2))
        _, k, v = projected_cross(g, mods, qkv_cross, gains, ones, False)
        keys.append(k)
        values.append(v)
    mixed = cross_attend(query[part], keys, values, ones)
    return finished(first[part], mixed, out_cross, mods_held(held, 0)(5))


def inner_kernel(count, _, held, first, query, kv, *refs):
    others, their_frames = refs[: count - 1], refs[count - 1 : 2 * count - 2]
    *weights, out = refs[2 * count - 2 :]
    out[...] = late_block(1, held, first, query, kv, others, their_frames, *weights)


def outer_kernel(count, held, first, query, kv, early_out, inner_out, *refs):
    others, their_frames = refs[: count - 1], refs[count - 1 : 2 * count - 2]
    *weights, out, outer_out, sems = refs[2 * count - 2 :]
    _, outer, inner, early = places(out.shape[1])
    copies = [
        pltpu.make_async_copy(source, out.at[0, pl.ds(at, BLOCK)], sems.at[n])
        for n, (source, at) in enumerate(((early_out, early), (inner_out, inner), (outer_out, outer)))
    ]
    copies[0].start()
    copies[1].start()
    outer_out[...] = late_block(0, held, first, query, kv, others, their_frames, *weights)
    copies[2].start()
    for copy in copies:
        copy.wait()


def on_device(
    frames,
    timestep,
    modulation,
    qkv_self,
    out_self,
    qk_gain_self,
    qkv_cross,
    out_cross,
    qk_gain_cross,
):
    stems = lax.axis_size("stem")
    count = lax.axis_size("tm")
    rows = frames.shape[1]
    assert count % 2 == 0 and rows == HALF + BLOCK
    modulation = jnp.transpose(modulation, (1, 0, 2))
    inside = [(i, i ^ 1) for i in range(count)]
    across = [(i, i + 2) for i in range(0, count - 2, 2)]
    across += [(i + 3, i + 1) for i in range(0, count - 2, 2)]

    def to_stems(array):
        return [
            lax.ppermute(array, "stem", [(i, (i + k) % stems) for i in range(stems)])
            for k in range(1, stems)
        ]

    def call(kernel, name, us, outs, *args, scratch=(), in_specs=None, out_specs=None):
        out_specs = out_specs or jax.tree.map(lambda _: VMEM, outs)
        return pl.pallas_call(
            kernel,
            out_shape=outs,
            in_specs=in_specs or [VMEM] * len(args),
            out_specs=out_specs,
            scratch_shapes=list(scratch),
            compiler_params=params(),
            cost_estimate=cost(us),
            name=name,
        )(*args)

    half = shape(BLOCK, D)
    late_rows, early_rows = call(
        split_kernel, "split", 6, (shape(HALF, D), half), frames,
        scratch=[pltpu.SemaphoreType.DMA((3,))], in_specs=[ANY], out_specs=(ANY, ANY),
    )
    their_frames = to_stems(late_rows)
    near = lax.ppermute(frames, "tm", inside)
    mate_rows = call(mate_kernel, "mate", 0.1, shape(HALF, D), near)
    far = lax.ppermute(mate_rows, "tm", across)

    late, block, part = shape(HALF, HW), shape(BLOCK, HW), shape(HALF, HW, dtype=F32)
    query, kv, first_early, q_early, kv_early, held = call(
        near_kernel, "near", 2,
        (late, shape(rows + HALF, 2 * HW), half, block, half, shape(stems, 8, D, dtype=F32)),
        timestep, modulation, early_rows, late_rows, near, qkv_self, qk_gain_self, out_self, qkv_cross, qk_gain_cross,
        in_specs=[SMEM] + [VMEM] * 9,
    )
    others_early = to_stems(kv_early)
    parts = call(part_kernel, "part", 0.3, (part, part, part), query, kv)

    self_weights = (qkv_self, qk_gain_self)
    att_inner, far_kv = call(
        lambda *refs: far_inner_kernel(rows, *refs), "far_inner", 2, (block, half),
        held, far, *self_weights, query, *parts, *their_frames,
        in_specs=[VMEM] * 8 + [ANY] * (stems - 1),
    )
    others_inner = to_stems(att_inner)
    att_outer = call(
        lambda *refs: far_outer_kernel(rows, *refs), "far_outer", 0.3, block,
        held, far, *self_weights, query, *parts, far_kv,
    )
    others_outer = to_stems(att_outer)

    weights = (out_self, qkv_cross, qk_gain_cross)
    own = call(
        own_kernel, "own", 0.3, (shape(HALF, D), late, shape(HALF, D)),
        held, late_rows, att_inner, att_outer, *weights,
    )
    early_out = call(
        early_kernel, "early", 0.3, half, own[0], held, first_early, q_early, kv_early, out_cross, *others_early,
        in_specs=[ANY] + [VMEM] * (4 + stems),
    )
    inner_out = call(
        lambda *refs: inner_kernel(stems, *refs), "inner", 0.6, half,
        early_out, held, *own, *others_inner, *their_frames, *weights, out_cross,
        in_specs=[ANY] + [VMEM] * (6 + 2 * stems),
    )
    return call(
        lambda *refs: outer_kernel(stems, *refs), "outer", 0.3, shape(1, rows, D),
        held, *own, early_out, inner_out, *others_outer, *their_frames, *weights, out_cross,
        scratch=[pltpu.VMEM((BLOCK, D), BF16), pltpu.SemaphoreType.DMA((3,))], out_specs=ANY,
    )


def solution(mesh):
    return jax.shard_map(
        on_device,
        mesh=mesh,
        in_specs=(P("stem", "tm", None), P(), P(), P(), P(), P(), P(), P(), P()),
        out_specs=P("stem", "tm", None),
        check_vma=False,
    )
```

```python
import jax
import jax.numpy as jnp
from jax import lax
from jax.experimental import pallas as pl
from jax.experimental.pallas import tpu as pltpu
from jax.sharding import PartitionSpec as P

D = 1024
H = 8
HD = 64
HW = H * HD
HALF = 256
BLOCK = 128
SLAB = 128
EPS = 1e-06
NEG = -1e30
F32 = jnp.float32
BF16 = jnp.bfloat16
VMEM = pl.BlockSpec(memory_space=pltpu.VMEM)
SMEM = pl.BlockSpec(memory_space=pltpu.SMEM)
ANY = pl.BlockSpec(memory_space=pl.ANY)
LIMIT = 16 * 1024 * 1024


def cost(us):
    return pl.CostEstimate(flops=int(us * 1e9), bytes_accessed=int(us * 3e6), transcendentals=0)


def params():
    return pltpu.CompilerParams(vmem_limit_bytes=LIMIT)


def shape(*dims, dtype=BF16):
    return jax.ShapeDtypeStruct(dims, dtype)


def dot(a, b, dims=((1,), (0,))):
    return lax.dot_general(a, b, (dims, ((), ())), preferred_element_type=F32)


def modulated(rows, shift, scale):
    values = rows.astype(F32)
    centred = values - jnp.mean(values, axis=-1, keepdims=True)
    spread = jnp.mean(centred * centred, axis=-1, keepdims=True)
    normed = centred * lax.rsqrt(spread + EPS)
    return (normed * (1.0 + scale) + shift).astype(BF16)


def head_ones():
    row = lax.broadcasted_iota(jnp.int32, (2 * SLAB, 2 * SLAB), 0) // HD
    col = lax.broadcasted_iota(jnp.int32, (2 * SLAB, 2 * SLAB), 1) // HD
    return jnp.where(row == col, 1.0, 0.0).astype(BF16)


def head_sums(values, ones):
    parts = [dot(values[:, at : at + 2 * SLAB], ones) for at in range(0, HW, 2 * SLAB)]
    return jnp.concatenate(parts, axis=1)


def exact_head_sums(values, ones):
    high = values.astype(BF16)
    low = (values - high.astype(F32)).astype(BF16)
    return head_sums(high, ones) + head_sums(low, ones)


def head_norm(values, gain, ones):
    mean = head_sums((values * values).astype(BF16), ones) * (1.0 / HD)
    return (values * lax.rsqrt(mean + EPS) * gain).astype(BF16)


def wide_gain(gain):
    return jnp.concatenate([gain] * H, axis=1)


def window_bias(keys, ahead, first_frame=0, total=1 << 30):
    i = lax.broadcasted_iota(jnp.int32, (BLOCK, keys), 0)
    j = lax.broadcasted_iota(jnp.int32, (BLOCK, keys), 1)
    frame = first_frame + j
    keep = (j + ahead >= i) & (j + ahead <= i + 2 * HALF) & (frame >= 0) & (frame < total)
    return jnp.where(keep, 0.0, NEG)


def left_half():
    return lax.broadcasted_iota(jnp.int32, (BLOCK, SLAB), 1) < HD


def by_head(pair):
    return jnp.where(left_half(), pair[:BLOCK], pair[BLOCK:])


def raised_scores(query, keys, bias):
    half, zero = left_half(), jnp.zeros_like(query)
    pair = jnp.concatenate([jnp.where(half, query, zero), jnp.where(half, zero, query)], axis=0)
    scores = dot(pair, keys, ((1,), (1,)))
    scores = jnp.concatenate([scores[:BLOCK] + bias, scores[BLOCK:] + bias], axis=0)
    top = jnp.max(scores, axis=-1, keepdims=True)
    return jnp.exp(scores - top).astype(BF16), top


def weighted(raised, values):
    summed = dot(raised, jnp.concatenate([values, jnp.ones_like(values)], axis=1))
    return by_head(summed[:, :SLAB]), by_head(summed[:, SLAB:])


def cross_attend(query, keys, values, ones):
    query = query.astype(F32)
    base = keys[0].astype(F32)
    scores = [
        exact_head_sums(query * (k.astype(F32) - base), ones) * (HD ** -0.5) for k in keys[1:]
    ]
    top = jnp.zeros_like(query)
    for s in scores:
        top = jnp.maximum(top, s)
    raised = [jnp.exp(-top)] + [jnp.exp(s - top) for s in scores]
    total = raised[0]
    for r in raised[1:]:
        total = total + r
    scale = 1.0 / total
    out = jnp.zeros_like(query)
    for r, v in zip(raised, values):
        out = out + (r * scale).astype(BF16).astype(F32) * v.astype(F32)
    return out.astype(BF16)


def mods_of(timestep, modulation, back):
    count = lax.axis_size("stem")
    step = timestep[lax.rem(lax.axis_index("stem") + count - back, count)]
    return lambda i: modulation[i, pl.ds(step, 1), :]


def mods_held(held, back):
    return lambda i: held[back, i : i + 1]


def places(rows):
    parity = lax.rem(lax.axis_index("tm"), 2)
    outer = pl.multiple_of(parity * HALF, BLOCK)
    early = pl.multiple_of((1 - parity) * HALF, BLOCK)
    return parity, outer, rows - HALF, early


def split_kernel(frames, late_rows, early_rows, sems):
    _, outer, inner, early = places(frames.shape[1])
    targets = (late_rows.at[pl.ds(0, BLOCK)], late_rows.at[pl.ds(BLOCK, BLOCK)], early_rows)
    copies = [
        pltpu.make_async_copy(frames.at[0, pl.ds(at, BLOCK)], to, sems.at[n])
        for n, (at, to) in enumerate(zip((outer, inner, early), targets))
    ]
    for copy in copies:
        copy.start()
    for copy in copies:
        copy.wait()


def mate_kernel(mate, rows):
    _, _, inner, outer = places(mate.shape[1])
    rows[:BLOCK] = mate[0, pl.ds(outer, BLOCK)]
    rows[BLOCK:] = mate[0, inner : inner + BLOCK]


def near_kernel(
    timestep, modulation, early_rows, late_rows, near, qkv_self, gains, out_self, qkv_cross, gains_cross,
    query, kv, first, first_q, first_kv, held,
):
    rows = near.shape[1]
    for k in range(held.shape[0]):
        row = mods_of(timestep, modulation, k)
        for i in range(6):
            held[k, i : i + 1] = row(i)
    parity, outer, inner, early = places(rows)
    mods = mods_of(timestep, modulation, 0)
    shift, scale = mods(0), mods(1)
    ones = head_ones()
    q_gain = wide_gain(gains[0:1]) * (HD ** -0.5)
    k_gain = wide_gain(gains[1:2])
    own_at = parity * HALF
    near_at = (1 - parity) * rows
    near_from = parity * (rows - HALF)

    sources = [(early_rows[...], own_at + early)]
    sources += [(late_rows[:BLOCK], own_at + outer), (late_rows[BLOCK:], own_at + inner)]
    sources += [
        (near[0, pl.ds(pl.multiple_of(near_from + at, BLOCK), BLOCK)], near_at + at)
        for at in range(0, HALF, BLOCK)
    ]
    queries = []
    for n, (source, to) in enumerate(sources):
        normed = modulated(source, shift, scale)
        if n < 3:
            projected = dot(normed, qkv_self[...])
            queries.append(head_norm(projected[:, :HW], q_gain, ones))
            projected = projected[:, HW:]
        else:
            projected = dot(normed, qkv_self[:, HW:])
        to = pl.multiple_of(to, BLOCK)
        kv[pl.ds(to, BLOCK), :HW] = head_norm(projected[:, :HW], k_gain, ones)
        kv[pl.ds(to, BLOCK), HW:] = projected[:, HW:].astype(BF16)
    query[:BLOCK] = queries[1]
    query[BLOCK:] = queries[2]

    window = rows + HALF
    bias = window_bias(window, 0)
    attended = []
    for at in range(0, HW, SLAB):
        raised, _ = raised_scores(queries[0][:, at : at + SLAB], kv[:, at : at + SLAB], bias)
        out, total = weighted(raised, kv[:, HW + at : HW + at + SLAB])
        attended.append((out / total).astype(BF16))
    attended = jnp.concatenate(attended, axis=1)

    f = first_of(early_rows[...], attended, out_self, mods(2))
    first[...] = f
    first_q[...], first_kv[:, :HW], first_kv[:, HW:] = projected_cross(
        f, mods, qkv_cross, gains_cross, ones, True
    )


def part_kernel(query, kv, part_out, part_sum, part_top):
    parity = lax.rem(lax.axis_index("tm"), 2)
    for n, width in ((0, HALF), (1, BLOCK)):
        start = pl.multiple_of(parity * width, BLOCK)
        count = kv.shape[0] - width
        bias = window_bias(count, (1 - parity) * width)
        to = slice(n * BLOCK, (n + 1) * BLOCK)
        for at in range(0, HW, SLAB):
            cols = slice(at, at + SLAB)
            raised, top = raised_scores(
                query[to, cols], kv[pl.ds(start, count), cols], bias
            )
            out, total = weighted(raised, kv[pl.ds(start, count), HW + at : HW + at + SLAB])
            part_out[to, cols] = out
            part_sum[to, cols] = total
            part_top[to, cols] = by_head(jnp.broadcast_to(top, (2 * BLOCK, SLAB)))


def far_keys(rows, held, qkv_self, gains):
    mods = mods_held(held, 0)
    normed = modulated(rows, mods(0), mods(1))
    keys = dot(normed, qkv_self[:, HW : 2 * HW])
    values = dot(normed, qkv_self[:, 2 * HW :]).astype(BF16)
    return head_norm(keys, wide_gain(gains[1:2]), head_ones()), values


def far_bias(rows, block_start, outermost):
    place = lax.axis_index("tm")
    below = -2 * BLOCK if outermost else -BLOCK
    start = jnp.where(lax.rem(place, 2) == 0, below, rows + (BLOCK if outermost else 0))
    total = rows * lax.axis_size("tm")
    return window_bias(BLOCK, start - block_start + HALF, place * rows + start, total)


def far_attend(block, bias, query, keys, values, part_out, part_sum, part_top, attended):
    to = slice(block * BLOCK, (block + 1) * BLOCK)
    for at in range(0, HW, SLAB):
        cols = slice(at, at + SLAB)
        raised, top = raised_scores(query[to, cols], keys[:, cols], bias)
        out, summed = weighted(raised, values[:, cols])
        top = by_head(jnp.broadcast_to(top, (2 * BLOCK, SLAB)))
        both = jnp.maximum(top, part_top[to, cols])
        here = jnp.exp(top - both)
        before = jnp.exp(part_top[to, cols] - both)
        out = out * here + part_out[to, cols] * before
        summed = summed * here + part_sum[to, cols] * before
        attended[:, cols] = (out / summed).astype(BF16)


def far_inner_kernel(rows, held, far, qkv_self, gains, query, *refs):
    parts, (attended, kv) = refs[:3], refs[-2:]
    keys, values = far_keys(far[:BLOCK], held, qkv_self, gains)
    far_attend(1, far_bias(rows, rows - HALF, False), query, keys, values, *parts, attended)
    kv[:, :HW], kv[:, HW:] = keys, values


def far_outer_kernel(rows, held, far, qkv_self, gains, query, *refs):
    *parts, kv, attended = refs
    keys, values = far_keys(far[BLOCK:], held, qkv_self, gains)
    keys = jnp.concatenate([kv[:, :HW], keys], axis=0)
    values = jnp.concatenate([kv[:, HW:], values], axis=0)
    start = lax.rem(lax.axis_index("tm"), 2) * HALF
    bias = [far_bias(rows, start, outermost) for outermost in (False, True)]
    far_attend(0, jnp.concatenate(bias, axis=1), query, keys, values, *parts, attended)


def first_of(frames, attended, weight, gate):
    mixed = dot(attended, weight[...])
    return (frames.astype(F32) + gate * mixed).astype(BF16)


def projected_cross(first, mods, weight, gains, ones, with_query):
    normed = modulated(first, mods(3), mods(4))
    raw = [dot(normed, weight[:, at : at + HW]) for at in range(0 if with_query else HW, 3 * HW, HW)]
    query = head_norm(raw[0], wide_gain(gains[0:1]), ones) if with_query else None
    keys = head_norm(raw[-2], wide_gain(gains[1:2]), ones)
    return query, keys, raw[-1].astype(BF16)


def finished(first, attended, weight, gate):
    out = dot(attended, weight[...]).astype(BF16)
    return (first.astype(F32) + gate * out.astype(F32)).astype(BF16)


def own_kernel(held, frames, inner, outer, out_self, qkv_cross, gains, first, query, kv):
    mods = mods_held(held, 0)
    ones = head_ones()
    parts = [slice(0, BLOCK), slice(BLOCK, HALF)]
    mixed = [dot(attended[...], out_self[...]) for attended in (outer, inner)]
    gains = [wide_gain(gains[i : i + 1]) for i in range(2)]

    def normed(n):
        f = (frames[parts[n]].astype(F32) + mods(2) * mixed[n]).astype(BF16)
        first[parts[n]] = f
        return modulated(f, mods(3), mods(4))

    rows = normed(0)
    for n, part in enumerate(parts):
        raw = [dot(rows, qkv_cross[:, at : at + HW]) for at in (2 * HW, 0, HW)]
        if n + 1 < len(parts):
            rows = normed(n + 1)
        kv[part, HW:] = raw[0].astype(BF16)
        query[part] = head_norm(raw[1], gains[0], ones)
        kv[part, :HW] = head_norm(raw[2], gains[1], ones)


def early_kernel(_, held, first, query, kv, out_cross, *refs):
    others, out = refs[:-1], refs[-1]
    keys = [each[:, :HW] for each in (kv, *others)]
    values = [each[:, HW:] for each in (kv, *others)]
    mixed = cross_attend(query[...], keys, values, head_ones())
    out[...] = finished(first[...], mixed, out_cross, mods_held(held, 0)(5))


def late_block(block, held, first, query, kv, others, their_frames, out_self, qkv_cross, gains, out_cross):
    ones = head_ones()
    part = slice(block * BLOCK, (block + 1) * BLOCK)
    keys, values = [kv[part, :HW]], [kv[part, HW:]]
    for n, (attended, source) in enumerate(zip(others, their_frames)):
        mods = mods_held(held, n + 1)
        g = first_of(source[part], attended[...], out_self, mods(2))
        _, k, v = projected_cross(g, mods, qkv_cross, gains, ones, False)
        keys.append(k)
        values.append(v)
    mixed = cross_attend(query[part], keys, values, ones)
    return finished(first[part], mixed, out_cross, mods_held(held, 0)(5))


def inner_kernel(count, _, held, first, query, kv, *refs):
    others, their_frames = refs[: count - 1], refs[count - 1 : 2 * count - 2]
    *weights, out = refs[2 * count - 2 :]
    out[...] = late_block(1, held, first, query, kv, others, their_frames, *weights)


def outer_kernel(count, held, first, query, kv, early_out, inner_out, *refs):
    others, their_frames = refs[: count - 1], refs[count - 1 : 2 * count - 2]
    *weights, out, outer_out, sems = refs[2 * count - 2 :]
    _, outer, inner, early = places(out.shape[1])
    copies = [
        pltpu.make_async_copy(source, out.at[0, pl.ds(at, BLOCK)], sems.at[n])
        for n, (source, at) in enumerate(((early_out, early), (inner_out, inner), (outer_out, outer)))
    ]
    copies[0].start()
    copies[1].start()
    outer_out[...] = late_block(0, held, first, query, kv, others, their_frames, *weights)
    copies[2].start()
    for copy in copies:
        copy.wait()


def on_device(
    frames,
    timestep,
    modulation,
    qkv_self,
    out_self,
    qk_gain_self,
    qkv_cross,
    out_cross,
    qk_gain_cross,
):
    stems = lax.axis_size("stem")
    count = lax.axis_size("tm")
    rows = frames.shape[1]
    assert count % 2 == 0 and rows == HALF + BLOCK
    modulation = jnp.transpose(modulation, (1, 0, 2))
    inside = [(i, i ^ 1) for i in range(count)]
    across = [(i, i + 2) for i in range(0, count - 2, 2)]
    across += [(i + 3, i + 1) for i in range(0, count - 2, 2)]
    across += [(count - 2, count - 1), (1, 0)]

    def to_stems(array):
        return [
            lax.ppermute(array, "stem", [(i, (i + k) % stems) for i in range(stems)])
            for k in range(1, stems)
        ]

    def call(kernel, name, us, outs, *args, scratch=(), in_specs=None, out_specs=None):
        out_specs = out_specs or jax.tree.map(lambda _: VMEM, outs)
        return pl.pallas_call(
            kernel,
            out_shape=outs,
            in_specs=in_specs or [VMEM] * len(args),
            out_specs=out_specs,
            scratch_shapes=list(scratch),
            compiler_params=params(),
            cost_estimate=cost(us),
            name=name,
        )(*args)

    half = shape(BLOCK, D)
    late_rows, early_rows = call(
        split_kernel, "split", 6, (shape(HALF, D), half), frames,
        scratch=[pltpu.SemaphoreType.DMA((3,))], in_specs=[ANY], out_specs=(ANY, ANY),
    )
    their_frames = to_stems(late_rows)
    near = lax.ppermute(frames, "tm", inside)
    mate_rows = call(mate_kernel, "mate", 0.1, shape(HALF, D), near)
    far = lax.ppermute(mate_rows, "tm", across)

    late, block, part = shape(HALF, HW), shape(BLOCK, HW), shape(HALF, HW, dtype=F32)
    query, kv, first_early, q_early, kv_early, held = call(
        near_kernel, "near", 2,
        (late, shape(rows + HALF, 2 * HW), half, block, half, shape(stems, 8, D, dtype=F32)),
        timestep, modulation, early_rows, late_rows, near, qkv_self, qk_gain_self, out_self, qkv_cross, qk_gain_cross,
        in_specs=[SMEM] + [VMEM] * 9,
    )
    others_early = to_stems(kv_early)
    parts = call(part_kernel, "part", 0.3, (part, part, part), query, kv)

    self_weights = (qkv_self, qk_gain_self)
    att_inner, far_kv = call(
        lambda *refs: far_inner_kernel(rows, *refs), "far_inner", 2, (block, half),
        held, far, *self_weights, query, *parts, *their_frames,
        in_specs=[VMEM] * 8 + [ANY] * (stems - 1),
    )
    others_inner = to_stems(att_inner)
    att_outer = call(
        lambda *refs: far_outer_kernel(rows, *refs), "far_outer", 0.3, block,
        held, far, *self_weights, query, *parts, far_kv,
    )
    others_outer = to_stems(att_outer)

    weights = (out_self, qkv_cross, qk_gain_cross)
    own = call(
        own_kernel, "own", 0.3, (shape(HALF, D), late, shape(HALF, D)),
        held, late_rows, att_inner, att_outer, *weights,
    )
    early_out = call(
        early_kernel, "early", 0.3, half, own[0], held, first_early, q_early, kv_early, out_cross, *others_early,
        in_specs=[ANY] + [VMEM] * (4 + stems),
    )
    inner_out = call(
        lambda *refs: inner_kernel(stems, *refs), "inner", 0.6, half,
        early_out, held, *own, *others_inner, *their_frames, *weights, out_cross,
        in_specs=[ANY] + [VMEM] * (6 + 2 * stems),
    )
    return call(
        lambda *refs: outer_kernel(stems, *refs), "outer", 0.3, shape(1, rows, D),
        held, *own, early_out, inner_out, *others_outer, *their_frames, *weights, out_cross,
        scratch=[pltpu.VMEM((BLOCK, D), BF16), pltpu.SemaphoreType.DMA((3,))], out_specs=ANY,
    )


def solution(mesh):
    return jax.shard_map(
        on_device,
        mesh=mesh,
        in_specs=(P("stem", "tm", None), P(), P(), P(), P(), P(), P(), P(), P()),
        out_specs=P("stem", "tm", None),
        check_vma=False,
    )
```

```python
import jax
import jax.numpy as jnp
from jax import lax
from jax.experimental import pallas as pl
from jax.experimental.pallas import tpu as pltpu
from jax.sharding import PartitionSpec as P

D = 1024
H = 8
HD = 64
HW = H * HD
HALF = 256
BLOCK = 128
SLAB = 128
EPS = 1e-06
NEG = -1e30
F32 = jnp.float32
BF16 = jnp.bfloat16
VMEM = pl.BlockSpec(memory_space=pltpu.VMEM)
SMEM = pl.BlockSpec(memory_space=pltpu.SMEM)
ANY = pl.BlockSpec(memory_space=pl.ANY)
LIMIT = 16 * 1024 * 1024


def cost(us):
    return pl.CostEstimate(flops=int(us * 1e9), bytes_accessed=int(us * 3e6), transcendentals=0)


def params():
    return pltpu.CompilerParams(vmem_limit_bytes=LIMIT)


def shape(*dims, dtype=BF16):
    return jax.ShapeDtypeStruct(dims, dtype)


def dot(a, b, dims=((1,), (0,))):
    return lax.dot_general(a, b, (dims, ((), ())), preferred_element_type=F32)


def modulated(rows, shift, scale):
    values = rows.astype(F32)
    centred = values - jnp.mean(values, axis=-1, keepdims=True)
    spread = jnp.mean(centred * centred, axis=-1, keepdims=True)
    normed = centred * lax.rsqrt(spread + EPS)
    return (normed * (1.0 + scale) + shift).astype(BF16)


def head_ones():
    row = lax.broadcasted_iota(jnp.int32, (2 * SLAB, 2 * SLAB), 0) // HD
    col = lax.broadcasted_iota(jnp.int32, (2 * SLAB, 2 * SLAB), 1) // HD
    return jnp.where(row == col, 1.0, 0.0).astype(BF16)


def head_sums(values, ones):
    parts = [dot(values[:, at : at + 2 * SLAB], ones) for at in range(0, HW, 2 * SLAB)]
    return jnp.concatenate(parts, axis=1)


def exact_head_sums(values, ones):
    high = values.astype(BF16)
    low = (values - high.astype(F32)).astype(BF16)
    return head_sums(high, ones) + head_sums(low, ones)


def head_norm(values, gain, ones):
    mean = head_sums((values * values).astype(BF16), ones) * (1.0 / HD)
    return (values * lax.rsqrt(mean + EPS) * gain).astype(BF16)


def wide_gain(gain):
    return jnp.concatenate([gain] * H, axis=1)


def window_bias(keys, ahead, first_frame=0, total=1 << 30):
    i = lax.broadcasted_iota(jnp.int32, (BLOCK, keys), 0)
    j = lax.broadcasted_iota(jnp.int32, (BLOCK, keys), 1)
    frame = first_frame + j
    keep = (j + ahead >= i) & (j + ahead <= i + 2 * HALF) & (frame >= 0) & (frame < total)
    return jnp.where(keep, 0.0, NEG)


def left_half():
    return lax.broadcasted_iota(jnp.int32, (BLOCK, SLAB), 1) < HD


def by_head(pair):
    return jnp.where(left_half(), pair[:BLOCK], pair[BLOCK:])


def raised_scores(query, keys, bias):
    half, zero = left_half(), jnp.zeros_like(query)
    pair = jnp.concatenate([jnp.where(half, query, zero), jnp.where(half, zero, query)], axis=0)
    scores = dot(pair, keys, ((1,), (1,)))
    scores = jnp.concatenate([scores[:BLOCK] + bias, scores[BLOCK:] + bias], axis=0)
    top = jnp.max(scores, axis=-1, keepdims=True)
    return jnp.exp(scores - top).astype(BF16), top


def weighted(raised, values):
    summed = dot(raised, jnp.concatenate([values, jnp.ones_like(values)], axis=1))
    return by_head(summed[:, :SLAB]), by_head(summed[:, SLAB:])


def cross_attend(query, keys, values, ones):
    query = query.astype(F32)
    base = keys[0].astype(F32)
    scores = [
        exact_head_sums(query * (k.astype(F32) - base), ones) * (HD ** -0.5) for k in keys[1:]
    ]
    top = jnp.zeros_like(query)
    for s in scores:
        top = jnp.maximum(top, s)
    raised = [jnp.exp(-top)] + [jnp.exp(s - top) for s in scores]
    total = raised[0]
    for r in raised[1:]:
        total = total + r
    scale = 1.0 / total
    out = jnp.zeros_like(query)
    for r, v in zip(raised, values):
        out = out + (r * scale).astype(BF16).astype(F32) * v.astype(F32)
    return out.astype(BF16)


def mods_of(timestep, modulation, back):
    count = lax.axis_size("stem")
    step = timestep[lax.rem(lax.axis_index("stem") + count - back, count)]
    return lambda i: modulation[i, pl.ds(step, 1), :]


def mods_held(held, back):
    return lambda i: held[back, i : i + 1]


def places(rows):
    parity = lax.rem(lax.axis_index("tm"), 2)
    outer = pl.multiple_of(parity * HALF, BLOCK)
    early = pl.multiple_of((1 - parity) * HALF, BLOCK)
    return parity, outer, rows - HALF, early


def split_kernel(frames, late_rows, early_rows, sems):
    _, outer, inner, early = places(frames.shape[1])
    targets = (late_rows.at[pl.ds(0, BLOCK)], late_rows.at[pl.ds(BLOCK, BLOCK)], early_rows)
    copies = [
        pltpu.make_async_copy(frames.at[0, pl.ds(at, BLOCK)], to, sems.at[n])
        for n, (at, to) in enumerate(zip((outer, inner, early), targets))
    ]
    for copy in copies:
        copy.start()
    for copy in copies:
        copy.wait()


def mate_kernel(mate, outer_rows, inner_rows):
    _, _, inner, outer = places(mate.shape[1])
    outer_rows[...] = mate[0, pl.ds(outer, BLOCK)]
    inner_rows[...] = mate[0, inner : inner + BLOCK]


def near_kernel(
    timestep, modulation, early_rows, late_rows, near, qkv_self, gains, out_self, qkv_cross, gains_cross,
    query, kv, first, first_q, first_kv, held,
):
    rows = near.shape[1]
    for k in range(held.shape[0]):
        row = mods_of(timestep, modulation, k)
        for i in range(6):
            held[k, i : i + 1] = row(i)
    parity, outer, inner, early = places(rows)
    mods = mods_of(timestep, modulation, 0)
    shift, scale = mods(0), mods(1)
    ones = head_ones()
    q_gain = wide_gain(gains[0:1]) * (HD ** -0.5)
    k_gain = wide_gain(gains[1:2])
    own_at = parity * HALF
    near_at = (1 - parity) * rows
    near_from = parity * (rows - HALF)

    sources = [(early_rows[...], own_at + early)]
    sources += [(late_rows[:BLOCK], own_at + outer), (late_rows[BLOCK:], own_at + inner)]
    sources += [
        (near[0, pl.ds(pl.multiple_of(near_from + at, BLOCK), BLOCK)], near_at + at)
        for at in range(0, HALF, BLOCK)
    ]
    queries = []
    for n, (source, to) in enumerate(sources):
        normed = modulated(source, shift, scale)
        if n < 3:
            projected = dot(normed, qkv_self[...])
            queries.append(head_norm(projected[:, :HW], q_gain, ones))
            projected = projected[:, HW:]
        else:
            projected = dot(normed, qkv_self[:, HW:])
        to = pl.multiple_of(to, BLOCK)
        kv[pl.ds(to, BLOCK), :HW] = head_norm(projected[:, :HW], k_gain, ones)
        kv[pl.ds(to, BLOCK), HW:] = projected[:, HW:].astype(BF16)
    query[:BLOCK] = queries[1]
    query[BLOCK:] = queries[2]

    window = rows + HALF
    bias = window_bias(window, 0)
    attended = []
    for at in range(0, HW, SLAB):
        raised, _ = raised_scores(queries[0][:, at : at + SLAB], kv[:, at : at + SLAB], bias)
        out, total = weighted(raised, kv[:, HW + at : HW + at + SLAB])
        attended.append((out / total).astype(BF16))
    attended = jnp.concatenate(attended, axis=1)

    f = first_of(early_rows[...], attended, out_self, mods(2))
    first[...] = f
    first_q[...], first_kv[:, :HW], first_kv[:, HW:] = projected_cross(
        f, mods, qkv_cross, gains_cross, ones, True
    )


def part_kernel(query, kv, part_out, part_sum, part_top):
    parity = lax.rem(lax.axis_index("tm"), 2)
    for n, width in ((0, HALF), (1, BLOCK)):
        start = pl.multiple_of(parity * width, BLOCK)
        count = kv.shape[0] - width
        bias = window_bias(count, (1 - parity) * width)
        to = slice(n * BLOCK, (n + 1) * BLOCK)
        for at in range(0, HW, SLAB):
            cols = slice(at, at + SLAB)
            raised, top = raised_scores(
                query[to, cols], kv[pl.ds(start, count), cols], bias
            )
            out, total = weighted(raised, kv[pl.ds(start, count), HW + at : HW + at + SLAB])
            part_out[to, cols] = out
            part_sum[to, cols] = total
            part_top[to, cols] = by_head(jnp.broadcast_to(top, (2 * BLOCK, SLAB)))


def far_keys(rows, held, qkv_self, gains):
    mods = mods_held(held, 0)
    normed = modulated(rows, mods(0), mods(1))
    keys = dot(normed, qkv_self[:, HW : 2 * HW])
    values = dot(normed, qkv_self[:, 2 * HW :]).astype(BF16)
    return head_norm(keys, wide_gain(gains[1:2]), head_ones()), values


def far_bias(rows, block_start, outermost):
    place = lax.axis_index("tm")
    below = -2 * BLOCK if outermost else -BLOCK
    start = jnp.where(lax.rem(place, 2) == 0, below, rows + (BLOCK if outermost else 0))
    total = rows * lax.axis_size("tm")
    return window_bias(BLOCK, start - block_start + HALF, place * rows + start, total)


def far_attend(block, bias, query, keys, values, part_out, part_sum, part_top, attended):
    to = slice(block * BLOCK, (block + 1) * BLOCK)
    for at in range(0, HW, SLAB):
        cols = slice(at, at + SLAB)
        raised, top = raised_scores(query[to, cols], keys[:, cols], bias)
        out, summed = weighted(raised, values[:, cols])
        top = by_head(jnp.broadcast_to(top, (2 * BLOCK, SLAB)))
        both = jnp.maximum(top, part_top[to, cols])
        here = jnp.exp(top - both)
        before = jnp.exp(part_top[to, cols] - both)
        out = out * here + part_out[to, cols] * before
        summed = summed * here + part_sum[to, cols] * before
        attended[:, cols] = (out / summed).astype(BF16)


def far_inner_kernel(rows, held, far, qkv_self, gains, query, *refs):
    *parts, attended, kv = refs
    keys, values = far_keys(far[...], held, qkv_self, gains)
    far_attend(1, far_bias(rows, rows - HALF, False), query, keys, values, *parts, attended)
    kv[:, :HW], kv[:, HW:] = keys, values


def far_outer_kernel(rows, held, far, qkv_self, gains, query, *refs):
    *parts, kv, attended = refs
    keys, values = far_keys(far[...], held, qkv_self, gains)
    keys = jnp.concatenate([kv[:, :HW], keys], axis=0)
    values = jnp.concatenate([kv[:, HW:], values], axis=0)
    start = lax.rem(lax.axis_index("tm"), 2) * HALF
    bias = [far_bias(rows, start, outermost) for outermost in (False, True)]
    far_attend(0, jnp.concatenate(bias, axis=1), query, keys, values, *parts, attended)


def first_of(frames, attended, weight, gate):
    mixed = dot(attended, weight[...])
    return (frames.astype(F32) + gate * mixed).astype(BF16)


def projected_cross(first, mods, weight, gains, ones, with_query):
    normed = modulated(first, mods(3), mods(4))
    raw = [dot(normed, weight[:, at : at + HW]) for at in range(0 if with_query else HW, 3 * HW, HW)]
    query = head_norm(raw[0], wide_gain(gains[0:1]), ones) if with_query else None
    keys = head_norm(raw[-2], wide_gain(gains[1:2]), ones)
    return query, keys, raw[-1].astype(BF16)


def finished(first, attended, weight, gate):
    out = dot(attended, weight[...]).astype(BF16)
    return (first.astype(F32) + gate * out.astype(F32)).astype(BF16)


def own_kernel(held, frames, inner, outer, out_self, qkv_cross, gains, first, query, kv):
    mods = mods_held(held, 0)
    ones = head_ones()
    parts = [slice(0, BLOCK), slice(BLOCK, HALF)]
    mixed = [dot(attended[...], out_self[...]) for attended in (outer, inner)]
    gains = [wide_gain(gains[i : i + 1]) for i in range(2)]

    def normed(n):
        f = (frames[parts[n]].astype(F32) + mods(2) * mixed[n]).astype(BF16)
        first[parts[n]] = f
        return modulated(f, mods(3), mods(4))

    rows = normed(0)
    for n, part in enumerate(parts):
        raw = [dot(rows, qkv_cross[:, at : at + HW]) for at in (2 * HW, 0, HW)]
        if n + 1 < len(parts):
            rows = normed(n + 1)
        kv[part, HW:] = raw[0].astype(BF16)
        query[part] = head_norm(raw[1], gains[0], ones)
        kv[part, :HW] = head_norm(raw[2], gains[1], ones)


def early_kernel(_, held, first, query, kv, out_cross, *refs):
    others, out = refs[:-1], refs[-1]
    keys = [each[:, :HW] for each in (kv, *others)]
    values = [each[:, HW:] for each in (kv, *others)]
    mixed = cross_attend(query[...], keys, values, head_ones())
    out[...] = finished(first[...], mixed, out_cross, mods_held(held, 0)(5))


def late_block(block, held, first, query, kv, others, their_frames, out_self, qkv_cross, gains, out_cross):
    ones = head_ones()
    part = slice(block * BLOCK, (block + 1) * BLOCK)
    keys, values = [kv[part, :HW]], [kv[part, HW:]]
    for n, (attended, source) in enumerate(zip(others, their_frames)):
        mods = mods_held(held, n + 1)
        g = first_of(source[part], attended[...], out_self, mods(2))
        _, k, v = projected_cross(g, mods, qkv_cross, gains, ones, False)
        keys.append(k)
        values.append(v)
    mixed = cross_attend(query[part], keys, values, ones)
    return finished(first[part], mixed, out_cross, mods_held(held, 0)(5))


def inner_kernel(count, _, held, first, query, kv, *refs):
    others, their_frames = refs[: count - 1], refs[count - 1 : 2 * count - 2]
    *weights, out = refs[2 * count - 2 :]
    out[...] = late_block(1, held, first, query, kv, others, their_frames, *weights)


def outer_kernel(count, held, first, query, kv, early_out, inner_out, *refs):
    others, their_frames = refs[: count - 1], refs[count - 1 : 2 * count - 2]
    *weights, out, outer_out, sems = refs[2 * count - 2 :]
    _, outer, inner, early = places(out.shape[1])
    copies = [
        pltpu.make_async_copy(source, out.at[0, pl.ds(at, BLOCK)], sems.at[n])
        for n, (source, at) in enumerate(((early_out, early), (inner_out, inner), (outer_out, outer)))
    ]
    copies[0].start()
    copies[1].start()
    outer_out[...] = late_block(0, held, first, query, kv, others, their_frames, *weights)
    copies[2].start()
    for copy in copies:
        copy.wait()


def on_device(
    frames,
    timestep,
    modulation,
    qkv_self,
    out_self,
    qk_gain_self,
    qkv_cross,
    out_cross,
    qk_gain_cross,
):
    stems = lax.axis_size("stem")
    count = lax.axis_size("tm")
    rows = frames.shape[1]
    assert count % 2 == 0 and rows == HALF + BLOCK
    modulation = jnp.transpose(modulation, (1, 0, 2))
    inside = [(i, i ^ 1) for i in range(count)]
    across = [(i, i + 2) for i in range(0, count - 2, 2)]
    across += [(i + 3, i + 1) for i in range(0, count - 2, 2)]
    across += [(count - 2, count - 1), (1, 0)]

    def to_stems(array):
        return [
            lax.ppermute(array, "stem", [(i, (i + k) % stems) for i in range(stems)])
            for k in range(1, stems)
        ]

    def call(kernel, name, us, outs, *args, scratch=(), in_specs=None, out_specs=None):
        out_specs = out_specs or jax.tree.map(lambda _: VMEM, outs)
        return pl.pallas_call(
            kernel,
            out_shape=outs,
            in_specs=in_specs or [VMEM] * len(args),
            out_specs=out_specs,
            scratch_shapes=list(scratch),
            compiler_params=params(),
            cost_estimate=cost(us),
            name=name,
        )(*args)

    half = shape(BLOCK, D)
    late_rows, early_rows = call(
        split_kernel, "split", 4, (shape(HALF, D), half), frames,
        scratch=[pltpu.SemaphoreType.DMA((3,))], in_specs=[ANY], out_specs=(ANY, ANY),
    )
    their_frames = to_stems(late_rows)
    near = lax.ppermute(frames, "tm", inside)
    mate_outer, mate_inner = call(mate_kernel, "mate", 0.1, (half, half), near)
    far = lax.ppermute(mate_outer, "tm", across)
    farther = lax.ppermute(mate_inner, "tm", across)

    late, block, part = shape(HALF, HW), shape(BLOCK, HW), shape(HALF, HW, dtype=F32)
    query, kv, first_early, q_early, kv_early, held = call(
        near_kernel, "near", 0.12,
        (late, shape(rows + HALF, 2 * HW), half, block, half, shape(stems, 8, D, dtype=F32)),
        timestep, modulation, early_rows, late_rows, near, qkv_self, qk_gain_self, out_self, qkv_cross, qk_gain_cross,
        in_specs=[SMEM] + [VMEM] * 9,
    )
    others_early = to_stems(kv_early)
    parts = call(part_kernel, "part", 0.04, (part, part, part), query, kv)

    self_weights = (qkv_self, qk_gain_self)
    att_inner, far_kv = call(
        lambda *refs: far_inner_kernel(rows, *refs), "far_inner", 0.04, (block, half),
        held, far, *self_weights, query, *parts,
    )
    others_inner = to_stems(att_inner)
    att_outer = call(
        lambda *refs: far_outer_kernel(rows, *refs), "far_outer", 0.006, block,
        held, farther, *self_weights, query, *parts, far_kv,
    )
    others_outer = to_stems(att_outer)

    weights = (out_self, qkv_cross, qk_gain_cross)
    own = call(
        own_kernel, "own", 0.02, (shape(HALF, D), late, shape(HALF, D)),
        held, late_rows, att_inner, att_outer, *weights,
    )
    early_out = call(
        early_kernel, "early", 0.012, half, own[0], held, first_early, q_early, kv_early, out_cross, *others_early,
        in_specs=[ANY] + [VMEM] * (4 + stems),
    )
    inner_out = call(
        lambda *refs: inner_kernel(stems, *refs), "inner", 0.04, half,
        early_out, held, *own, *others_inner, *their_frames, *weights, out_cross,
        in_specs=[ANY] + [VMEM] * (6 + 2 * stems),
    )
    return call(
        lambda *refs: outer_kernel(stems, *refs), "outer", 2, shape(1, rows, D),
        held, *own, early_out, inner_out, *others_outer, *their_frames, *weights, out_cross,
        scratch=[pltpu.VMEM((BLOCK, D), BF16), pltpu.SemaphoreType.DMA((3,))], out_specs=ANY,
    )


def solution(mesh):
    return jax.shard_map(
        on_device,
        mesh=mesh,
        in_specs=(P("stem", "tm", None), P(), P(), P(), P(), P(), P(), P(), P()),
        out_specs=P("stem", "tm", None),
        check_vma=False,
    )
```

```python
import jax
import jax.numpy as jnp
from jax import lax
from jax.experimental import pallas as pl
from jax.experimental.pallas import tpu as pltpu
from jax.sharding import PartitionSpec as P

D = 1024
H = 8
HD = 64
HW = H * HD
HALF = 256
BLOCK = 128
SLAB = 128
EPS = 1e-06
NEG = -1e30
F32 = jnp.float32
BF16 = jnp.bfloat16
VMEM = pl.BlockSpec(memory_space=pltpu.VMEM)
SMEM = pl.BlockSpec(memory_space=pltpu.SMEM)
ANY = pl.BlockSpec(memory_space=pl.ANY)
LIMIT = 16 * 1024 * 1024


def cost(us):
    return pl.CostEstimate(flops=int(us * 1e9), bytes_accessed=int(us * 3e6), transcendentals=0)


def params():
    return pltpu.CompilerParams(vmem_limit_bytes=LIMIT)


def shape(*dims, dtype=BF16):
    return jax.ShapeDtypeStruct(dims, dtype)


def dot(a, b, dims=((1,), (0,))):
    return lax.dot_general(a, b, (dims, ((), ())), preferred_element_type=F32)


def modulated(rows, shift, scale):
    values = rows.astype(F32)
    centred = values - jnp.mean(values, axis=-1, keepdims=True)
    spread = jnp.mean(centred * centred, axis=-1, keepdims=True)
    normed = centred * lax.rsqrt(spread + EPS)
    return (normed * (1.0 + scale) + shift).astype(BF16)


def head_ones():
    row = lax.broadcasted_iota(jnp.int32, (2 * SLAB, 2 * SLAB), 0) // HD
    col = lax.broadcasted_iota(jnp.int32, (2 * SLAB, 2 * SLAB), 1) // HD
    return jnp.where(row == col, 1.0, 0.0).astype(BF16)


def head_sums(values, ones):
    parts = [dot(values[:, at : at + 2 * SLAB], ones) for at in range(0, HW, 2 * SLAB)]
    return jnp.concatenate(parts, axis=1)


def exact_head_sums(values, ones):
    high = values.astype(BF16)
    low = (values - high.astype(F32)).astype(BF16)
    return head_sums(high, ones) + head_sums(low, ones)


def head_norm(values, gain, ones):
    mean = head_sums((values * values).astype(BF16), ones) * (1.0 / HD)
    return (values * lax.rsqrt(mean + EPS) * gain).astype(BF16)


def wide_gain(gain):
    return jnp.concatenate([gain] * H, axis=1)


def window_bias(keys, ahead, first_frame=0, total=1 << 30):
    i = lax.broadcasted_iota(jnp.int32, (BLOCK, keys), 0)
    j = lax.broadcasted_iota(jnp.int32, (BLOCK, keys), 1)
    frame = first_frame + j
    keep = (j + ahead >= i) & (j + ahead <= i + 2 * HALF) & (frame >= 0) & (frame < total)
    return jnp.where(keep, 0.0, NEG)


def left_half():
    return lax.broadcasted_iota(jnp.int32, (BLOCK, SLAB), 1) < HD


def by_head(pair):
    return jnp.where(left_half(), pair[:BLOCK], pair[BLOCK:])


def raised_scores(query, keys, bias):
    half, zero = left_half(), jnp.zeros_like(query)
    pair = jnp.concatenate([jnp.where(half, query, zero), jnp.where(half, zero, query)], axis=0)
    scores = dot(pair, keys, ((1,), (1,)))
    scores = jnp.concatenate([scores[:BLOCK] + bias, scores[BLOCK:] + bias], axis=0)
    top = jnp.max(scores, axis=-1, keepdims=True)
    return jnp.exp(scores - top).astype(BF16), top


def weighted(raised, values):
    summed = dot(raised, jnp.concatenate([values, jnp.ones_like(values)], axis=1))
    return by_head(summed[:, :SLAB]), by_head(summed[:, SLAB:])


def cross_attend(query, keys, values, ones):
    query = query.astype(F32)
    base = keys[0].astype(F32)
    scores = [
        exact_head_sums(query * (k.astype(F32) - base), ones) * (HD ** -0.5) for k in keys[1:]
    ]
    top = jnp.zeros_like(query)
    for s in scores:
        top = jnp.maximum(top, s)
    raised = [jnp.exp(-top)] + [jnp.exp(s - top) for s in scores]
    total = raised[0]
    for r in raised[1:]:
        total = total + r
    scale = 1.0 / total
    out = jnp.zeros_like(query)
    for r, v in zip(raised, values):
        out = out + (r * scale).astype(BF16).astype(F32) * v.astype(F32)
    return out.astype(BF16)


def mods_of(timestep, modulation, back):
    count = lax.axis_size("stem")
    step = timestep[lax.rem(lax.axis_index("stem") + count - back, count)]
    return lambda i: modulation[i, pl.ds(step, 1), :]


def mods_held(held, back):
    return lambda i: held[back, i : i + 1]


def places(rows):
    parity = lax.rem(lax.axis_index("tm"), 2)
    outer = pl.multiple_of(parity * HALF, BLOCK)
    early = pl.multiple_of((1 - parity) * HALF, BLOCK)
    return parity, outer, rows - HALF, early


def split_kernel(frames, late_rows, early_rows, sems):
    _, outer, inner, early = places(frames.shape[1])
    targets = (late_rows.at[pl.ds(0, BLOCK)], late_rows.at[pl.ds(BLOCK, BLOCK)], early_rows)
    copies = [
        pltpu.make_async_copy(frames.at[0, pl.ds(at, BLOCK)], to, sems.at[n])
        for n, (at, to) in enumerate(zip((outer, inner, early), targets))
    ]
    for copy in copies:
        copy.start()
    for copy in copies:
        copy.wait()


def mate_kernel(mate, outer_rows, inner_rows):
    _, _, inner, outer = places(mate.shape[1])
    outer_rows[...] = mate[0, pl.ds(outer, BLOCK)]
    inner_rows[...] = mate[0, inner : inner + BLOCK]


def near_kernel(
    timestep, modulation, early_rows, late_rows, near, qkv_self, gains, out_self, qkv_cross, gains_cross,
    query, kv, first, first_q, first_k, first_v, held,
):
    rows = near.shape[1]
    for k in range(held.shape[0]):
        row = mods_of(timestep, modulation, k)
        for i in range(6):
            held[k, i : i + 1] = row(i)
    parity, outer, inner, early = places(rows)
    mods = mods_of(timestep, modulation, 0)
    shift, scale = mods(0), mods(1)
    ones = head_ones()
    q_gain = wide_gain(gains[0:1]) * (HD ** -0.5)
    k_gain = wide_gain(gains[1:2])
    own_at = parity * HALF
    near_at = (1 - parity) * rows
    near_from = parity * (rows - HALF)

    sources = [(early_rows[...], own_at + early)]
    sources += [(late_rows[:BLOCK], own_at + outer), (late_rows[BLOCK:], own_at + inner)]
    sources += [
        (near[0, pl.ds(pl.multiple_of(near_from + at, BLOCK), BLOCK)], near_at + at)
        for at in range(0, HALF, BLOCK)
    ]
    queries = []
    for n, (source, to) in enumerate(sources):
        normed = modulated(source, shift, scale)
        if n < 3:
            projected = dot(normed, qkv_self[...])
            queries.append(head_norm(projected[:, :HW], q_gain, ones))
            projected = projected[:, HW:]
        else:
            projected = dot(normed, qkv_self[:, HW:])
        to = pl.multiple_of(to, BLOCK)
        kv[pl.ds(to, BLOCK), :HW] = head_norm(projected[:, :HW], k_gain, ones)
        kv[pl.ds(to, BLOCK), HW:] = projected[:, HW:].astype(BF16)
    query[:BLOCK] = queries[1]
    query[BLOCK:] = queries[2]

    window = rows + HALF
    bias = window_bias(window, 0)
    attended = []
    for at in range(0, HW, SLAB):
        raised, _ = raised_scores(queries[0][:, at : at + SLAB], kv[:, at : at + SLAB], bias)
        out, total = weighted(raised, kv[:, HW + at : HW + at + SLAB])
        attended.append((out / total).astype(BF16))
    attended = jnp.concatenate(attended, axis=1)

    f = first_of(early_rows[...], attended, out_self, mods(2))
    first[...] = f
    first_q[...], first_k[...], first_v[...] = projected_cross(
        f, mods, qkv_cross, gains_cross, ones, True
    )


def part_kernel(query, kv, part_out, part_sum, part_top):
    parity = lax.rem(lax.axis_index("tm"), 2)
    for n, width in ((0, HALF), (1, BLOCK)):
        start = pl.multiple_of(parity * width, BLOCK)
        count = kv.shape[0] - width
        bias = window_bias(count, (1 - parity) * width)
        to = slice(n * BLOCK, (n + 1) * BLOCK)
        for at in range(0, HW, SLAB):
            cols = slice(at, at + SLAB)
            raised, top = raised_scores(
                query[to, cols], kv[pl.ds(start, count), cols], bias
            )
            out, total = weighted(raised, kv[pl.ds(start, count), HW + at : HW + at + SLAB])
            part_out[to, cols] = out
            part_sum[to, cols] = total
            part_top[to, cols] = by_head(jnp.broadcast_to(top, (2 * BLOCK, SLAB)))


def far_keys(rows, held, qkv_self, gains):
    mods = mods_held(held, 0)
    normed = modulated(rows, mods(0), mods(1))
    keys = dot(normed, qkv_self[:, HW : 2 * HW])
    values = dot(normed, qkv_self[:, 2 * HW :]).astype(BF16)
    return head_norm(keys, wide_gain(gains[1:2]), head_ones()), values


def far_bias(rows, block_start, outermost):
    place = lax.axis_index("tm")
    below = -2 * BLOCK if outermost else -BLOCK
    start = jnp.where(lax.rem(place, 2) == 0, below, rows + (BLOCK if outermost else 0))
    total = rows * lax.axis_size("tm")
    return window_bias(BLOCK, start - block_start + HALF, place * rows + start, total)


def far_attend(block, bias, query, keys, values, part_out, part_sum, part_top, attended):
    to = slice(block * BLOCK, (block + 1) * BLOCK)
    for at in range(0, HW, SLAB):
        cols = slice(at, at + SLAB)
        raised, top = raised_scores(query[to, cols], keys[:, cols], bias)
        out, summed = weighted(raised, values[:, cols])
        top = by_head(jnp.broadcast_to(top, (2 * BLOCK, SLAB)))
        both = jnp.maximum(top, part_top[to, cols])
        here = jnp.exp(top - both)
        before = jnp.exp(part_top[to, cols] - both)
        out = out * here + part_out[to, cols] * before
        summed = summed * here + part_sum[to, cols] * before
        attended[:, cols] = (out / summed).astype(BF16)


def far_inner_kernel(rows, held, far, qkv_self, gains, query, *refs):
    *parts, attended, kv = refs
    keys, values = far_keys(far[...], held, qkv_self, gains)
    far_attend(1, far_bias(rows, rows - HALF, False), query, keys, values, *parts, attended)
    kv[:, :HW], kv[:, HW:] = keys, values


def far_outer_kernel(rows, early_values, held, far, qkv_self, gains, query, *refs):
    *parts, kv, attended, passed = refs
    passed[...] = early_values[...]
    keys, values = far_keys(far[...], held, qkv_self, gains)
    keys = jnp.concatenate([kv[:, :HW], keys], axis=0)
    values = jnp.concatenate([kv[:, HW:], values], axis=0)
    start = lax.rem(lax.axis_index("tm"), 2) * HALF
    bias = [far_bias(rows, start, outermost) for outermost in (False, True)]
    far_attend(0, jnp.concatenate(bias, axis=1), query, keys, values, *parts, attended)


def first_of(frames, attended, weight, gate):
    mixed = dot(attended, weight[...])
    return (frames.astype(F32) + gate * mixed).astype(BF16)


def projected_cross(first, mods, weight, gains, ones, with_query):
    normed = modulated(first, mods(3), mods(4))
    raw = [dot(normed, weight[:, at : at + HW]) for at in range(0 if with_query else HW, 3 * HW, HW)]
    query = head_norm(raw[0], wide_gain(gains[0:1]), ones) if with_query else None
    keys = head_norm(raw[-2], wide_gain(gains[1:2]), ones)
    return query, keys, raw[-1].astype(BF16)


def finished(first, attended, weight, gate):
    out = dot(attended, weight[...]).astype(BF16)
    return (first.astype(F32) + gate * out.astype(F32)).astype(BF16)


def own_kernel(held, frames, inner, outer, out_self, qkv_cross, gains, *refs):
    first, query, kv = refs[-3:]
    mods = mods_held(held, 0)
    ones = head_ones()
    parts = [slice(0, BLOCK), slice(BLOCK, HALF)]
    mixed = [dot(attended[...], out_self[...]) for attended in (outer, inner)]
    gains = [wide_gain(gains[i : i + 1]) for i in range(2)]

    def normed(n):
        f = (frames[parts[n]].astype(F32) + mods(2) * mixed[n]).astype(BF16)
        first[parts[n]] = f
        return modulated(f, mods(3), mods(4))

    rows = normed(0)
    for n, part in enumerate(parts):
        raw = [dot(rows, qkv_cross[:, at : at + HW]) for at in (2 * HW, 0, HW)]
        if n + 1 < len(parts):
            rows = normed(n + 1)
        kv[part, HW:] = raw[0].astype(BF16)
        query[part] = head_norm(raw[1], gains[0], ones)
        kv[part, :HW] = head_norm(raw[2], gains[1], ones)


def late_block(block, held, first, query, kv, others, their_frames, out_self, qkv_cross, gains, out_cross):
    ones = head_ones()
    part = slice(block * BLOCK, (block + 1) * BLOCK)
    keys, values = [kv[part, :HW]], [kv[part, HW:]]
    for n, (attended, source) in enumerate(zip(others, their_frames)):
        mods = mods_held(held, n + 1)
        g = first_of(source[part], attended[...], out_self, mods(2))
        _, k, v = projected_cross(g, mods, qkv_cross, gains, ones, False)
        keys.append(k)
        values.append(v)
    mixed = cross_attend(query[part], keys, values, ones)
    return finished(first[part], mixed, out_cross, mods_held(held, 0)(5))


def late_kernel(block, count, held, first, query, kv, *refs):
    others, their_frames = refs[: count - 1], refs[count - 1 : 2 * count - 2]
    *weights, out = refs[2 * count - 2 :]
    out[...] = late_block(block, held, first, query, kv, others, their_frames, *weights)


def early_kernel(count, held, inner_out, outer_out, out_cross, first, query, *refs):
    keys, values = refs[:count], refs[count : 2 * count]
    out, early_out, sems = refs[2 * count :]
    _, outer, inner, early = places(out.shape[1])
    copies = [
        pltpu.make_async_copy(source, out.at[0, pl.ds(at, BLOCK)], sems.at[n])
        for n, (source, at) in enumerate(((inner_out, inner), (outer_out, outer), (early_out, early)))
    ]
    copies[0].start()
    copies[1].start()
    mixed = cross_attend(
        query[...], [k[...] for k in keys], [v[...] for v in values], head_ones()
    )
    early_out[...] = finished(first[...], mixed, out_cross, mods_held(held, 0)(5))
    copies[2].start()
    for copy in copies:
        copy.wait()


def on_device(
    frames,
    timestep,
    modulation,
    qkv_self,
    out_self,
    qk_gain_self,
    qkv_cross,
    out_cross,
    qk_gain_cross,
):
    stems = lax.axis_size("stem")
    count = lax.axis_size("tm")
    rows = frames.shape[1]
    assert count % 2 == 0 and rows == HALF + BLOCK
    modulation = jnp.transpose(modulation, (1, 0, 2))
    inside = [(i, i ^ 1) for i in range(count)]
    across = [(i, i + 2) for i in range(0, count - 2, 2)]
    across += [(i + 3, i + 1) for i in range(0, count - 2, 2)]
    across += [(count - 2, count - 1), (1, 0)]

    def to_stems(array):
        return [
            lax.ppermute(array, "stem", [(i, (i + k) % stems) for i in range(stems)])
            for k in range(1, stems)
        ]

    def call(kernel, name, us, outs, *args, scratch=(), in_specs=None, out_specs=None):
        out_specs = out_specs or jax.tree.map(lambda _: VMEM, outs)
        return pl.pallas_call(
            kernel,
            out_shape=outs,
            in_specs=in_specs or [VMEM] * len(args),
            out_specs=out_specs,
            scratch_shapes=list(scratch),
            compiler_params=params(),
            cost_estimate=cost(us),
            name=name,
        )(*args)

    half = shape(BLOCK, D)
    late_rows, early_rows = call(
        split_kernel, "split", 4, (shape(HALF, D), half), frames,
        scratch=[pltpu.SemaphoreType.DMA((3,))], in_specs=[ANY], out_specs=(ANY, ANY),
    )
    their_frames = to_stems(late_rows)
    near = lax.ppermute(frames, "tm", inside)
    mate_outer, mate_inner = call(mate_kernel, "mate", 0.1, (half, half), near)
    far = lax.ppermute(mate_outer, "tm", across)
    farther = lax.ppermute(mate_inner, "tm", across)

    late, block, part = shape(HALF, HW), shape(BLOCK, HW), shape(HALF, HW, dtype=F32)
    query, kv, first_early, q_early, k_early, v_early, held = call(
        near_kernel, "near", 0.12,
        (late, shape(rows + HALF, 2 * HW), half, block, block, block, shape(stems, 8, D, dtype=F32)),
        timestep, modulation, early_rows, late_rows, near, qkv_self, qk_gain_self, out_self, qkv_cross, qk_gain_cross,
        in_specs=[SMEM] + [VMEM] * 9,
    )
    their_keys = to_stems(k_early)
    parts = call(part_kernel, "part", 0.04, (part, part, part), query, kv)

    self_weights = (qkv_self, qk_gain_self)
    att_inner, far_kv = call(
        lambda *refs: far_inner_kernel(rows, *refs), "far_inner", 0.04, (block, half),
        held, far, *self_weights, query, *parts,
    )
    others_inner = to_stems(att_inner)
    att_outer, passed = call(
        lambda *refs: far_outer_kernel(rows, *refs), "far_outer", 0.006, (block, block),
        v_early, held, farther, *self_weights, query, *parts, far_kv,
    )
    others_outer = to_stems(att_outer)
    their_values = to_stems(passed)

    weights = (out_self, qkv_cross, qk_gain_cross)
    own = call(
        own_kernel, "own", 0.02, (shape(HALF, D), late, shape(HALF, D)),
        held, late_rows, att_inner, att_outer, *weights, *their_keys,
        in_specs=[VMEM] * 7 + [ANY] * (stems - 1),
    )
    inner_out, outer_out = (
        call(
            lambda *refs, n=n: late_kernel(n, stems, *refs), name, us, half,
            held, *own, *others, *their_frames, *weights, out_cross,
        )
        for n, name, us, others in ((1, "inner", 0.04, others_inner), (0, "outer", 0.04, others_outer))
    )
    return call(
        lambda *refs: early_kernel(stems, *refs), "early", 2, shape(1, rows, D),
        held, inner_out, outer_out, out_cross, first_early, q_early, k_early, *their_keys, v_early, *their_values,
        scratch=[pltpu.VMEM((BLOCK, D), BF16), pltpu.SemaphoreType.DMA((3,))], out_specs=ANY,
    )


def solution(mesh):
    return jax.shard_map(
        on_device,
        mesh=mesh,
        in_specs=(P("stem", "tm", None), P(), P(), P(), P(), P(), P(), P(), P()),
        out_specs=P("stem", "tm", None),
        check_vma=False,
    )
```

```python
import jax
import jax.numpy as jnp
from jax import lax
from jax.experimental import pallas as pl
from jax.experimental.pallas import tpu as pltpu
from jax.sharding import PartitionSpec as P

D = 1024
H = 8
HD = 64
HW = H * HD
HALF = 256
BLOCK = 128
SLAB = 128
EPS = 1e-06
NEG = -1e30
F32 = jnp.float32
BF16 = jnp.bfloat16
VMEM = pl.BlockSpec(memory_space=pltpu.VMEM)
ANY = pl.BlockSpec(memory_space=pl.ANY)
LIMIT = 16 * 1024 * 1024


def cost(us):
    return pl.CostEstimate(flops=int(us * 1e9), bytes_accessed=int(us * 3e6), transcendentals=0)


def params():
    return pltpu.CompilerParams(vmem_limit_bytes=LIMIT)


def shape(*dims, dtype=BF16):
    return jax.ShapeDtypeStruct(dims, dtype)


def dot(a, b, dims=((1,), (0,))):
    return lax.dot_general(a, b, (dims, ((), ())), preferred_element_type=F32)


def modulated(rows, shift, scale):
    values = rows.astype(F32)
    centred = values - jnp.mean(values, axis=-1, keepdims=True)
    spread = jnp.mean(centred * centred, axis=-1, keepdims=True)
    normed = centred * lax.rsqrt(spread + EPS)
    return (normed * (1.0 + scale) + shift).astype(BF16)


def head_ones():
    row = lax.broadcasted_iota(jnp.int32, (2 * SLAB, 2 * SLAB), 0) // HD
    col = lax.broadcasted_iota(jnp.int32, (2 * SLAB, 2 * SLAB), 1) // HD
    return jnp.where(row == col, 1.0, 0.0).astype(BF16)


def head_sums(values, ones):
    parts = [dot(values[:, at : at + 2 * SLAB], ones) for at in range(0, HW, 2 * SLAB)]
    return jnp.concatenate(parts, axis=1)


def exact_head_sums(values, ones):
    high = values.astype(BF16)
    low = (values - high.astype(F32)).astype(BF16)
    return head_sums(high, ones) + head_sums(low, ones)


def head_norm(values, gain, ones):
    mean = head_sums((values * values).astype(BF16), ones) * (1.0 / HD)
    return (values * lax.rsqrt(mean + EPS) * gain).astype(BF16)


def wide_gain(gain):
    return jnp.concatenate([gain] * H, axis=1)


def window_bias(keys, ahead, first_frame=0, total=1 << 30):
    i = lax.broadcasted_iota(jnp.int32, (BLOCK, keys), 0)
    j = lax.broadcasted_iota(jnp.int32, (BLOCK, keys), 1)
    frame = first_frame + j
    keep = (j + ahead >= i) & (j + ahead <= i + 2 * HALF) & (frame >= 0) & (frame < total)
    return jnp.where(keep, 0.0, NEG)


def left_half():
    return lax.broadcasted_iota(jnp.int32, (BLOCK, SLAB), 1) < HD


def by_head(pair):
    return jnp.where(left_half(), pair[:BLOCK], pair[BLOCK:])


def window_scores(query, keys, bias):
    half, zero = left_half(), jnp.zeros_like(query)
    pair = jnp.concatenate([jnp.where(half, query, zero), jnp.where(half, zero, query)], axis=0)
    scores = dot(pair, keys, ((1,), (1,)))
    return jnp.concatenate([scores[:BLOCK] + bias, scores[BLOCK:] + bias], axis=0)


def raised(scores):
    top = jnp.max(scores, axis=-1, keepdims=True)
    return jnp.exp(scores - top).astype(BF16), top


def weighted(powers, values):
    summed = dot(powers, jnp.concatenate([values, jnp.ones_like(values)], axis=1))
    return by_head(summed[:, :SLAB]), by_head(summed[:, SLAB:])


SLABS = [slice(at, at + SLAB) for at in range(0, HW, SLAB)]


def cross_attend(query, keys, values, ones):
    query = query.astype(F32)
    base = keys[0].astype(F32)
    scores = [
        exact_head_sums(query * (k.astype(F32) - base), ones) * (HD ** -0.5) for k in keys[1:]
    ]
    top = jnp.zeros_like(query)
    for s in scores:
        top = jnp.maximum(top, s)
    powers = [jnp.exp(-top)] + [jnp.exp(s - top) for s in scores]
    total = powers[0]
    for p in powers[1:]:
        total = total + p
    scale = 1.0 / total
    out = jnp.zeros_like(query)
    for p, v in zip(powers, values):
        out = out + (p * scale).astype(BF16).astype(F32) * v.astype(F32)
    return out.astype(BF16)


def mods_of(timestep, modulation, back):
    count = lax.axis_size("stem")
    stem = lax.rem(lax.axis_index("stem") + count - back, count)
    at = lax.broadcasted_iota(jnp.int32, (1, count), 1)
    step = jnp.sum(jnp.where(at == stem, timestep[...], 0).astype(F32), axis=1, keepdims=True)
    rows = lax.broadcasted_iota(jnp.int32, (modulation.shape[1], 1), 0).astype(F32)
    picked = rows == step
    return [
        jnp.sum(jnp.where(picked, modulation[i], 0.0), axis=0, keepdims=True) for i in range(6)
    ]


def mods_held(held, back):
    return lambda i: held[back, i : i + 1]


def places(rows):
    parity = lax.rem(lax.axis_index("tm"), 2)
    outer = pl.multiple_of(parity * HALF, BLOCK)
    early = pl.multiple_of((1 - parity) * HALF, BLOCK)
    return parity, outer, rows - HALF, early


def split_kernel(frames, late_rows, early_rows, sems):
    _, outer, inner, early = places(frames.shape[1])
    targets = (late_rows.at[pl.ds(0, BLOCK)], late_rows.at[pl.ds(BLOCK, BLOCK)], early_rows)
    copies = [
        pltpu.make_async_copy(frames.at[0, pl.ds(at, BLOCK)], to, sems.at[n])
        for n, (at, to) in enumerate(zip((outer, inner, early), targets))
    ]
    for copy in copies:
        copy.start()
    for copy in copies:
        copy.wait()


def mate_kernel(mate, outer_rows, inner_rows):
    _, _, inner, outer = places(mate.shape[1])
    outer_rows[...] = mate[0, pl.ds(outer, BLOCK)]
    inner_rows[...] = mate[0, inner : inner + BLOCK]


def part_steps(block, query, kv, part_out, part_sum, part_top):
    parity = lax.rem(lax.axis_index("tm"), 2)
    width = (HALF, BLOCK)[block]
    start = pl.multiple_of(parity * width, BLOCK)
    count = kv.shape[0] - width
    bias = window_bias(count, (1 - parity) * width)
    to = slice(block * BLOCK, (block + 1) * BLOCK)
    for cols in SLABS:
        scores = window_scores(query[:, cols], kv[pl.ds(start, count), cols], bias)
        yield
        powers, top = raised(scores)
        values = kv[pl.ds(start, count), HW + cols.start : HW + cols.stop]
        part_out[to, cols], part_sum[to, cols] = weighted(powers, values)
        part_top[to, cols] = by_head(jnp.broadcast_to(top, (2 * BLOCK, SLAB)))
        yield


def near_kernel(
    timestep, modulation, early_rows, late_rows, near, qkv_self, gains, out_self, qkv_cross, gains_cross,
    query, part_out, part_sum, part_top, first, first_q, first_k, first_v, held, kv,
):
    rows = near.shape[1]

    def hold(k):
        for i, row in enumerate(mods_of(timestep, modulation, k)):
            held[k, i : i + 1] = row

    hold(0)
    parity, outer, inner, early = places(rows)
    mods = mods_held(held, 0)
    shift, scale = mods(0), mods(1)
    ones = head_ones()
    q_gain = wide_gain(gains[0:1]) * (HD ** -0.5)
    k_gain = wide_gain(gains[1:2])
    own_at = parity * HALF
    near_at = (1 - parity) * rows
    near_from = parity * (rows - HALF)

    sources = [
        (early_rows, 0, own_at + early),
        (late_rows, 0, own_at + outer),
        (late_rows, BLOCK, own_at + inner),
    ]
    for at in range(0, HALF, BLOCK):
        sources.append((near.at[0], pl.multiple_of(near_from + at, BLOCK), near_at + at))

    def normed(n):
        source, at, _ = sources[n]
        return modulated(source[pl.ds(at, BLOCK)], shift, scale)

    queries = []
    rows_n = normed(0)
    for n, (_, _, to) in enumerate(sources):
        at = pl.ds(pl.multiple_of(to, BLOCK), BLOCK)
        columns = (0, HW, 2 * HW) if n < 3 else (HW, 2 * HW)
        raw = [dot(rows_n, qkv_self[:, c : c + HW]) for c in columns]
        if n + 1 < len(sources):
            rows_n = normed(n + 1)
        if n < 3:
            queries.append(head_norm(raw[0], q_gain, ones))
        kv[at, :HW] = head_norm(raw[-2], k_gain, ones)
        kv[at, HW:] = raw[-1].astype(BF16)
    query[:BLOCK] = queries[1]
    query[BLOCK:] = queries[2]
    for k in range(1, held.shape[0]):
        hold(k)

    parts = [part_steps(n, queries[n + 1], kv, part_out, part_sum, part_top) for n in range(2)]

    def meanwhile(steps):
        while steps and parts:
            if next(parts[0], parts) is parts:
                parts.pop(0)
            else:
                steps -= 1

    bias = window_bias(rows + HALF, 0)
    attended = []
    for cols in SLABS:
        scores = window_scores(queries[0][:, cols], kv[:, cols], bias)
        meanwhile(2)
        powers, _ = raised(scores)
        out, total = weighted(powers, kv[:, HW + cols.start : HW + cols.stop])
        attended.append((out / total).astype(BF16))
    f = first_of(early_rows[...], jnp.concatenate(attended, axis=1), out_self, mods(2))
    first[...] = f
    meanwhile(3)
    normed_f = modulated(f, mods(3), mods(4))
    meanwhile(3)
    raw = [dot(normed_f, qkv_cross[:, at : at + HW]) for at in range(0, 3 * HW, HW)]
    meanwhile(4)
    first_q[...] = head_norm(raw[0], wide_gain(gains_cross[0:1]), ones)
    first_k[...] = head_norm(raw[1], wide_gain(gains_cross[1:2]), ones)
    first_v[...] = raw[2].astype(BF16)
    meanwhile(4 * HW)


def far_keys(rows, held, qkv_self, gains):
    mods = mods_held(held, 0)
    normed = modulated(rows, mods(0), mods(1))
    keys = dot(normed, qkv_self[:, HW : 2 * HW])
    values = dot(normed, qkv_self[:, 2 * HW :]).astype(BF16)
    return head_norm(keys, wide_gain(gains[1:2]), head_ones()), values


def far_bias(rows, block_start, outermost):
    place = lax.axis_index("tm")
    below = -2 * BLOCK if outermost else -BLOCK
    start = jnp.where(lax.rem(place, 2) == 0, below, rows + (BLOCK if outermost else 0))
    total = rows * lax.axis_size("tm")
    return window_bias(BLOCK, start - block_start + HALF, place * rows + start, total)


def far_attend(block, bias, query, keys, values, part_out, part_sum, part_top, attended):
    to = slice(block * BLOCK, (block + 1) * BLOCK)
    scores = [window_scores(query[to, cols], keys[:, cols], bias) for cols in SLABS]
    powers = [raised(each) for each in scores]
    sums = [weighted(each, values[:, cols]) for (each, _), cols in zip(powers, SLABS)]
    for cols, (_, top), (out, summed) in zip(SLABS, powers, sums):
        top = by_head(jnp.broadcast_to(top, (2 * BLOCK, SLAB)))
        both = jnp.maximum(top, part_top[to, cols])
        here = jnp.exp(top - both)
        before = jnp.exp(part_top[to, cols] - both)
        out = out * here + part_out[to, cols] * before
        summed = summed * here + part_sum[to, cols] * before
        attended[:, cols] = (out / summed).astype(BF16)


def far_inner_kernel(rows, held, far, qkv_self, gains, query, *refs):
    *parts, attended, kv = refs
    keys, values = far_keys(far[...], held, qkv_self, gains)
    far_attend(1, far_bias(rows, rows - HALF, False), query, keys, values, *parts, attended)
    kv[:, :HW], kv[:, HW:] = keys, values


def far_outer_kernel(rows, early_values, held, far, qkv_self, gains, query, *refs):
    *parts, kv, attended, passed = refs
    passed[...] = early_values[...]
    keys, values = far_keys(far[...], held, qkv_self, gains)
    keys = jnp.concatenate([kv[:, :HW], keys], axis=0)
    values = jnp.concatenate([kv[:, HW:], values], axis=0)
    start = lax.rem(lax.axis_index("tm"), 2) * HALF
    bias = [far_bias(rows, start, outermost) for outermost in (False, True)]
    far_attend(0, jnp.concatenate(bias, axis=1), query, keys, values, *parts, attended)


def first_of(frames, attended, weight, gate):
    mixed = dot(attended, weight[...])
    return (frames.astype(F32) + gate * mixed).astype(BF16)


def projected_cross(first, mods, weight, gains, ones, with_query):
    normed = modulated(first, mods(3), mods(4))
    raw = [dot(normed, weight[:, at : at + HW]) for at in range(0 if with_query else HW, 3 * HW, HW)]
    query = head_norm(raw[0], wide_gain(gains[0:1]), ones) if with_query else None
    keys = head_norm(raw[-2], wide_gain(gains[1:2]), ones)
    return query, keys, raw[-1].astype(BF16)


def finished(first, attended, weight, gate):
    out = dot(attended, weight[...]).astype(BF16)
    return (first.astype(F32) + gate * out.astype(F32)).astype(BF16)


def own_kernel(held, frames, inner, outer, out_self, qkv_cross, gains, *refs):
    first, query, kv = refs[-3:]
    mods = mods_held(held, 0)
    ones = head_ones()
    parts = [slice(0, BLOCK), slice(BLOCK, HALF)]
    mixed = [dot(attended[...], out_self[...]) for attended in (outer, inner)]
    gains = [wide_gain(gains[i : i + 1]) for i in range(2)]

    def normed(n):
        f = (frames[parts[n]].astype(F32) + mods(2) * mixed[n]).astype(BF16)
        first[parts[n]] = f
        return modulated(f, mods(3), mods(4))

    rows = normed(0)
    for n, part in enumerate(parts):
        raw = [dot(rows, qkv_cross[:, at : at + HW]) for at in (2 * HW, 0, HW)]
        if n + 1 < len(parts):
            rows = normed(n + 1)
        kv[part, HW:] = raw[0].astype(BF16)
        query[part] = head_norm(raw[1], gains[0], ones)
        kv[part, :HW] = head_norm(raw[2], gains[1], ones)


def late_block(block, held, first, query, kv, others, their_frames, out_self, qkv_cross, gains, out_cross):
    ones = head_ones()
    part = slice(block * BLOCK, (block + 1) * BLOCK)
    keys, values = [kv[part, :HW]], [kv[part, HW:]]
    for n, (attended, source) in enumerate(zip(others, their_frames)):
        mods = mods_held(held, n + 1)
        g = first_of(source[part], attended[...], out_self, mods(2))
        _, k, v = projected_cross(g, mods, qkv_cross, gains, ones, False)
        keys.append(k)
        values.append(v)
    mixed = cross_attend(query[part], keys, values, ones)
    return finished(first[part], mixed, out_cross, mods_held(held, 0)(5))


def late_kernel(block, count, held, first, query, kv, *refs):
    others, their_frames = refs[: count - 1], refs[count - 1 : 2 * count - 2]
    *weights, out = refs[2 * count - 2 :]
    out[...] = late_block(block, held, first, query, kv, others, their_frames, *weights)


def early_kernel(count, held, inner_out, outer_out, out_cross, first, query, *refs):
    keys, values = refs[:count], refs[count : 2 * count]
    out, early_out, sems = refs[2 * count :]
    _, outer, inner, early = places(out.shape[1])
    copies = [
        pltpu.make_async_copy(source, out.at[0, pl.ds(at, BLOCK)], sems.at[n])
        for n, (source, at) in enumerate(((inner_out, inner), (outer_out, outer), (early_out, early)))
    ]
    copies[0].start()
    copies[1].start()
    mixed = cross_attend(
        query[...], [k[...] for k in keys], [v[...] for v in values], head_ones()
    )
    early_out[...] = finished(first[...], mixed, out_cross, mods_held(held, 0)(5))
    copies[2].start()
    for copy in copies:
        copy.wait()


def on_device(
    frames,
    timestep,
    modulation,
    qkv_self,
    out_self,
    qk_gain_self,
    qkv_cross,
    out_cross,
    qk_gain_cross,
):
    stems = lax.axis_size("stem")
    count = lax.axis_size("tm")
    rows = frames.shape[1]
    assert count % 2 == 0 and rows == HALF + BLOCK
    modulation = jnp.transpose(modulation, (1, 0, 2))
    inside = [(i, i ^ 1) for i in range(count)]
    across = [(i, i + 2) for i in range(0, count - 2, 2)]
    across += [(i + 3, i + 1) for i in range(0, count - 2, 2)]
    across += [(count - 2, count - 1), (1, 0)]

    def to_stems(array):
        return [
            lax.ppermute(array, "stem", [(i, (i + k) % stems) for i in range(stems)])
            for k in range(1, stems)
        ]

    def call(kernel, name, us, outs, *args, scratch=(), in_specs=None, out_specs=None):
        out_specs = out_specs or jax.tree.map(lambda _: VMEM, outs)
        return pl.pallas_call(
            kernel,
            out_shape=outs,
            in_specs=in_specs or [VMEM] * len(args),
            out_specs=out_specs,
            scratch_shapes=list(scratch),
            compiler_params=params(),
            cost_estimate=cost(us),
            name=name,
        )(*args)

    half = shape(BLOCK, D)
    late_rows, early_rows = call(
        split_kernel, "split", 4, (shape(HALF, D), half), frames,
        scratch=[pltpu.SemaphoreType.DMA((3,))], in_specs=[ANY], out_specs=(ANY, ANY),
    )
    their_frames = to_stems(late_rows)
    near = lax.ppermute(frames, "tm", inside)
    mate_outer, mate_inner = call(mate_kernel, "mate", 0.1, (half, half), near)
    far = lax.ppermute(mate_outer, "tm", across)
    farther = lax.ppermute(mate_inner, "tm", across)

    late, block, part = shape(HALF, HW), shape(BLOCK, HW), shape(HALF, HW, dtype=F32)
    query, part_out, part_sum, part_top, first_early, q_early, k_early, v_early, held = call(
        near_kernel, "near", 0.12,
        (late, part, part, part, half, block, block, block, shape(stems, 8, D, dtype=F32)),
        timestep.reshape(1, -1), modulation, early_rows, late_rows, near, qkv_self, qk_gain_self, out_self, qkv_cross, qk_gain_cross,
        scratch=[pltpu.VMEM((rows + HALF, 2 * HW), BF16)],
    )
    their_keys = to_stems(k_early)
    parts = (part_out, part_sum, part_top)

    self_weights = (qkv_self, qk_gain_self)
    att_inner, far_kv = call(
        lambda *refs: far_inner_kernel(rows, *refs), "far_inner", 0.04, (block, half),
        held, far, *self_weights, query, *parts,
    )
    others_inner = to_stems(att_inner)
    att_outer, passed = call(
        lambda *refs: far_outer_kernel(rows, *refs), "far_outer", 0.006, (block, block),
        v_early, held, farther, *self_weights, query, *parts, far_kv,
    )
    others_outer = to_stems(att_outer)
    their_values = to_stems(passed)

    weights = (out_self, qkv_cross, qk_gain_cross)
    own = call(
        own_kernel, "own", 0.02, (shape(HALF, D), late, shape(HALF, D)),
        held, late_rows, att_inner, att_outer, *weights, *their_keys,
        in_specs=[VMEM] * 7 + [ANY] * (stems - 1),
    )
    inner_out = call(
        lambda *refs: late_kernel(1, stems, *refs), "inner", 0.04, half,
        held, *own, *others_inner, *their_frames, *weights, out_cross,
    )
    outer_out = call(
        lambda _, *refs: late_kernel(0, stems, *refs), "outer", 0.04, half,
        inner_out, held, *own, *others_outer, *their_frames, *weights, out_cross,
        in_specs=[ANY] + [VMEM] * (6 + 2 * stems),
    )
    return call(
        lambda *refs: early_kernel(stems, *refs), "early", 2, shape(1, rows, D),
        held, inner_out, outer_out, out_cross, first_early, q_early, k_early, *their_keys, v_early, *their_values,
        scratch=[pltpu.VMEM((BLOCK, D), BF16), pltpu.SemaphoreType.DMA((3,))], out_specs=ANY,
    )


def solution(mesh):
    return jax.shard_map(
        on_device,
        mesh=mesh,
        in_specs=(P("stem", "tm", None), P(), P(), P(), P(), P(), P(), P(), P()),
        out_specs=P("stem", "tm", None),
        check_vma=False,
    )
```

```python
import jax
import jax.numpy as jnp
from jax import lax
from jax.experimental import pallas as pl
from jax.experimental.pallas import tpu as pltpu
from jax.sharding import PartitionSpec as P

D = 1024
H = 8
HD = 64
HW = H * HD
HALF = 256
BLOCK = 128
SLAB = 128
EPS = 1e-06
NEG = -1e30
F32 = jnp.float32
BF16 = jnp.bfloat16
VMEM = pl.BlockSpec(memory_space=pltpu.VMEM)
ANY = pl.BlockSpec(memory_space=pl.ANY)
LIMIT = 16 * 1024 * 1024


def cost(us):
    return pl.CostEstimate(flops=int(us * 1e9), bytes_accessed=int(us * 3e6), transcendentals=0)


def params():
    return pltpu.CompilerParams(vmem_limit_bytes=LIMIT)


def shape(*dims, dtype=BF16):
    return jax.ShapeDtypeStruct(dims, dtype)


def dot(a, b, dims=((1,), (0,))):
    return lax.dot_general(a, b, (dims, ((), ())), preferred_element_type=F32)


def modulated(rows, shift, scale):
    values = rows.astype(F32)
    centred = values - jnp.mean(values, axis=-1, keepdims=True)
    spread = jnp.mean(centred * centred, axis=-1, keepdims=True)
    normed = centred * lax.rsqrt(spread + EPS)
    return (normed * (1.0 + scale) + shift).astype(BF16)


def head_ones():
    row = lax.broadcasted_iota(jnp.int32, (2 * SLAB, 2 * SLAB), 0) // HD
    col = lax.broadcasted_iota(jnp.int32, (2 * SLAB, 2 * SLAB), 1) // HD
    return jnp.where(row == col, 1.0, 0.0).astype(BF16)


def head_sums(values, ones):
    parts = [dot(values[:, at : at + 2 * SLAB], ones) for at in range(0, HW, 2 * SLAB)]
    return jnp.concatenate(parts, axis=1)


def exact_head_sums(values, ones):
    high = values.astype(BF16)
    low = (values - high.astype(F32)).astype(BF16)
    return head_sums(high, ones) + head_sums(low, ones)


def head_norm(values, gain, ones):
    mean = head_sums((values * values).astype(BF16), ones) * (1.0 / HD)
    return (values * lax.rsqrt(mean + EPS) * gain).astype(BF16)


def wide_gain(gain):
    return jnp.concatenate([gain] * H, axis=1)


def window_bias(keys, ahead, first_frame=0, total=1 << 30):
    i = lax.broadcasted_iota(jnp.int32, (BLOCK, keys), 0)
    j = lax.broadcasted_iota(jnp.int32, (BLOCK, keys), 1)
    frame = first_frame + j
    keep = (j + ahead >= i) & (j + ahead <= i + 2 * HALF) & (frame >= 0) & (frame < total)
    return jnp.where(keep, 0.0, NEG)


def left_half():
    return lax.broadcasted_iota(jnp.int32, (BLOCK, SLAB), 1) < HD


def by_head(pair):
    return jnp.where(left_half(), pair[:BLOCK], pair[BLOCK:])


def window_scores(query, keys, bias):
    half, zero = left_half(), jnp.zeros_like(query)
    pair = jnp.concatenate([jnp.where(half, query, zero), jnp.where(half, zero, query)], axis=0)
    scores = dot(pair, keys, ((1,), (1,)))
    return jnp.concatenate([scores[:BLOCK] + bias, scores[BLOCK:] + bias], axis=0)


def raised(scores):
    top = jnp.max(scores, axis=-1, keepdims=True)
    return jnp.exp(scores - top).astype(BF16), top


def weighted(powers, values):
    summed = dot(powers, jnp.concatenate([values, jnp.ones_like(values)], axis=1))
    return by_head(summed[:, :SLAB]), by_head(summed[:, SLAB:])


SLABS = [slice(at, at + SLAB) for at in range(0, HW, SLAB)]


def cross_weights(query, keys, ones):
    query = query.astype(F32)
    base = keys[0].astype(F32)
    scores = [
        exact_head_sums(query * (k.astype(F32) - base), ones) * (HD ** -0.5) for k in keys[1:]
    ]
    top = jnp.zeros_like(query)
    for s in scores:
        top = jnp.maximum(top, s)
    powers = [jnp.exp(-top)] + [jnp.exp(s - top) for s in scores]
    total = powers[0]
    for p in powers[1:]:
        total = total + p
    scale = 1.0 / total
    return [(p * scale).astype(BF16) for p in powers]


def cross_sum(weights, values):
    out = jnp.zeros(values[0].shape, F32)
    for w, v in zip(weights, values):
        out = out + w.astype(F32) * v.astype(F32)
    return out.astype(BF16)


def mods_of(timestep, modulation, back):
    count = lax.axis_size("stem")
    stem = lax.rem(lax.axis_index("stem") + count - back, count)
    at = lax.broadcasted_iota(jnp.int32, (1, count), 1)
    step = jnp.sum(jnp.where(at == stem, timestep[...], 0).astype(F32), axis=1, keepdims=True)
    rows = lax.broadcasted_iota(jnp.int32, (modulation.shape[1], 1), 0).astype(F32)
    picked = rows == step
    return [
        jnp.sum(jnp.where(picked, modulation[i], 0.0), axis=0, keepdims=True) for i in range(6)
    ]


def mods_held(held, back):
    return lambda i: held[back, i : i + 1]


def places(rows):
    parity = lax.rem(lax.axis_index("tm"), 2)
    outer = pl.multiple_of(parity * HALF, BLOCK)
    early = pl.multiple_of((1 - parity) * HALF, BLOCK)
    return parity, outer, rows - HALF, early


def split_kernel(frames, late_rows, early_rows, sems):
    _, outer, inner, early = places(frames.shape[1])
    targets = (late_rows.at[pl.ds(0, BLOCK)], late_rows.at[pl.ds(BLOCK, BLOCK)], early_rows)
    copies = [
        pltpu.make_async_copy(frames.at[0, pl.ds(at, BLOCK)], to, sems.at[n])
        for n, (at, to) in enumerate(zip((outer, inner, early), targets))
    ]
    for copy in copies:
        copy.start()
    for copy in copies:
        copy.wait()


def mate_kernel(mate, outer_rows, inner_rows):
    _, _, inner, outer = places(mate.shape[1])
    outer_rows[...] = mate[0, pl.ds(outer, BLOCK)]
    inner_rows[...] = mate[0, inner : inner + BLOCK]


def part_steps(block, query, kv, part_out, part_sum, part_top):
    parity = lax.rem(lax.axis_index("tm"), 2)
    width = (HALF, BLOCK)[block]
    start = pl.multiple_of(parity * width, BLOCK)
    count = kv.shape[0] - width
    bias = window_bias(count, (1 - parity) * width)
    to = slice(block * BLOCK, (block + 1) * BLOCK)
    for cols in SLABS:
        scores = window_scores(query[:, cols], kv[pl.ds(start, count), cols], bias)
        yield
        powers, top = raised(scores)
        values = kv[pl.ds(start, count), HW + cols.start : HW + cols.stop]
        part_out[to, cols], part_sum[to, cols] = weighted(powers, values)
        part_top[to, cols] = by_head(jnp.broadcast_to(top, (2 * BLOCK, SLAB)))
        yield


def near_kernel(
    timestep, modulation, early_rows, late_rows, near, qkv_self, gains, out_self, qkv_cross, gains_cross,
    query, part_out, part_sum, part_top, first, first_q, first_k, first_v, held, kv,
):
    rows = near.shape[1]

    def hold(k):
        for i, row in enumerate(mods_of(timestep, modulation, k)):
            held[k, i : i + 1] = row

    hold(0)
    parity, outer, inner, early = places(rows)
    mods = mods_held(held, 0)
    shift, scale = mods(0), mods(1)
    ones = head_ones()
    q_gain = wide_gain(gains[0:1]) * (HD ** -0.5)
    k_gain = wide_gain(gains[1:2])
    own_at = parity * HALF
    near_at = (1 - parity) * rows
    near_from = parity * (rows - HALF)

    sources = [
        (early_rows, 0, own_at + early),
        (late_rows, 0, own_at + outer),
        (late_rows, BLOCK, own_at + inner),
    ]
    for at in range(0, HALF, BLOCK):
        sources.append((near.at[0], pl.multiple_of(near_from + at, BLOCK), near_at + at))

    def normed(n):
        source, at, _ = sources[n]
        return modulated(source[pl.ds(at, BLOCK)], shift, scale)

    queries = []
    rows_n = normed(0)
    for n, (_, _, to) in enumerate(sources):
        at = pl.ds(pl.multiple_of(to, BLOCK), BLOCK)
        columns = (0, HW, 2 * HW) if n < 3 else (HW, 2 * HW)
        raw = [dot(rows_n, qkv_self[:, c : c + HW]) for c in columns]
        if n + 1 < len(sources):
            rows_n = normed(n + 1)
        if n < 3:
            queries.append(head_norm(raw[0], q_gain, ones))
        kv[at, :HW] = head_norm(raw[-2], k_gain, ones)
        kv[at, HW:] = raw[-1].astype(BF16)
    query[:BLOCK] = queries[1]
    query[BLOCK:] = queries[2]
    for k in range(1, held.shape[0]):
        hold(k)

    parts = [part_steps(n, queries[n + 1], kv, part_out, part_sum, part_top) for n in range(2)]

    def meanwhile(steps):
        while steps and parts:
            if next(parts[0], parts) is parts:
                parts.pop(0)
            else:
                steps -= 1

    bias = window_bias(rows + HALF, 0)
    attended = []
    for cols in SLABS:
        scores = window_scores(queries[0][:, cols], kv[:, cols], bias)
        meanwhile(2)
        powers, _ = raised(scores)
        out, total = weighted(powers, kv[:, HW + cols.start : HW + cols.stop])
        attended.append((out / total).astype(BF16))
    f = first_of(early_rows[...], jnp.concatenate(attended, axis=1), out_self, mods(2))
    first[...] = f
    meanwhile(3)
    normed_f = modulated(f, mods(3), mods(4))
    meanwhile(3)
    raw = [dot(normed_f, qkv_cross[:, at : at + HW]) for at in range(0, 3 * HW, HW)]
    meanwhile(4)
    first_q[...] = head_norm(raw[0], wide_gain(gains_cross[0:1]), ones)
    first_k[...] = head_norm(raw[1], wide_gain(gains_cross[1:2]), ones)
    first_v[...] = raw[2].astype(BF16)
    meanwhile(4 * HW)


def far_keys(rows, held, qkv_self, gains):
    mods = mods_held(held, 0)
    normed = modulated(rows, mods(0), mods(1))
    keys = dot(normed, qkv_self[:, HW : 2 * HW])
    values = dot(normed, qkv_self[:, 2 * HW :]).astype(BF16)
    return head_norm(keys, wide_gain(gains[1:2]), head_ones()), values


def far_bias(rows, block_start, outermost):
    place = lax.axis_index("tm")
    below = -2 * BLOCK if outermost else -BLOCK
    start = jnp.where(lax.rem(place, 2) == 0, below, rows + (BLOCK if outermost else 0))
    total = rows * lax.axis_size("tm")
    return window_bias(BLOCK, start - block_start + HALF, place * rows + start, total)


def far_attend(block, bias, query, keys, values, part_out, part_sum, part_top, attended):
    to = slice(block * BLOCK, (block + 1) * BLOCK)
    scores = [window_scores(query[to, cols], keys[:, cols], bias) for cols in SLABS]
    powers = [raised(each) for each in scores]
    sums = [weighted(each, values[:, cols]) for (each, _), cols in zip(powers, SLABS)]
    for cols, (_, top), (out, summed) in zip(SLABS, powers, sums):
        top = by_head(jnp.broadcast_to(top, (2 * BLOCK, SLAB)))
        both = jnp.maximum(top, part_top[to, cols])
        here = jnp.exp(top - both)
        before = jnp.exp(part_top[to, cols] - both)
        out = out * here + part_out[to, cols] * before
        summed = summed * here + part_sum[to, cols] * before
        attended[:, cols] = (out / summed).astype(BF16)


def far_inner_kernel(rows, held, far, qkv_self, gains, query, *refs):
    *parts, attended, kv = refs
    keys, values = far_keys(far[...], held, qkv_self, gains)
    far_attend(1, far_bias(rows, rows - HALF, False), query, keys, values, *parts, attended)
    kv[:, :HW], kv[:, HW:] = keys, values


def far_outer_kernel(rows, early_values, held, far, qkv_self, gains, query, *refs):
    *parts, kv, attended, passed = refs
    passed[...] = early_values[...]
    keys, values = far_keys(far[...], held, qkv_self, gains)
    keys = jnp.concatenate([kv[:, :HW], keys], axis=0)
    values = jnp.concatenate([kv[:, HW:], values], axis=0)
    start = lax.rem(lax.axis_index("tm"), 2) * HALF
    bias = [far_bias(rows, start, outermost) for outermost in (False, True)]
    far_attend(0, jnp.concatenate(bias, axis=1), query, keys, values, *parts, attended)


def first_of(frames, attended, weight, gate):
    mixed = dot(attended, weight[...])
    return (frames.astype(F32) + gate * mixed).astype(BF16)


def projected_cross(first, mods, weight, gains, ones, with_query):
    normed = modulated(first, mods(3), mods(4))
    raw = [dot(normed, weight[:, at : at + HW]) for at in range(0 if with_query else HW, 3 * HW, HW)]
    query = head_norm(raw[0], wide_gain(gains[0:1]), ones) if with_query else None
    keys = head_norm(raw[-2], wide_gain(gains[1:2]), ones)
    return query, keys, raw[-1].astype(BF16)


def finished(first, attended, weight, gate):
    out = dot(attended, weight[...]).astype(BF16)
    return (first.astype(F32) + gate * out.astype(F32)).astype(BF16)


def own_kernel(held, frames, inner, outer, out_self, qkv_cross, gains, *refs):
    first, query, kv = refs[-3:]
    mods = mods_held(held, 0)
    ones = head_ones()
    parts = [slice(0, BLOCK), slice(BLOCK, HALF)]
    mixed = [dot(attended[...], out_self[...]) for attended in (outer, inner)]
    gains = [wide_gain(gains[i : i + 1]) for i in range(2)]

    def normed(n):
        f = (frames[parts[n]].astype(F32) + mods(2) * mixed[n]).astype(BF16)
        first[parts[n]] = f
        return modulated(f, mods(3), mods(4))

    rows = normed(0)
    for n, part in enumerate(parts):
        raw = [dot(rows, qkv_cross[:, at : at + HW]) for at in (2 * HW, 0, HW)]
        if n + 1 < len(parts):
            rows = normed(n + 1)
        kv[part, HW:] = raw[0].astype(BF16)
        query[part] = head_norm(raw[1], gains[0], ones)
        kv[part, :HW] = head_norm(raw[2], gains[1], ones)


def late_block(block, held, first, query, kv, others, their_frames, out_self, qkv_cross, gains, out_cross):
    ones = head_ones()
    part = slice(block * BLOCK, (block + 1) * BLOCK)
    keys, values = [kv[part, :HW]], [kv[part, HW:]]
    for n, (attended, source) in enumerate(zip(others, their_frames)):
        mods = mods_held(held, n + 1)
        g = first_of(source[part], attended[...], out_self, mods(2))
        _, k, v = projected_cross(g, mods, qkv_cross, gains, ones, False)
        keys.append(k)
        values.append(v)
    mixed = cross_sum(cross_weights(query[part], keys, ones), values)
    return finished(first[part], mixed, out_cross, mods_held(held, 0)(5))


def late_kernel(block, count, held, first, query, kv, *refs):
    others, their_frames = refs[: count - 1], refs[count - 1 : 2 * count - 2]
    *weights, out = refs[2 * count - 2 :]
    out[...] = late_block(block, held, first, query, kv, others, their_frames, *weights)


def weights_kernel(_, query, *refs):
    keys, out = refs[:-1], refs[-1]
    for n, each in enumerate(cross_weights(query[...], [k[...] for k in keys], head_ones())):
        out[n] = each


def early_kernel(count, held, inner_out, outer_out, out_cross, first, weights, *refs):
    values = refs[:count]
    out, early_out, sems = refs[count:]
    _, outer, inner, early = places(out.shape[1])
    copies = [
        pltpu.make_async_copy(source, out.at[0, pl.ds(at, BLOCK)], sems.at[n])
        for n, (source, at) in enumerate(((inner_out, inner), (outer_out, outer), (early_out, early)))
    ]
    copies[0].start()
    copies[1].start()
    mixed = cross_sum([weights[n] for n in range(count)], [v[...] for v in values])
    early_out[...] = finished(first[...], mixed, out_cross, mods_held(held, 0)(5))
    copies[2].start()
    for copy in copies:
        copy.wait()


def on_device(
    frames,
    timestep,
    modulation,
    qkv_self,
    out_self,
    qk_gain_self,
    qkv_cross,
    out_cross,
    qk_gain_cross,
):
    stems = lax.axis_size("stem")
    count = lax.axis_size("tm")
    rows = frames.shape[1]
    assert count % 2 == 0 and rows == HALF + BLOCK
    modulation = jnp.transpose(modulation, (1, 0, 2))
    inside = [(i, i ^ 1) for i in range(count)]
    across = [(i, i + 2) for i in range(0, count - 2, 2)]
    across += [(i + 3, i + 1) for i in range(0, count - 2, 2)]
    across += [(count - 2, count - 1), (1, 0)]

    def to_stems(array):
        return [
            lax.ppermute(array, "stem", [(i, (i + k) % stems) for i in range(stems)])
            for k in range(1, stems)
        ]

    def call(kernel, name, us, outs, *args, scratch=(), in_specs=None, out_specs=None):
        out_specs = out_specs or jax.tree.map(lambda _: VMEM, outs)
        return pl.pallas_call(
            kernel,
            out_shape=outs,
            in_specs=in_specs or [VMEM] * len(args),
            out_specs=out_specs,
            scratch_shapes=list(scratch),
            compiler_params=params(),
            cost_estimate=cost(us),
            name=name,
        )(*args)

    half = shape(BLOCK, D)
    late_rows, early_rows = call(
        split_kernel, "split", 4, (shape(HALF, D), half), frames,
        scratch=[pltpu.SemaphoreType.DMA((3,))], in_specs=[ANY], out_specs=(ANY, ANY),
    )
    their_frames = to_stems(late_rows)
    near = lax.ppermute(frames, "tm", inside)
    mate_outer, mate_inner = call(mate_kernel, "mate", 0.1, (half, half), near)
    far = lax.ppermute(mate_outer, "tm", across)
    farther = lax.ppermute(mate_inner, "tm", across)

    late, block, part = shape(HALF, HW), shape(BLOCK, HW), shape(HALF, HW, dtype=F32)
    query, part_out, part_sum, part_top, first_early, q_early, k_early, v_early, held = call(
        near_kernel, "near", 0.12,
        (late, part, part, part, half, block, block, block, shape(stems, 8, D, dtype=F32)),
        timestep.reshape(1, -1), modulation, early_rows, late_rows, near, qkv_self, qk_gain_self, out_self, qkv_cross, qk_gain_cross,
        scratch=[pltpu.VMEM((rows + HALF, 2 * HW), BF16)],
    )
    their_keys = to_stems(k_early)
    parts = (part_out, part_sum, part_top)

    self_weights = (qkv_self, qk_gain_self)
    att_inner, far_kv = call(
        lambda *refs: far_inner_kernel(rows, *refs), "far_inner", 0.04, (block, half),
        held, far, *self_weights, query, *parts,
    )
    others_inner = to_stems(att_inner)
    att_outer, passed = call(
        lambda *refs: far_outer_kernel(rows, *refs), "far_outer", 0.006, (block, block),
        v_early, held, farther, *self_weights, query, *parts, far_kv,
    )
    others_outer = to_stems(att_outer)
    their_values = to_stems(passed)

    weights = (out_self, qkv_cross, qk_gain_cross)
    own = call(
        own_kernel, "own", 0.02, (shape(HALF, D), late, shape(HALF, D)),
        held, late_rows, att_inner, att_outer, *weights, *their_keys,
        in_specs=[VMEM] * 7 + [ANY] * (stems - 1),
    )
    inner_out = call(
        lambda *refs: late_kernel(1, stems, *refs), "inner", 0.04, half,
        held, *own, *others_inner, *their_frames, *weights, out_cross,
    )
    early_weights = call(
        weights_kernel, "weights", 0.02, shape(stems, BLOCK, HW),
        inner_out, q_early, k_early, *their_keys,
        in_specs=[ANY] + [VMEM] * (1 + stems),
    )
    outer_out = call(
        lambda _, *refs: late_kernel(0, stems, *refs), "outer", 0.04, half,
        early_weights, held, *own, *others_outer, *their_frames, *weights, out_cross,
        in_specs=[ANY] + [VMEM] * (6 + 2 * stems),
    )
    return call(
        lambda *refs: early_kernel(stems, *refs), "early", 2, shape(1, rows, D),
        held, inner_out, outer_out, out_cross, first_early, early_weights, v_early, *their_values,
        scratch=[pltpu.VMEM((BLOCK, D), BF16), pltpu.SemaphoreType.DMA((3,))], out_specs=ANY,
    )


def solution(mesh):
    return jax.shard_map(
        on_device,
        mesh=mesh,
        in_specs=(P("stem", "tm", None), P(), P(), P(), P(), P(), P(), P(), P()),
        out_specs=P("stem", "tm", None),
        check_vma=False,
    )
```

```python
import jax
import jax.numpy as jnp
from jax import lax
from jax.experimental import pallas as pl
from jax.experimental.pallas import tpu as pltpu
from jax.sharding import PartitionSpec as P

D = 1024
H = 8
HD = 64
HW = H * HD
HALF = 256
BLOCK = 128
SLAB = 128
EPS = 1e-06
NEG = -1e30
F32 = jnp.float32
BF16 = jnp.bfloat16
VMEM = pl.BlockSpec(memory_space=pltpu.VMEM)
ANY = pl.BlockSpec(memory_space=pl.ANY)
LIMIT = 16 * 1024 * 1024


def cost(us):
    return pl.CostEstimate(flops=int(us * 1e9), bytes_accessed=int(us * 3e6), transcendentals=0)


def params():
    return pltpu.CompilerParams(vmem_limit_bytes=LIMIT)


def shape(*dims, dtype=BF16):
    return jax.ShapeDtypeStruct(dims, dtype)


def dot(a, b, dims=((1,), (0,))):
    return lax.dot_general(a, b, (dims, ((), ())), preferred_element_type=F32)


def modulated(rows, shift, scale):
    values = rows.astype(F32)
    centred = values - jnp.mean(values, axis=-1, keepdims=True)
    spread = jnp.mean(centred * centred, axis=-1, keepdims=True)
    normed = centred * lax.rsqrt(spread + EPS)
    return (normed * (1.0 + scale) + shift).astype(BF16)


def head_ones():
    row = lax.broadcasted_iota(jnp.int32, (2 * SLAB, 2 * SLAB), 0) // HD
    col = lax.broadcasted_iota(jnp.int32, (2 * SLAB, 2 * SLAB), 1) // HD
    return jnp.where(row == col, 1.0, 0.0).astype(BF16)


def head_sums(values, ones):
    parts = [dot(values[:, at : at + 2 * SLAB], ones) for at in range(0, HW, 2 * SLAB)]
    return jnp.concatenate(parts, axis=1)


def exact_head_sums(values, ones):
    high = values.astype(BF16)
    low = (values - high.astype(F32)).astype(BF16)
    return head_sums(high, ones) + head_sums(low, ones)


def head_norm(values, gain, ones):
    mean = head_sums((values * values).astype(BF16), ones) * (1.0 / HD)
    return (values * lax.rsqrt(mean + EPS) * gain).astype(BF16)


def wide_gain(gain):
    return jnp.concatenate([gain] * H, axis=1)


def window_bias(keys, ahead, first_frame=0, total=1 << 30):
    i = lax.broadcasted_iota(jnp.int32, (BLOCK, keys), 0)
    j = lax.broadcasted_iota(jnp.int32, (BLOCK, keys), 1)
    frame = first_frame + j
    keep = (j + ahead >= i) & (j + ahead <= i + 2 * HALF) & (frame >= 0) & (frame < total)
    return jnp.where(keep, 0.0, NEG)


def left_half():
    return lax.broadcasted_iota(jnp.int32, (BLOCK, SLAB), 1) < HD


def by_head(pair):
    return jnp.where(left_half(), pair[:BLOCK], pair[BLOCK:])


def window_scores(query, keys, bias):
    half, zero = left_half(), jnp.zeros_like(query)
    pair = jnp.concatenate([jnp.where(half, query, zero), jnp.where(half, zero, query)], axis=0)
    scores = dot(pair, keys, ((1,), (1,)))
    return jnp.concatenate([scores[:BLOCK] + bias, scores[BLOCK:] + bias], axis=0)


def raised(scores):
    top = jnp.max(scores, axis=-1, keepdims=True)
    return jnp.exp(scores - top).astype(BF16), top


def weighted(powers, values):
    summed = dot(powers, jnp.concatenate([values, jnp.ones_like(values)], axis=1))
    return by_head(summed[:, :SLAB]), by_head(summed[:, SLAB:])


SLABS = [slice(at, at + SLAB) for at in range(0, HW, SLAB)]


def cross_weights(query, keys, ones):
    query = query.astype(F32)
    base = keys[0].astype(F32)
    scores = [
        exact_head_sums(query * (k.astype(F32) - base), ones) * (HD ** -0.5) for k in keys[1:]
    ]
    top = jnp.zeros_like(query)
    for s in scores:
        top = jnp.maximum(top, s)
    powers = [jnp.exp(-top)] + [jnp.exp(s - top) for s in scores]
    total = powers[0]
    for p in powers[1:]:
        total = total + p
    scale = 1.0 / total
    return [(p * scale).astype(BF16) for p in powers]


def cross_sum(weights, values):
    out = jnp.zeros(values[0].shape, F32)
    for w, v in zip(weights, values):
        out = out + w.astype(F32) * v.astype(F32)
    return out.astype(BF16)


def mods_of(timestep, modulation, back):
    count = lax.axis_size("stem")
    stem = lax.rem(lax.axis_index("stem") + count - back, count)
    at = lax.broadcasted_iota(jnp.int32, (1, count), 1)
    step = jnp.sum(jnp.where(at == stem, timestep[...], 0).astype(F32), axis=1, keepdims=True)
    rows = lax.broadcasted_iota(jnp.int32, (modulation.shape[1], 1), 0).astype(F32)
    picked = rows == step
    return [
        jnp.sum(jnp.where(picked, modulation[i], 0.0), axis=0, keepdims=True) for i in range(6)
    ]


def mods_held(held, back):
    return lambda i: held[back, i : i + 1]


def places(rows):
    parity = lax.rem(lax.axis_index("tm"), 2)
    outer = pl.multiple_of(parity * HALF, BLOCK)
    early = pl.multiple_of((1 - parity) * HALF, BLOCK)
    return parity, outer, rows - HALF, early


def split_kernel(frames, late_rows, early_rows, sems):
    _, outer, inner, early = places(frames.shape[1])
    targets = (late_rows.at[pl.ds(0, BLOCK)], late_rows.at[pl.ds(BLOCK, BLOCK)], early_rows)
    copies = [
        pltpu.make_async_copy(frames.at[0, pl.ds(at, BLOCK)], to, sems.at[n])
        for n, (at, to) in enumerate(zip((outer, inner, early), targets))
    ]
    for copy in copies:
        copy.start()
    for copy in copies:
        copy.wait()


def mate_kernel(mate, outer_rows):
    outer_rows[...] = mate[0, pl.ds(places(mate.shape[1])[3], BLOCK)]


def part_steps(block, query, kv, part_out, part_sum, part_top):
    parity = lax.rem(lax.axis_index("tm"), 2)
    width = (HALF, BLOCK)[block]
    start = pl.multiple_of(parity * width, BLOCK)
    count = kv.shape[0] - width
    bias = window_bias(count, (1 - parity) * width)
    to = slice(block * BLOCK, (block + 1) * BLOCK)
    for cols in SLABS:
        scores = window_scores(query[:, cols], kv[pl.ds(start, count), cols], bias)
        yield
        powers, top = raised(scores)
        values = kv[pl.ds(start, count), HW + cols.start : HW + cols.stop]
        part_out[to, cols], part_sum[to, cols] = weighted(powers, values)
        part_top[to, cols] = by_head(jnp.broadcast_to(top, (2 * BLOCK, SLAB)))
        yield


def qkv_kernel(
    timestep, modulation, early_rows, late_rows, near, qkv_self, gains, query, kv, mate_kv, held
):
    rows = near.shape[1]

    def hold(k):
        for i, row in enumerate(mods_of(timestep, modulation, k)):
            held[k, i : i + 1] = row

    hold(0)
    parity, outer, inner, early = places(rows)
    mods = mods_held(held, 0)
    shift, scale = mods(0), mods(1)
    ones = head_ones()
    q_gain = wide_gain(gains[0:1]) * (HD ** -0.5)
    k_gain = wide_gain(gains[1:2])
    own_at = parity * HALF
    near_at = (1 - parity) * rows
    near_from = parity * (rows - HALF)

    sources = [
        (early_rows, 0, own_at + early),
        (late_rows, 0, own_at + outer),
        (late_rows, BLOCK, own_at + inner),
    ]
    for at in range(0, HALF, BLOCK):
        sources.append((near.at[0], pl.multiple_of(near_from + at, BLOCK), near_at + at))

    def normed(n):
        source, at, _ = sources[n]
        return modulated(source[pl.ds(at, BLOCK)], shift, scale)

    queries = []
    rows_n = normed(0)
    for n, (_, _, to) in enumerate(sources):
        at = pl.ds(pl.multiple_of(to, BLOCK), BLOCK)
        columns = (0, HW, 2 * HW) if n < 3 else (HW, 2 * HW)
        raw = [dot(rows_n, qkv_self[:, c : c + HW]) for c in columns]
        if n + 1 < len(sources):
            rows_n = normed(n + 1)
        if n < 3:
            queries.append(head_norm(raw[0], q_gain, ones))
        kv[at, :HW] = head_norm(raw[-2], k_gain, ones)
        kv[at, HW:] = raw[-1].astype(BF16)
    for n, each in enumerate(queries):
        query[n] = each
    mate_kv[...] = kv[pl.ds(pl.multiple_of((1 - parity) * (rows + BLOCK), BLOCK), BLOCK)]
    for k in range(1, held.shape[0]):
        hold(k)


def near_kernel(
    _, held, early_rows, query, kv, out_self, qkv_cross, gains_cross,
    part_out, part_sum, part_top, first, first_q, first_k, first_v,
):
    mods = mods_held(held, 0)
    ones = head_ones()
    parts = [part_steps(n, query.at[n + 1], kv, part_out, part_sum, part_top) for n in range(2)]

    def meanwhile(steps):
        while steps and parts:
            if next(parts[0], parts) is parts:
                parts.pop(0)
            else:
                steps -= 1

    bias = window_bias(kv.shape[0], 0)
    attended = []
    for cols in SLABS:
        scores = window_scores(query[0, :, cols], kv[:, cols], bias)
        meanwhile(2)
        powers, _ = raised(scores)
        out, total = weighted(powers, kv[:, HW + cols.start : HW + cols.stop])
        attended.append((out / total).astype(BF16))
    f = first_of(early_rows[...], jnp.concatenate(attended, axis=1), out_self, mods(2))
    first[...] = f
    meanwhile(3)
    normed_f = modulated(f, mods(3), mods(4))
    meanwhile(3)
    raw = [dot(normed_f, qkv_cross[:, at : at + HW]) for at in range(0, 3 * HW, HW)]
    meanwhile(4)
    first_q[...] = head_norm(raw[0], wide_gain(gains_cross[0:1]), ones)
    first_k[...] = head_norm(raw[1], wide_gain(gains_cross[1:2]), ones)
    first_v[...] = raw[2].astype(BF16)
    meanwhile(4 * HW)


def far_keys(rows, held, qkv_self, gains):
    mods = mods_held(held, 0)
    normed = modulated(rows, mods(0), mods(1))
    keys = dot(normed, qkv_self[:, HW : 2 * HW])
    values = dot(normed, qkv_self[:, 2 * HW :]).astype(BF16)
    return head_norm(keys, wide_gain(gains[1:2]), head_ones()), values


def far_bias(rows, block_start, outermost):
    place = lax.axis_index("tm")
    below = -2 * BLOCK if outermost else -BLOCK
    start = jnp.where(lax.rem(place, 2) == 0, below, rows + (BLOCK if outermost else 0))
    total = rows * lax.axis_size("tm")
    return window_bias(BLOCK, start - block_start + HALF, place * rows + start, total)


def far_attend(block, bias, query, keys, values, part_out, part_sum, part_top, attended):
    to = slice(block * BLOCK, (block + 1) * BLOCK)
    scores = [window_scores(query[block + 1, :, cols], keys[:, cols], bias) for cols in SLABS]
    powers = [raised(each) for each in scores]
    sums = [weighted(each, values[:, cols]) for (each, _), cols in zip(powers, SLABS)]
    for cols, (_, top), (out, summed) in zip(SLABS, powers, sums):
        top = by_head(jnp.broadcast_to(top, (2 * BLOCK, SLAB)))
        both = jnp.maximum(top, part_top[to, cols])
        here = jnp.exp(top - both)
        before = jnp.exp(part_top[to, cols] - both)
        out = out * here + part_out[to, cols] * before
        summed = summed * here + part_sum[to, cols] * before
        attended[:, cols] = (out / summed).astype(BF16)


def far_inner_kernel(rows, held, far, qkv_self, gains, query, *refs):
    *parts, attended, kv = refs
    keys, values = far_keys(far[...], held, qkv_self, gains)
    far_attend(1, far_bias(rows, rows - HALF, False), query, keys, values, *parts, attended)
    kv[:, :HW], kv[:, HW:] = keys, values


def far_outer_kernel(rows, early_values, far_kv, query, *refs):
    *parts, kv, attended, passed = refs
    passed[...] = early_values[...]
    keys = jnp.concatenate([kv[:, :HW], far_kv[:, :HW]], axis=0)
    values = jnp.concatenate([kv[:, HW:], far_kv[:, HW:]], axis=0)
    start = lax.rem(lax.axis_index("tm"), 2) * HALF
    bias = [far_bias(rows, start, outermost) for outermost in (False, True)]
    far_attend(0, jnp.concatenate(bias, axis=1), query, keys, values, *parts, attended)


def first_of(frames, attended, weight, gate):
    mixed = dot(attended, weight[...])
    return (frames.astype(F32) + gate * mixed).astype(BF16)


def projected_cross(first, mods, weight, gains, ones, with_query):
    normed = modulated(first, mods(3), mods(4))
    raw = [dot(normed, weight[:, at : at + HW]) for at in range(0 if with_query else HW, 3 * HW, HW)]
    query = head_norm(raw[0], wide_gain(gains[0:1]), ones) if with_query else None
    keys = head_norm(raw[-2], wide_gain(gains[1:2]), ones)
    return query, keys, raw[-1].astype(BF16)


def finished(first, attended, weight, gate):
    out = dot(attended, weight[...]).astype(BF16)
    return (first.astype(F32) + gate * out.astype(F32)).astype(BF16)


def own_kernel(held, frames, inner, outer, out_self, qkv_cross, gains, *refs):
    first, query, kv = refs[-3:]
    mods = mods_held(held, 0)
    ones = head_ones()
    parts = [slice(0, BLOCK), slice(BLOCK, HALF)]
    mixed = [dot(attended[...], out_self[...]) for attended in (outer, inner)]
    gains = [wide_gain(gains[i : i + 1]) for i in range(2)]

    def normed(n):
        f = (frames[parts[n]].astype(F32) + mods(2) * mixed[n]).astype(BF16)
        first[parts[n]] = f
        return modulated(f, mods(3), mods(4))

    rows = normed(0)
    for n, part in enumerate(parts):
        raw = [dot(rows, qkv_cross[:, at : at + HW]) for at in (2 * HW, 0, HW)]
        if n + 1 < len(parts):
            rows = normed(n + 1)
        kv[part, HW:] = raw[0].astype(BF16)
        query[part] = head_norm(raw[1], gains[0], ones)
        kv[part, :HW] = head_norm(raw[2], gains[1], ones)


def late_block(block, held, first, query, kv, others, their_frames, out_self, qkv_cross, gains, out_cross):
    ones = head_ones()
    part = slice(block * BLOCK, (block + 1) * BLOCK)
    keys, values = [kv[part, :HW]], [kv[part, HW:]]
    for n, (attended, source) in enumerate(zip(others, their_frames)):
        mods = mods_held(held, n + 1)
        g = first_of(source[part], attended[...], out_self, mods(2))
        _, k, v = projected_cross(g, mods, qkv_cross, gains, ones, False)
        keys.append(k)
        values.append(v)
    mixed = cross_sum(cross_weights(query[part], keys, ones), values)
    return finished(first[part], mixed, out_cross, mods_held(held, 0)(5))


def late_kernel(block, count, held, first, query, kv, *refs):
    others, their_frames = refs[: count - 1], refs[count - 1 : 2 * count - 2]
    *weights, out = refs[2 * count - 2 :]
    out[...] = late_block(block, held, first, query, kv, others, their_frames, *weights)


def weights_kernel(_, query, *refs):
    keys, out = refs[:-1], refs[-1]
    for n, each in enumerate(cross_weights(query[...], [k[...] for k in keys], head_ones())):
        out[n] = each


def early_kernel(count, held, inner_out, outer_out, out_cross, first, weights, *refs):
    values = refs[:count]
    out, early_out, sems = refs[count:]
    _, outer, inner, early = places(out.shape[1])
    copies = [
        pltpu.make_async_copy(source, out.at[0, pl.ds(at, BLOCK)], sems.at[n])
        for n, (source, at) in enumerate(((inner_out, inner), (outer_out, outer), (early_out, early)))
    ]
    copies[0].start()
    copies[1].start()
    mixed = cross_sum([weights[n] for n in range(count)], [v[...] for v in values])
    early_out[...] = finished(first[...], mixed, out_cross, mods_held(held, 0)(5))
    copies[2].start()
    for copy in copies:
        copy.wait()


def on_device(
    frames,
    timestep,
    modulation,
    qkv_self,
    out_self,
    qk_gain_self,
    qkv_cross,
    out_cross,
    qk_gain_cross,
):
    stems = lax.axis_size("stem")
    count = lax.axis_size("tm")
    rows = frames.shape[1]
    assert count % 2 == 0 and rows == HALF + BLOCK
    modulation = jnp.transpose(modulation, (1, 0, 2))
    inside = [(i, i ^ 1) for i in range(count)]
    across = [(i, i + 2) for i in range(0, count - 2, 2)]
    across += [(i + 3, i + 1) for i in range(0, count - 2, 2)]
    across += [(count - 2, count - 1), (1, 0)]

    def to_stems(array):
        return [
            lax.ppermute(array, "stem", [(i, (i + k) % stems) for i in range(stems)])
            for k in range(1, stems)
        ]

    def call(kernel, name, us, outs, *args, scratch=(), in_specs=None, out_specs=None):
        out_specs = out_specs or jax.tree.map(lambda _: VMEM, outs)
        return pl.pallas_call(
            kernel,
            out_shape=outs,
            in_specs=in_specs or [VMEM] * len(args),
            out_specs=out_specs,
            scratch_shapes=list(scratch),
            compiler_params=params(),
            cost_estimate=cost(us),
            name=name,
        )(*args)

    half = shape(BLOCK, D)
    late_rows, early_rows = call(
        split_kernel, "split", 4, (shape(HALF, D), half), frames,
        scratch=[pltpu.SemaphoreType.DMA((3,))], in_specs=[ANY], out_specs=(ANY, ANY),
    )
    their_frames = to_stems(late_rows)
    near = lax.ppermute(frames, "tm", inside)
    mate_outer = call(mate_kernel, "mate", 0.1, half, near)
    far = lax.ppermute(mate_outer, "tm", across)

    late, block, part = shape(HALF, HW), shape(BLOCK, HW), shape(HALF, HW, dtype=F32)
    query, kv, mate_kv, held = call(
        qkv_kernel, "qkv", 0.06,
        (shape(3, BLOCK, HW), shape(rows + HALF, 2 * HW), half, shape(stems, 8, D, dtype=F32)),
        timestep.reshape(1, -1), modulation, early_rows, late_rows, near, qkv_self, qk_gain_self,
    )
    farther = lax.ppermute(mate_kv, "tm", across)
    part_out, part_sum, part_top, first_early, q_early, k_early, v_early = call(
        near_kernel, "near", 0.06, (part, part, part, half, block, block, block),
        mate_kv, held, early_rows, query, kv, out_self, qkv_cross, qk_gain_cross,
        in_specs=[ANY] + [VMEM] * 7,
    )
    their_keys = to_stems(k_early)
    parts = (part_out, part_sum, part_top)

    self_weights = (qkv_self, qk_gain_self)
    att_inner, far_kv = call(
        lambda *refs: far_inner_kernel(rows, *refs), "far_inner", 0.04, (block, half),
        held, far, *self_weights, query, *parts,
    )
    others_inner = to_stems(att_inner)
    att_outer, passed = call(
        lambda *refs: far_outer_kernel(rows, *refs), "far_outer", 0.006, (block, block),
        v_early, farther, query, *parts, far_kv,
    )
    others_outer = to_stems(att_outer)
    their_values = to_stems(passed)

    weights = (out_self, qkv_cross, qk_gain_cross)
    own = call(
        own_kernel, "own", 0.02, (shape(HALF, D), late, shape(HALF, D)),
        held, late_rows, att_inner, att_outer, *weights, *their_keys,
        in_specs=[VMEM] * 7 + [ANY] * (stems - 1),
    )
    inner_out = call(
        lambda *refs: late_kernel(1, stems, *refs), "inner", 0.04, half,
        held, *own, *others_inner, *their_frames, *weights, out_cross,
    )
    early_weights = call(
        weights_kernel, "weights", 0.02, shape(stems, BLOCK, HW),
        inner_out, q_early, k_early, *their_keys,
        in_specs=[ANY] + [VMEM] * (1 + stems),
    )
    outer_out = call(
        lambda _, *refs: late_kernel(0, stems, *refs), "outer", 0.04, half,
        early_weights, held, *own, *others_outer, *their_frames, *weights, out_cross,
        in_specs=[ANY] + [VMEM] * (6 + 2 * stems),
    )
    return call(
        lambda *refs: early_kernel(stems, *refs), "early", 2, shape(1, rows, D),
        held, inner_out, outer_out, out_cross, first_early, early_weights, v_early, *their_values,
        scratch=[pltpu.VMEM((BLOCK, D), BF16), pltpu.SemaphoreType.DMA((3,))], out_specs=ANY,
    )


def solution(mesh):
    return jax.shard_map(
        on_device,
        mesh=mesh,
        in_specs=(P("stem", "tm", None), P(), P(), P(), P(), P(), P(), P(), P()),
        out_specs=P("stem", "tm", None),
        check_vma=False,
    )
```

```python
import jax
import jax.numpy as jnp
from jax import lax
from jax.experimental import pallas as pl
from jax.experimental.pallas import tpu as pltpu
from jax.sharding import PartitionSpec as P

D = 1024
H = 8
HD = 64
HW = H * HD
HALF = 256
BLOCK = 128
SLAB = 128
EPS = 1e-06
NEG = -1e30
F32 = jnp.float32
BF16 = jnp.bfloat16
VMEM = pl.BlockSpec(memory_space=pltpu.VMEM)
ANY = pl.BlockSpec(memory_space=pl.ANY)
LIMIT = 16 * 1024 * 1024


def cost(us):
    return pl.CostEstimate(flops=int(us * 1e9), bytes_accessed=int(us * 3e6), transcendentals=0)


def params():
    return pltpu.CompilerParams(vmem_limit_bytes=LIMIT)


def shape(*dims, dtype=BF16):
    return jax.ShapeDtypeStruct(dims, dtype)


def dot(a, b, dims=((1,), (0,))):
    return lax.dot_general(a, b, (dims, ((), ())), preferred_element_type=F32)


def modulated(rows, shift, scale):
    values = rows.astype(F32)
    centred = values - jnp.mean(values, axis=-1, keepdims=True)
    spread = jnp.mean(centred * centred, axis=-1, keepdims=True)
    normed = centred * lax.rsqrt(spread + EPS)
    return (normed * (1.0 + scale) + shift).astype(BF16)


def head_ones():
    row = lax.broadcasted_iota(jnp.int32, (2 * SLAB, 2 * SLAB), 0) // HD
    col = lax.broadcasted_iota(jnp.int32, (2 * SLAB, 2 * SLAB), 1) // HD
    return jnp.where(row == col, 1.0, 0.0).astype(BF16)


def head_sums(values, ones):
    parts = [dot(values[:, at : at + 2 * SLAB], ones) for at in range(0, HW, 2 * SLAB)]
    return jnp.concatenate(parts, axis=1)


def exact_head_sums(values, ones):
    high = values.astype(BF16)
    low = (values - high.astype(F32)).astype(BF16)
    return head_sums(high, ones) + head_sums(low, ones)


def head_norm(values, gain, ones):
    mean = head_sums((values * values).astype(BF16), ones) * (1.0 / HD)
    return (values * lax.rsqrt(mean + EPS) * gain).astype(BF16)


def wide_gain(gain):
    return jnp.concatenate([gain] * H, axis=1)


def window_bias(keys, ahead, first_frame=0, total=1 << 30):
    i = lax.broadcasted_iota(jnp.int32, (BLOCK, keys), 0)
    j = lax.broadcasted_iota(jnp.int32, (BLOCK, keys), 1)
    frame = first_frame + j
    keep = (j + ahead >= i) & (j + ahead <= i + 2 * HALF) & (frame >= 0) & (frame < total)
    return jnp.where(keep, 0.0, NEG)


def left_half():
    return lax.broadcasted_iota(jnp.int32, (BLOCK, SLAB), 1) < HD


def by_head(pair):
    return jnp.where(left_half(), pair[:BLOCK], pair[BLOCK:])


def window_scores(query, keys, bias):
    half, zero = left_half(), jnp.zeros_like(query)
    pair = jnp.concatenate([jnp.where(half, query, zero), jnp.where(half, zero, query)], axis=0)
    scores = dot(pair, keys, ((1,), (1,)))
    return jnp.concatenate([scores[:BLOCK] + bias, scores[BLOCK:] + bias], axis=0)


def raised(scores):
    top = jnp.max(scores, axis=-1, keepdims=True)
    return jnp.exp(scores - top).astype(BF16), top


def weighted(powers, values):
    summed = dot(powers, jnp.concatenate([values, jnp.ones_like(values)], axis=1))
    return by_head(summed[:, :SLAB]), by_head(summed[:, SLAB:])


SLABS = [slice(at, at + SLAB) for at in range(0, HW, SLAB)]


def cross_weights(query, keys, ones):
    query = query.astype(F32)
    base = keys[0].astype(F32)
    scores = [
        exact_head_sums(query * (k.astype(F32) - base), ones) * (HD ** -0.5) for k in keys[1:]
    ]
    top = jnp.zeros_like(query)
    for s in scores:
        top = jnp.maximum(top, s)
    powers = [jnp.exp(-top)] + [jnp.exp(s - top) for s in scores]
    total = powers[0]
    for p in powers[1:]:
        total = total + p
    scale = 1.0 / total
    return [(p * scale).astype(BF16) for p in powers]


def cross_sum(weights, values):
    out = jnp.zeros(values[0].shape, F32)
    for w, v in zip(weights, values):
        out = out + w.astype(F32) * v.astype(F32)
    return out.astype(BF16)


def mods_of(timestep, modulation, back):
    count = lax.axis_size("stem")
    stem = lax.rem(lax.axis_index("stem") + count - back, count)
    at = lax.broadcasted_iota(jnp.int32, (1, count), 1)
    step = jnp.sum(jnp.where(at == stem, timestep[...], 0).astype(F32), axis=1, keepdims=True)
    rows = lax.broadcasted_iota(jnp.int32, (modulation.shape[1], 1), 0).astype(F32)
    picked = rows == step
    return [
        jnp.sum(jnp.where(picked, modulation[i], 0.0), axis=0, keepdims=True) for i in range(6)
    ]


def mods_held(held, back):
    return lambda i: held[back, i : i + 1]


def places(rows):
    parity = lax.rem(lax.axis_index("tm"), 2)
    outer = pl.multiple_of(parity * HALF, BLOCK)
    early = pl.multiple_of((1 - parity) * HALF, BLOCK)
    return parity, outer, rows - HALF, early


def split_kernel(frames, late_rows, early_rows, sems):
    _, outer, inner, early = places(frames.shape[1])
    targets = (late_rows.at[pl.ds(0, BLOCK)], late_rows.at[pl.ds(BLOCK, BLOCK)], early_rows)
    copies = [
        pltpu.make_async_copy(frames.at[0, pl.ds(at, BLOCK)], to, sems.at[n])
        for n, (at, to) in enumerate(zip((outer, inner, early), targets))
    ]
    for copy in copies:
        copy.start()
    for copy in copies:
        copy.wait()


def mate_kernel(mate, outer_rows):
    outer_rows[...] = mate[0, pl.ds(places(mate.shape[1])[3], BLOCK)]


def part_steps(block, query, kv, part_out, part_sum, part_top):
    parity = lax.rem(lax.axis_index("tm"), 2)
    width = (HALF, BLOCK)[block]
    start = pl.multiple_of(parity * width, BLOCK)
    count = kv.shape[0] - width
    bias = window_bias(count, (1 - parity) * width)
    to = slice(block * BLOCK, (block + 1) * BLOCK)
    for cols in SLABS:
        scores = window_scores(query[:, cols], kv[pl.ds(start, count), cols], bias)
        yield
        powers, top = raised(scores)
        values = kv[pl.ds(start, count), HW + cols.start : HW + cols.stop]
        part_out[to, cols], part_sum[to, cols] = weighted(powers, values)
        part_top[to, cols] = by_head(jnp.broadcast_to(top, (2 * BLOCK, SLAB)))
        yield


def qkv_kernel(
    timestep, modulation, early_rows, late_rows, near, qkv_self, gains, query, kv, mate_kv, held
):
    rows = near.shape[1]

    def hold(k):
        for i, row in enumerate(mods_of(timestep, modulation, k)):
            held[k, i : i + 1] = row

    hold(0)
    parity, outer, inner, early = places(rows)
    mods = mods_held(held, 0)
    shift, scale = mods(0), mods(1)
    ones = head_ones()
    q_gain = wide_gain(gains[0:1]) * (HD ** -0.5)
    k_gain = wide_gain(gains[1:2])
    own_at = parity * HALF
    near_at = (1 - parity) * rows
    near_from = parity * (rows - HALF)

    sources = [
        (early_rows, 0, own_at + early),
        (late_rows, 0, own_at + outer),
        (late_rows, BLOCK, own_at + inner),
    ]
    for at in range(0, HALF, BLOCK):
        sources.append((near.at[0], pl.multiple_of(near_from + at, BLOCK), near_at + at))

    def normed(n):
        source, at, _ = sources[n]
        return modulated(source[pl.ds(at, BLOCK)], shift, scale)

    queries = []
    rows_n = normed(0)
    for n, (_, _, to) in enumerate(sources):
        at = pl.ds(pl.multiple_of(to, BLOCK), BLOCK)
        columns = (0, HW, 2 * HW) if n < 3 else (HW, 2 * HW)
        raw = [dot(rows_n, qkv_self[:, c : c + HW]) for c in columns]
        if n + 1 < len(sources):
            rows_n = normed(n + 1)
        if n < 3:
            queries.append(head_norm(raw[0], q_gain, ones))
        kv[at, :HW] = head_norm(raw[-2], k_gain, ones)
        kv[at, HW:] = raw[-1].astype(BF16)
    for n, each in enumerate(queries):
        query[n] = each
    mate_kv[...] = kv[pl.ds(pl.multiple_of((1 - parity) * (rows + BLOCK), BLOCK), BLOCK)]
    for k in range(1, held.shape[0]):
        hold(k)


def near_kernel(
    _, held, early_rows, query, kv, out_self, qkv_cross, gains_cross,
    part_out, part_sum, part_top, first, first_q, first_k, first_v,
):
    mods = mods_held(held, 0)
    ones = head_ones()
    parts = [part_steps(n, query.at[n + 1], kv, part_out, part_sum, part_top) for n in range(2)]

    def meanwhile(steps):
        while steps and parts:
            if next(parts[0], parts) is parts:
                parts.pop(0)
            else:
                steps -= 1

    bias = window_bias(kv.shape[0], 0)
    attended = []
    for cols in SLABS:
        scores = window_scores(query[0, :, cols], kv[:, cols], bias)
        meanwhile(2)
        powers, _ = raised(scores)
        out, total = weighted(powers, kv[:, HW + cols.start : HW + cols.stop])
        attended.append((out / total).astype(BF16))
    f = first_of(early_rows[...], jnp.concatenate(attended, axis=1), out_self, mods(2))
    first[...] = f
    meanwhile(3)
    normed_f = modulated(f, mods(3), mods(4))
    meanwhile(3)
    raw = [dot(normed_f, qkv_cross[:, at : at + HW]) for at in range(0, 3 * HW, HW)]
    meanwhile(4)
    first_q[...] = head_norm(raw[0], wide_gain(gains_cross[0:1]), ones)
    first_k[...] = head_norm(raw[1], wide_gain(gains_cross[1:2]), ones)
    first_v[...] = raw[2].astype(BF16)
    meanwhile(4 * HW)


def far_keys(rows, held, qkv_self, gains):
    mods = mods_held(held, 0)
    normed = modulated(rows, mods(0), mods(1))
    keys = dot(normed, qkv_self[:, HW : 2 * HW])
    values = dot(normed, qkv_self[:, 2 * HW :]).astype(BF16)
    return head_norm(keys, wide_gain(gains[1:2]), head_ones()), values


def far_bias(rows, block_start, outermost):
    place = lax.axis_index("tm")
    below = -2 * BLOCK if outermost else -BLOCK
    start = jnp.where(lax.rem(place, 2) == 0, below, rows + (BLOCK if outermost else 0))
    total = rows * lax.axis_size("tm")
    return window_bias(BLOCK, start - block_start + HALF, place * rows + start, total)


def far_attend(block, bias, query, keys, values, part_out, part_sum, part_top, attended):
    to = slice(block * BLOCK, (block + 1) * BLOCK)
    scores = [window_scores(query[block + 1, :, cols], keys[:, cols], bias) for cols in SLABS]
    powers = [raised(each) for each in scores]
    sums = [weighted(each, values[:, cols]) for (each, _), cols in zip(powers, SLABS)]
    for cols, (_, top), (out, summed) in zip(SLABS, powers, sums):
        top = by_head(jnp.broadcast_to(top, (2 * BLOCK, SLAB)))
        both = jnp.maximum(top, part_top[to, cols])
        here = jnp.exp(top - both)
        before = jnp.exp(part_top[to, cols] - both)
        out = out * here + part_out[to, cols] * before
        summed = summed * here + part_sum[to, cols] * before
        attended[:, cols] = (out / summed).astype(BF16)


def far_inner_kernel(rows, held, far, qkv_self, gains, query, *refs):
    *parts, attended, kv = refs
    keys, values = far_keys(far[...], held, qkv_self, gains)
    far_attend(1, far_bias(rows, rows - HALF, False), query, keys, values, *parts, attended)
    kv[:, :HW], kv[:, HW:] = keys, values


def far_outer_kernel(rows, far_kv, query, *refs):
    *parts, kv, attended = refs
    keys = jnp.concatenate([kv[:, :HW], far_kv[:, :HW]], axis=0)
    values = jnp.concatenate([kv[:, HW:], far_kv[:, HW:]], axis=0)
    start = lax.rem(lax.axis_index("tm"), 2) * HALF
    bias = [far_bias(rows, start, outermost) for outermost in (False, True)]
    far_attend(0, jnp.concatenate(bias, axis=1), query, keys, values, *parts, attended)


def first_of(frames, attended, weight, gate):
    mixed = dot(attended, weight[...])
    return (frames.astype(F32) + gate * mixed).astype(BF16)


def projected_cross(first, mods, weight, gains, ones, with_query):
    normed = modulated(first, mods(3), mods(4))
    raw = [dot(normed, weight[:, at : at + HW]) for at in range(0 if with_query else HW, 3 * HW, HW)]
    query = head_norm(raw[0], wide_gain(gains[0:1]), ones) if with_query else None
    keys = head_norm(raw[-2], wide_gain(gains[1:2]), ones)
    return query, keys, raw[-1].astype(BF16)


def finished(first, attended, weight, gate):
    out = dot(attended, weight[...]).astype(BF16)
    return (first.astype(F32) + gate * out.astype(F32)).astype(BF16)


def own_kernel(early_values, held, frames, inner, outer, out_self, qkv_cross, gains, *refs):
    first, query, kv, passed = refs[-4:]
    passed[...] = early_values[...]
    mods = mods_held(held, 0)
    ones = head_ones()
    parts = [slice(0, BLOCK), slice(BLOCK, HALF)]
    mixed = [dot(attended[...], out_self[...]) for attended in (outer, inner)]
    gains = [wide_gain(gains[i : i + 1]) for i in range(2)]

    def normed(n):
        f = (frames[parts[n]].astype(F32) + mods(2) * mixed[n]).astype(BF16)
        first[parts[n]] = f
        return modulated(f, mods(3), mods(4))

    rows = normed(0)
    for n, part in enumerate(parts):
        raw = [dot(rows, qkv_cross[:, at : at + HW]) for at in (2 * HW, 0, HW)]
        if n + 1 < len(parts):
            rows = normed(n + 1)
        kv[part, HW:] = raw[0].astype(BF16)
        query[part] = head_norm(raw[1], gains[0], ones)
        kv[part, :HW] = head_norm(raw[2], gains[1], ones)


def late_block(block, held, first, query, kv, others, their_frames, out_self, qkv_cross, gains, out_cross):
    ones = head_ones()
    part = slice(block * BLOCK, (block + 1) * BLOCK)
    keys, values = [kv[part, :HW]], [kv[part, HW:]]
    for n, (attended, source) in enumerate(zip(others, their_frames)):
        mods = mods_held(held, n + 1)
        g = first_of(source[part], attended[...], out_self, mods(2))
        _, k, v = projected_cross(g, mods, qkv_cross, gains, ones, False)
        keys.append(k)
        values.append(v)
    mixed = cross_sum(cross_weights(query[part], keys, ones), values)
    return finished(first[part], mixed, out_cross, mods_held(held, 0)(5))


def late_kernel(block, count, held, first, query, kv, *refs):
    others, their_frames = refs[: count - 1], refs[count - 1 : 2 * count - 2]
    *weights, out = refs[2 * count - 2 :]
    out[...] = late_block(block, held, first, query, kv, others, their_frames, *weights)


def weights_kernel(_, query, *refs):
    keys, out = refs[:-1], refs[-1]
    for n, each in enumerate(cross_weights(query[...], [k[...] for k in keys], head_ones())):
        out[n] = each


def early_kernel(count, held, inner_out, outer_out, out_cross, first, weights, *refs):
    values = refs[:count]
    out, early_out, sems = refs[count:]
    _, outer, inner, early = places(out.shape[1])
    copies = [
        pltpu.make_async_copy(source, out.at[0, pl.ds(at, BLOCK)], sems.at[n])
        for n, (source, at) in enumerate(((inner_out, inner), (outer_out, outer), (early_out, early)))
    ]
    copies[0].start()
    copies[1].start()
    mixed = cross_sum([weights[n] for n in range(count)], [v[...] for v in values])
    early_out[...] = finished(first[...], mixed, out_cross, mods_held(held, 0)(5))
    copies[2].start()
    for copy in copies:
        copy.wait()


def on_device(
    frames,
    timestep,
    modulation,
    qkv_self,
    out_self,
    qk_gain_self,
    qkv_cross,
    out_cross,
    qk_gain_cross,
):
    stems = lax.axis_size("stem")
    count = lax.axis_size("tm")
    rows = frames.shape[1]
    assert count % 2 == 0 and rows == HALF + BLOCK
    modulation = jnp.transpose(modulation, (1, 0, 2))
    inside = [(i, i ^ 1) for i in range(count)]
    across = [(i, i + 2) for i in range(0, count - 2, 2)]
    across += [(i + 3, i + 1) for i in range(0, count - 2, 2)]
    across += [(count - 2, count - 1), (1, 0)]

    def to_stems(array):
        return [
            lax.ppermute(array, "stem", [(i, (i + k) % stems) for i in range(stems)])
            for k in range(1, stems)
        ]

    def call(kernel, name, us, outs, *args, scratch=(), in_specs=None, out_specs=None):
        out_specs = out_specs or jax.tree.map(lambda _: VMEM, outs)
        return pl.pallas_call(
            kernel,
            out_shape=outs,
            in_specs=in_specs or [VMEM] * len(args),
            out_specs=out_specs,
            scratch_shapes=list(scratch),
            compiler_params=params(),
            cost_estimate=cost(us),
            name=name,
        )(*args)

    half = shape(BLOCK, D)
    late_rows, early_rows = call(
        split_kernel, "split", 4, (shape(HALF, D), half), frames,
        scratch=[pltpu.SemaphoreType.DMA((3,))], in_specs=[ANY], out_specs=(ANY, ANY),
    )
    their_frames = to_stems(late_rows)
    near = lax.ppermute(frames, "tm", inside)
    mate_outer = call(mate_kernel, "mate", 0.1, half, near)
    far = lax.ppermute(mate_outer, "tm", across)

    late, block, part = shape(HALF, HW), shape(BLOCK, HW), shape(HALF, HW, dtype=F32)
    query, kv, mate_kv, held = call(
        qkv_kernel, "qkv", 0.06,
        (shape(3, BLOCK, HW), shape(rows + HALF, 2 * HW), half, shape(stems, 8, D, dtype=F32)),
        timestep.reshape(1, -1), modulation, early_rows, late_rows, near, qkv_self, qk_gain_self,
    )
    farther = lax.ppermute(mate_kv, "tm", across)
    part_out, part_sum, part_top, first_early, q_early, k_early, v_early = call(
        near_kernel, "near", 0.06, (part, part, part, half, block, block, block),
        mate_kv, held, early_rows, query, kv, out_self, qkv_cross, qk_gain_cross,
        in_specs=[ANY] + [VMEM] * 7,
    )
    their_keys = to_stems(k_early)
    parts = (part_out, part_sum, part_top)

    self_weights = (qkv_self, qk_gain_self)
    att_inner, far_kv = call(
        lambda *refs: far_inner_kernel(rows, *refs), "far_inner", 0.04, (block, half),
        held, far, *self_weights, query, *parts,
    )
    others_inner = to_stems(att_inner)
    att_outer = call(
        lambda *refs: far_outer_kernel(rows, *refs), "far_outer", 0.006, block,
        farther, query, *parts, far_kv,
    )
    others_outer = to_stems(att_outer)

    weights = (out_self, qkv_cross, qk_gain_cross)
    *own, passed = call(
        own_kernel, "own", 0.02, (shape(HALF, D), late, shape(HALF, D), block),
        v_early, held, late_rows, att_inner, att_outer, *weights, *their_keys,
        in_specs=[VMEM] * 8 + [ANY] * (stems - 1),
    )
    their_values = to_stems(passed)
    inner_out = call(
        lambda *refs: late_kernel(1, stems, *refs), "inner", 0.04, half,
        held, *own, *others_inner, *their_frames, *weights, out_cross,
    )
    early_weights = call(
        weights_kernel, "weights", 0.02, shape(stems, BLOCK, HW),
        inner_out, q_early, k_early, *their_keys,
        in_specs=[ANY] + [VMEM] * (1 + stems),
    )
    outer_out = call(
        lambda _, *refs: late_kernel(0, stems, *refs), "outer", 0.04, half,
        early_weights, held, *own, *others_outer, *their_frames, *weights, out_cross,
        in_specs=[ANY] + [VMEM] * (6 + 2 * stems),
    )
    return call(
        lambda *refs: early_kernel(stems, *refs), "early", 2, shape(1, rows, D),
        held, inner_out, outer_out, out_cross, first_early, early_weights, v_early, *their_values,
        scratch=[pltpu.VMEM((BLOCK, D), BF16), pltpu.SemaphoreType.DMA((3,))], out_specs=ANY,
    )


def solution(mesh):
    return jax.shard_map(
        on_device,
        mesh=mesh,
        in_specs=(P("stem", "tm", None), P(), P(), P(), P(), P(), P(), P(), P()),
        out_specs=P("stem", "tm", None),
        check_vma=False,
    )
```

```python
import jax
import jax.numpy as jnp
from jax import lax
from jax.experimental import pallas as pl
from jax.experimental.pallas import tpu as pltpu
from jax.sharding import PartitionSpec as P

D = 1024
H = 8
HD = 64
HW = H * HD
HALF = 256
BLOCK = 128
SLAB = 128
EPS = 1e-06
NEG = -1e30
F32 = jnp.float32
BF16 = jnp.bfloat16
VMEM = pl.BlockSpec(memory_space=pltpu.VMEM)
ANY = pl.BlockSpec(memory_space=pl.ANY)
LIMIT = 16 * 1024 * 1024


def cost(us):
    return pl.CostEstimate(flops=int(us * 1e9), bytes_accessed=int(us * 3e6), transcendentals=0)


def params():
    return pltpu.CompilerParams(vmem_limit_bytes=LIMIT)


def shape(*dims, dtype=BF16):
    return jax.ShapeDtypeStruct(dims, dtype)


def dot(a, b, dims=((1,), (0,))):
    return lax.dot_general(a, b, (dims, ((), ())), preferred_element_type=F32)


def modulated(rows, shift, scale):
    values = rows.astype(F32)
    centred = values - jnp.mean(values, axis=-1, keepdims=True)
    spread = jnp.mean(centred * centred, axis=-1, keepdims=True)
    normed = centred * lax.rsqrt(spread + EPS)
    return (normed * (1.0 + scale) + shift).astype(BF16)


def head_ones():
    row = lax.broadcasted_iota(jnp.int32, (2 * SLAB, 2 * SLAB), 0) // HD
    col = lax.broadcasted_iota(jnp.int32, (2 * SLAB, 2 * SLAB), 1) // HD
    return jnp.where(row == col, 1.0, 0.0).astype(BF16)


def head_sums(values, ones):
    parts = [dot(values[:, at : at + 2 * SLAB], ones) for at in range(0, HW, 2 * SLAB)]
    return jnp.concatenate(parts, axis=1)


def exact_head_sums(values, ones):
    high = values.astype(BF16)
    low = (values - high.astype(F32)).astype(BF16)
    return head_sums(high, ones) + head_sums(low, ones)


def head_norm(values, gain, ones):
    mean = head_sums((values * values).astype(BF16), ones) * (1.0 / HD)
    return (values * lax.rsqrt(mean + EPS) * gain).astype(BF16)


def wide_gain(gain):
    return jnp.concatenate([gain] * H, axis=1)


def window_bias(keys, ahead, first_frame=0, total=1 << 30):
    i = lax.broadcasted_iota(jnp.int32, (BLOCK, keys), 0)
    j = lax.broadcasted_iota(jnp.int32, (BLOCK, keys), 1)
    frame = first_frame + j
    keep = (j + ahead >= i) & (j + ahead <= i + 2 * HALF) & (frame >= 0) & (frame < total)
    return jnp.where(keep, 0.0, NEG)


def left_half():
    return lax.broadcasted_iota(jnp.int32, (BLOCK, SLAB), 1) < HD


def by_head(pair):
    return jnp.where(left_half(), pair[:BLOCK], pair[BLOCK:])


def window_scores(query, keys, bias):
    half, zero = left_half(), jnp.zeros_like(query)
    pair = jnp.concatenate([jnp.where(half, query, zero), jnp.where(half, zero, query)], axis=0)
    scores = dot(pair, keys, ((1,), (1,)))
    return jnp.concatenate([scores[:BLOCK] + bias, scores[BLOCK:] + bias], axis=0)


def raised(scores):
    top = jnp.max(scores, axis=-1, keepdims=True)
    return jnp.exp(scores - top).astype(BF16), top


def weighted(powers, values):
    summed = dot(powers, jnp.concatenate([values, jnp.ones_like(values)], axis=1))
    return by_head(summed[:, :SLAB]), by_head(summed[:, SLAB:])


SLABS = [slice(at, at + SLAB) for at in range(0, HW, SLAB)]


def cross_weights(query, keys, ones):
    query = query.astype(F32)
    base = keys[0].astype(F32)
    scores = [
        exact_head_sums(query * (k.astype(F32) - base), ones) * (HD ** -0.5) for k in keys[1:]
    ]
    top = jnp.zeros_like(query)
    for s in scores:
        top = jnp.maximum(top, s)
    powers = [jnp.exp(-top)] + [jnp.exp(s - top) for s in scores]
    total = powers[0]
    for p in powers[1:]:
        total = total + p
    scale = 1.0 / total
    return [(p * scale).astype(BF16) for p in powers]


def cross_sum(weights, values):
    out = jnp.zeros(values[0].shape, F32)
    for w, v in zip(weights, values):
        out = out + w.astype(F32) * v.astype(F32)
    return out.astype(BF16)


def mods_of(timestep, modulation, back):
    count = lax.axis_size("stem")
    stem = lax.rem(lax.axis_index("stem") + count - back, count)
    at = lax.broadcasted_iota(jnp.int32, (1, count), 1)
    step = jnp.sum(jnp.where(at == stem, timestep[...], 0).astype(F32), axis=1, keepdims=True)
    rows = lax.broadcasted_iota(jnp.int32, (modulation.shape[1], 1), 0).astype(F32)
    picked = rows == step
    return [
        jnp.sum(jnp.where(picked, modulation[i], 0.0), axis=0, keepdims=True) for i in range(6)
    ]


def mods_held(held, back):
    return lambda i: held[back, i : i + 1]


def places(rows):
    parity = lax.rem(lax.axis_index("tm"), 2)
    outer = pl.multiple_of(parity * HALF, BLOCK)
    early = pl.multiple_of((1 - parity) * HALF, BLOCK)
    return parity, outer, rows - HALF, early


def split_kernel(frames, late_rows, early_rows, sems):
    _, outer, inner, early = places(frames.shape[1])
    targets = (late_rows.at[pl.ds(0, BLOCK)], late_rows.at[pl.ds(BLOCK, BLOCK)], early_rows)
    copies = [
        pltpu.make_async_copy(frames.at[0, pl.ds(at, BLOCK)], to, sems.at[n])
        for n, (at, to) in enumerate(zip((outer, inner, early), targets))
    ]
    for copy in copies:
        copy.start()
    for copy in copies:
        copy.wait()


def mate_kernel(mate, outer_rows, inner_rows):
    _, _, inner, outer = places(mate.shape[1])
    outer_rows[...] = mate[0, pl.ds(outer, BLOCK)]
    inner_rows[...] = mate[0, inner : inner + BLOCK]


def part_steps(block, query, kv, part_out, part_sum, part_top):
    parity = lax.rem(lax.axis_index("tm"), 2)
    width = (HALF, BLOCK)[block]
    start = pl.multiple_of(parity * width, BLOCK)
    count = kv.shape[0] - width
    bias = window_bias(count, (1 - parity) * width)
    to = slice(block * BLOCK, (block + 1) * BLOCK)
    for cols in SLABS:
        scores = window_scores(query[:, cols], kv[pl.ds(start, count), cols], bias)
        yield
        powers, top = raised(scores)
        values = kv[pl.ds(start, count), HW + cols.start : HW + cols.stop]
        part_out[to, cols], part_sum[to, cols] = weighted(powers, values)
        part_top[to, cols] = by_head(jnp.broadcast_to(top, (2 * BLOCK, SLAB)))
        yield


def near_kernel(
    timestep, modulation, early_rows, late_rows, near, qkv_self, gains, out_self, qkv_cross, gains_cross,
    query, part_out, part_sum, part_top, first, first_q, first_k, first_v, held, kv,
):
    rows = near.shape[1]

    def hold(k):
        for i, row in enumerate(mods_of(timestep, modulation, k)):
            held[k, i : i + 1] = row

    hold(0)
    parity, outer, inner, early = places(rows)
    mods = mods_held(held, 0)
    shift, scale = mods(0), mods(1)
    ones = head_ones()
    q_gain = wide_gain(gains[0:1]) * (HD ** -0.5)
    k_gain = wide_gain(gains[1:2])
    own_at = parity * HALF
    near_at = (1 - parity) * rows
    near_from = parity * (rows - HALF)

    sources = [
        (early_rows, 0, own_at + early),
        (late_rows, 0, own_at + outer),
        (late_rows, BLOCK, own_at + inner),
    ]
    for at in range(0, HALF, BLOCK):
        sources.append((near.at[0], pl.multiple_of(near_from + at, BLOCK), near_at + at))

    def normed(n):
        source, at, _ = sources[n]
        return modulated(source[pl.ds(at, BLOCK)], shift, scale)

    queries = []
    rows_n = normed(0)
    for n, (_, _, to) in enumerate(sources):
        at = pl.ds(pl.multiple_of(to, BLOCK), BLOCK)
        columns = (0, HW, 2 * HW) if n < 3 else (HW, 2 * HW)
        raw = [dot(rows_n, qkv_self[:, c : c + HW]) for c in columns]
        if n + 1 < len(sources):
            rows_n = normed(n + 1)
        if n < 3:
            queries.append(head_norm(raw[0], q_gain, ones))
        kv[at, :HW] = head_norm(raw[-2], k_gain, ones)
        kv[at, HW:] = raw[-1].astype(BF16)
    query[:BLOCK] = queries[1]
    query[BLOCK:] = queries[2]
    for k in range(1, held.shape[0]):
        hold(k)

    parts = [part_steps(n, queries[n + 1], kv, part_out, part_sum, part_top) for n in range(2)]

    def meanwhile(steps):
        while steps and parts:
            if next(parts[0], parts) is parts:
                parts.pop(0)
            else:
                steps -= 1

    bias = window_bias(rows + HALF, 0)
    attended = []
    for cols in SLABS:
        scores = window_scores(queries[0][:, cols], kv[:, cols], bias)
        meanwhile(2)
        powers, _ = raised(scores)
        out, total = weighted(powers, kv[:, HW + cols.start : HW + cols.stop])
        attended.append((out / total).astype(BF16))
    f = first_of(early_rows[...], jnp.concatenate(attended, axis=1), out_self, mods(2))
    first[...] = f
    meanwhile(3)
    normed_f = modulated(f, mods(3), mods(4))
    meanwhile(3)
    raw = [dot(normed_f, qkv_cross[:, at : at + HW]) for at in range(0, 3 * HW, HW)]
    meanwhile(4)
    first_q[...] = head_norm(raw[0], wide_gain(gains_cross[0:1]), ones)
    first_k[...] = head_norm(raw[1], wide_gain(gains_cross[1:2]), ones)
    first_v[...] = raw[2].astype(BF16)
    meanwhile(4 * HW)


def far_keys(rows, held, qkv_self, gains):
    mods = mods_held(held, 0)
    normed = modulated(rows, mods(0), mods(1))
    keys = dot(normed, qkv_self[:, HW : 2 * HW])
    values = dot(normed, qkv_self[:, 2 * HW :]).astype(BF16)
    return head_norm(keys, wide_gain(gains[1:2]), head_ones()), values


def far_bias(rows, block_start, outermost):
    place = lax.axis_index("tm")
    below = -2 * BLOCK if outermost else -BLOCK
    start = jnp.where(lax.rem(place, 2) == 0, below, rows + (BLOCK if outermost else 0))
    total = rows * lax.axis_size("tm")
    return window_bias(BLOCK, start - block_start + HALF, place * rows + start, total)


def far_attend(block, bias, query, keys, values, part_out, part_sum, part_top, attended):
    to = slice(block * BLOCK, (block + 1) * BLOCK)
    scores = [window_scores(query[to, cols], keys[:, cols], bias) for cols in SLABS]
    powers = [raised(each) for each in scores]
    sums = [weighted(each, values[:, cols]) for (each, _), cols in zip(powers, SLABS)]
    for cols, (_, top), (out, summed) in zip(SLABS, powers, sums):
        top = by_head(jnp.broadcast_to(top, (2 * BLOCK, SLAB)))
        both = jnp.maximum(top, part_top[to, cols])
        here = jnp.exp(top - both)
        before = jnp.exp(part_top[to, cols] - both)
        out = out * here + part_out[to, cols] * before
        summed = summed * here + part_sum[to, cols] * before
        attended[:, cols] = (out / summed).astype(BF16)


def far_inner_kernel(rows, held, far, qkv_self, gains, query, *refs):
    *parts, attended, kv = refs
    keys, values = far_keys(far[...], held, qkv_self, gains)
    far_attend(1, far_bias(rows, rows - HALF, False), query, keys, values, *parts, attended)
    kv[:, :HW], kv[:, HW:] = keys, values


def far_outer_kernel(rows, early_values, held, far, qkv_self, gains, query, *refs):
    *parts, kv, attended, passed = refs
    passed[...] = early_values[...]
    keys, values = far_keys(far[...], held, qkv_self, gains)
    keys = jnp.concatenate([kv[:, :HW], keys], axis=0)
    values = jnp.concatenate([kv[:, HW:], values], axis=0)
    start = lax.rem(lax.axis_index("tm"), 2) * HALF
    bias = [far_bias(rows, start, outermost) for outermost in (False, True)]
    far_attend(0, jnp.concatenate(bias, axis=1), query, keys, values, *parts, attended)


def first_of(frames, attended, weight, gate):
    mixed = dot(attended, weight[...])
    return (frames.astype(F32) + gate * mixed).astype(BF16)


def projected_cross(first, mods, weight, gains, ones, with_query):
    normed = modulated(first, mods(3), mods(4))
    raw = [dot(normed, weight[:, at : at + HW]) for at in range(0 if with_query else HW, 3 * HW, HW)]
    query = head_norm(raw[0], wide_gain(gains[0:1]), ones) if with_query else None
    keys = head_norm(raw[-2], wide_gain(gains[1:2]), ones)
    return query, keys, raw[-1].astype(BF16)


def finished(first, attended, weight, gate):
    out = dot(attended, weight[...]).astype(BF16)
    return (first.astype(F32) + gate * out.astype(F32)).astype(BF16)


def own_kernel(held, frames, inner, outer, out_self, qkv_cross, gains, *refs):
    first, query, kv = refs[-3:]
    mods = mods_held(held, 0)
    ones = head_ones()
    parts = [slice(0, BLOCK), slice(BLOCK, HALF)]
    mixed = [dot(attended[...], out_self[...]) for attended in (outer, inner)]
    gains = [wide_gain(gains[i : i + 1]) for i in range(2)]

    def normed(n):
        f = (frames[parts[n]].astype(F32) + mods(2) * mixed[n]).astype(BF16)
        first[parts[n]] = f
        return modulated(f, mods(3), mods(4))

    rows = normed(0)
    for n, part in enumerate(parts):
        raw = [dot(rows, qkv_cross[:, at : at + HW]) for at in (2 * HW, 0, HW)]
        if n + 1 < len(parts):
            rows = normed(n + 1)
        kv[part, HW:] = raw[0].astype(BF16)
        query[part] = head_norm(raw[1], gains[0], ones)
        kv[part, :HW] = head_norm(raw[2], gains[1], ones)


def late_block(block, held, first, query, kv, others, their_frames, out_self, qkv_cross, gains, out_cross):
    ones = head_ones()
    part = slice(block * BLOCK, (block + 1) * BLOCK)
    keys, values = [kv[part, :HW]], [kv[part, HW:]]
    for n, (attended, source) in enumerate(zip(others, their_frames)):
        mods = mods_held(held, n + 1)
        g = first_of(source[part], attended[...], out_self, mods(2))
        _, k, v = projected_cross(g, mods, qkv_cross, gains, ones, False)
        keys.append(k)
        values.append(v)
    mixed = cross_sum(cross_weights(query[part], keys, ones), values)
    return finished(first[part], mixed, out_cross, mods_held(held, 0)(5))


def late_kernel(block, count, held, first, query, kv, *refs):
    others, their_frames = refs[: count - 1], refs[count - 1 : 2 * count - 2]
    *weights, out = refs[2 * count - 2 :]
    out[...] = late_block(block, held, first, query, kv, others, their_frames, *weights)


def weights_kernel(_, query, *refs):
    keys, out = refs[:-1], refs[-1]
    for n, each in enumerate(cross_weights(query[...], [k[...] for k in keys], head_ones())):
        out[n] = each


def early_kernel(count, held, inner_out, outer_out, out_cross, first, weights, *refs):
    values = refs[:count]
    out, early_out, sems = refs[count:]
    _, outer, inner, early = places(out.shape[1])
    copies = [
        pltpu.make_async_copy(source, out.at[0, pl.ds(at, BLOCK)], sems.at[n])
        for n, (source, at) in enumerate(((inner_out, inner), (outer_out, outer)))
    ]
    for n in range(2):
        to = out.at[0, pl.ds(early, BLOCK), pl.ds(n * HW, HW)]
        copies.append(pltpu.make_async_copy(early_out.at[n], to, sems.at[2 + n]))
    copies[0].start()
    copies[1].start()
    mixed = cross_sum([weights[n] for n in range(count)], [v[...] for v in values])
    gate = mods_held(held, 0)(5)
    for n in range(2):
        cols = slice(n * HW, (n + 1) * HW)
        early_out[n] = finished(first[:, cols], mixed, out_cross.at[:, cols], gate[:, cols])
        copies[2 + n].start()
    for copy in copies:
        copy.wait()


def on_device(
    frames,
    timestep,
    modulation,
    qkv_self,
    out_self,
    qk_gain_self,
    qkv_cross,
    out_cross,
    qk_gain_cross,
):
    stems = lax.axis_size("stem")
    count = lax.axis_size("tm")
    rows = frames.shape[1]
    assert count % 2 == 0 and rows == HALF + BLOCK
    modulation = jnp.transpose(modulation, (1, 0, 2))
    inside = [(i, i ^ 1) for i in range(count)]
    across = [(i, i + 2) for i in range(0, count - 2, 2)]
    across += [(i + 3, i + 1) for i in range(0, count - 2, 2)]
    across += [(count - 2, count - 1), (1, 0)]

    def to_stems(array):
        return [
            lax.ppermute(array, "stem", [(i, (i + k) % stems) for i in range(stems)])
            for k in range(1, stems)
        ]

    def call(kernel, name, us, outs, *args, scratch=(), in_specs=None, out_specs=None):
        out_specs = out_specs or jax.tree.map(lambda _: VMEM, outs)
        return pl.pallas_call(
            kernel,
            out_shape=outs,
            in_specs=in_specs or [VMEM] * len(args),
            out_specs=out_specs,
            scratch_shapes=list(scratch),
            compiler_params=params(),
            cost_estimate=cost(us),
            name=name,
        )(*args)

    half = shape(BLOCK, D)
    late_rows, early_rows = call(
        split_kernel, "split", 4, (shape(HALF, D), half), frames,
        scratch=[pltpu.SemaphoreType.DMA((3,))], in_specs=[ANY], out_specs=(ANY, ANY),
    )
    their_frames = to_stems(late_rows)
    near = lax.ppermute(frames, "tm", inside)
    mate_outer, mate_inner = call(mate_kernel, "mate", 0.1, (half, half), near)
    far = lax.ppermute(mate_outer, "tm", across)
    farther = lax.ppermute(mate_inner, "tm", across)

    late, block, part = shape(HALF, HW), shape(BLOCK, HW), shape(HALF, HW, dtype=F32)
    query, part_out, part_sum, part_top, first_early, q_early, k_early, v_early, held = call(
        near_kernel, "near", 0.12,
        (late, part, part, part, half, block, block, block, shape(stems, 8, D, dtype=F32)),
        timestep.reshape(1, -1), modulation, early_rows, late_rows, near, qkv_self, qk_gain_self, out_self, qkv_cross, qk_gain_cross,
        scratch=[pltpu.VMEM((rows + HALF, 2 * HW), BF16)],
    )
    their_keys = to_stems(k_early)
    parts = (part_out, part_sum, part_top)

    self_weights = (qkv_self, qk_gain_self)
    att_inner, far_kv = call(
        lambda *refs: far_inner_kernel(rows, *refs), "far_inner", 0.04, (block, half),
        held, far, *self_weights, query, *parts,
    )
    others_inner = to_stems(att_inner)
    att_outer, passed = call(
        lambda *refs: far_outer_kernel(rows, *refs), "far_outer", 0.006, (block, block),
        v_early, held, farther, *self_weights, query, *parts, far_kv,
    )
    others_outer = to_stems(att_outer)
    their_values = to_stems(passed)

    weights = (out_self, qkv_cross, qk_gain_cross)
    own = call(
        own_kernel, "own", 0.02, (shape(HALF, D), late, shape(HALF, D)),
        held, late_rows, att_inner, att_outer, *weights, *their_keys,
        in_specs=[VMEM] * 7 + [ANY] * (stems - 1),
    )
    inner_out = call(
        lambda *refs: late_kernel(1, stems, *refs), "inner", 0.04, half,
        held, *own, *others_inner, *their_frames, *weights, out_cross,
    )
    early_weights = call(
        weights_kernel, "weights", 0.02, shape(stems, BLOCK, HW),
        inner_out, q_early, k_early, *their_keys,
        in_specs=[ANY] + [VMEM] * (1 + stems),
    )
    outer_out = call(
        lambda _, *refs: late_kernel(0, stems, *refs), "outer", 0.04, half,
        early_weights, held, *own, *others_outer, *their_frames, *weights, out_cross,
        in_specs=[ANY] + [VMEM] * (6 + 2 * stems),
    )
    return call(
        lambda *refs: early_kernel(stems, *refs), "early", 2, shape(1, rows, D),
        held, inner_out, outer_out, out_cross, first_early, early_weights, v_early, *their_values,
        scratch=[pltpu.VMEM((2, BLOCK, HW), BF16), pltpu.SemaphoreType.DMA((4,))], out_specs=ANY,
    )


def solution(mesh):
    return jax.shard_map(
        on_device,
        mesh=mesh,
        in_specs=(P("stem", "tm", None), P(), P(), P(), P(), P(), P(), P(), P()),
        out_specs=P("stem", "tm", None),
        check_vma=False,
    )
```

```python
import jax
import jax.numpy as jnp
from jax import lax
from jax.experimental import pallas as pl
from jax.experimental.pallas import tpu as pltpu
from jax.sharding import PartitionSpec as P

D = 1024
H = 8
HD = 64
HW = H * HD
HALF = 256
BLOCK = 128
SLAB = 128
EPS = 1e-06
NEG = -1e30
F32 = jnp.float32
BF16 = jnp.bfloat16
VMEM = pl.BlockSpec(memory_space=pltpu.VMEM)
ANY = pl.BlockSpec(memory_space=pl.ANY)
LIMIT = 16 * 1024 * 1024


def cost(us):
    return pl.CostEstimate(flops=int(us * 1e9), bytes_accessed=int(us * 3e6), transcendentals=0)


def params():
    return pltpu.CompilerParams(vmem_limit_bytes=LIMIT)


def shape(*dims, dtype=BF16):
    return jax.ShapeDtypeStruct(dims, dtype)


def dot(a, b, dims=((1,), (0,))):
    return lax.dot_general(a, b, (dims, ((), ())), preferred_element_type=F32)


def modulated(rows, shift, scale):
    values = rows.astype(F32)
    centred = values - jnp.mean(values, axis=-1, keepdims=True)
    spread = jnp.mean(centred * centred, axis=-1, keepdims=True)
    normed = centred * lax.rsqrt(spread + EPS)
    return (normed * (1.0 + scale) + shift).astype(BF16)


def head_ones():
    row = lax.broadcasted_iota(jnp.int32, (2 * SLAB, 2 * SLAB), 0) // HD
    col = lax.broadcasted_iota(jnp.int32, (2 * SLAB, 2 * SLAB), 1) // HD
    return jnp.where(row == col, 1.0, 0.0).astype(BF16)


def head_sums(values, ones):
    parts = [dot(values[:, at : at + 2 * SLAB], ones) for at in range(0, HW, 2 * SLAB)]
    return jnp.concatenate(parts, axis=1)


def exact_head_sums(values, ones):
    high = values.astype(BF16)
    low = (values - high.astype(F32)).astype(BF16)
    return head_sums(high, ones) + head_sums(low, ones)


def head_norm(values, gain, ones):
    mean = head_sums((values * values).astype(BF16), ones) * (1.0 / HD)
    return (values * lax.rsqrt(mean + EPS) * gain).astype(BF16)


def wide_gain(gain):
    return jnp.concatenate([gain] * H, axis=1)


def window_bias(keys, ahead, first_frame=0, total=1 << 30):
    i = lax.broadcasted_iota(jnp.int32, (BLOCK, keys), 0)
    j = lax.broadcasted_iota(jnp.int32, (BLOCK, keys), 1)
    frame = first_frame + j
    keep = (j + ahead >= i) & (j + ahead <= i + 2 * HALF) & (frame >= 0) & (frame < total)
    return jnp.where(keep, 0.0, NEG)


def left_half():
    return lax.broadcasted_iota(jnp.int32, (BLOCK, SLAB), 1) < HD


def by_head(pair):
    return jnp.where(left_half(), pair[:BLOCK], pair[BLOCK:])


def window_scores(query, keys, bias):
    half, zero = left_half(), jnp.zeros_like(query)
    pair = jnp.concatenate([jnp.where(half, query, zero), jnp.where(half, zero, query)], axis=0)
    scores = dot(pair, keys, ((1,), (1,)))
    return jnp.concatenate([scores[:BLOCK] + bias, scores[BLOCK:] + bias], axis=0)


def raised(scores):
    top = jnp.max(scores, axis=-1, keepdims=True)
    return jnp.exp(scores - top).astype(BF16), top


def weighted(powers, values):
    summed = dot(powers, jnp.concatenate([values, jnp.ones_like(values)], axis=1))
    return by_head(summed[:, :SLAB]), by_head(summed[:, SLAB:])


SLABS = [slice(at, at + SLAB) for at in range(0, HW, SLAB)]


def cross_weights(query, keys, ones):
    query = query.astype(F32)
    base = keys[0].astype(F32)
    scores = [
        exact_head_sums(query * (k.astype(F32) - base), ones) * (HD ** -0.5) for k in keys[1:]
    ]
    top = jnp.zeros_like(query)
    for s in scores:
        top = jnp.maximum(top, s)
    powers = [jnp.exp(-top)] + [jnp.exp(s - top) for s in scores]
    total = powers[0]
    for p in powers[1:]:
        total = total + p
    scale = 1.0 / total
    return [(p * scale).astype(BF16) for p in powers]


def cross_sum(weights, values):
    out = jnp.zeros(values[0].shape, F32)
    for w, v in zip(weights, values):
        out = out + w.astype(F32) * v.astype(F32)
    return out.astype(BF16)


def mods_of(timestep, modulation, back):
    count = lax.axis_size("stem")
    stem = lax.rem(lax.axis_index("stem") + count - back, count)
    at = lax.broadcasted_iota(jnp.int32, (1, count), 1)
    step = jnp.sum(jnp.where(at == stem, timestep[...], 0).astype(F32), axis=1, keepdims=True)
    rows = lax.broadcasted_iota(jnp.int32, (modulation.shape[1], 1), 0).astype(F32)
    picked = rows == step
    return [
        jnp.sum(jnp.where(picked, modulation[i], 0.0), axis=0, keepdims=True) for i in range(6)
    ]


def mods_held(held, back):
    return lambda i: held[back, i : i + 1]


def places(rows):
    parity = lax.rem(lax.axis_index("tm"), 2)
    outer = pl.multiple_of(parity * HALF, BLOCK)
    early = pl.multiple_of((1 - parity) * HALF, BLOCK)
    return parity, outer, rows - HALF, early


def split_kernel(frames, late_rows, sems):
    _, outer, inner, _ = places(frames.shape[1])
    copies = [
        pltpu.make_async_copy(
            frames.at[0, pl.ds(at, BLOCK)], late_rows.at[pl.ds(n * BLOCK, BLOCK)], sems.at[n]
        )
        for n, at in enumerate((outer, inner))
    ]
    for copy in copies:
        copy.start()
    for copy in copies:
        copy.wait()


def mate_kernel(mate, outer_rows, inner_rows):
    _, _, inner, outer = places(mate.shape[1])
    outer_rows[...] = mate[0, pl.ds(outer, BLOCK)]
    inner_rows[...] = mate[0, inner : inner + BLOCK]


def part_steps(block, query, kv, part_out, part_sum, part_top):
    parity = lax.rem(lax.axis_index("tm"), 2)
    width = (HALF, BLOCK)[block]
    start = pl.multiple_of(parity * width, BLOCK)
    count = kv.shape[0] - width
    bias = window_bias(count, (1 - parity) * width)
    to = slice(block * BLOCK, (block + 1) * BLOCK)
    for cols in SLABS:
        scores = window_scores(query[:, cols], kv[pl.ds(start, count), cols], bias)
        yield
        powers, top = raised(scores)
        values = kv[pl.ds(start, count), HW + cols.start : HW + cols.stop]
        part_out[to, cols], part_sum[to, cols] = weighted(powers, values)
        part_top[to, cols] = by_head(jnp.broadcast_to(top, (2 * BLOCK, SLAB)))
        yield


def near_kernel(
    timestep, modulation, frames, late_rows, near, qkv_self, gains, out_self, qkv_cross, gains_cross,
    query, part_out, part_sum, part_top, first, first_q, first_k, first_v, held, kv, early_rows, sem,
):
    rows = near.shape[1]
    copy = pltpu.make_async_copy(frames.at[0, pl.ds(places(rows)[3], BLOCK)], early_rows, sem)
    copy.start()

    def hold(k):
        for i, row in enumerate(mods_of(timestep, modulation, k)):
            held[k, i : i + 1] = row

    hold(0)
    parity, outer, inner, early = places(rows)
    mods = mods_held(held, 0)
    shift, scale = mods(0), mods(1)
    ones = head_ones()
    q_gain = wide_gain(gains[0:1]) * (HD ** -0.5)
    k_gain = wide_gain(gains[1:2])
    own_at = parity * HALF
    near_at = (1 - parity) * rows
    near_from = parity * (rows - HALF)

    sources = [
        (late_rows, 0, own_at + outer),
        (late_rows, BLOCK, own_at + inner),
        (early_rows, 0, own_at + early),
    ]
    for at in range(0, HALF, BLOCK):
        sources.append((near.at[0], pl.multiple_of(near_from + at, BLOCK), near_at + at))

    def normed(n):
        source, at, _ = sources[n]
        if source is early_rows:
            copy.wait()
        return modulated(source[pl.ds(at, BLOCK)], shift, scale)

    queries = []
    rows_n = normed(0)
    for n, (_, _, to) in enumerate(sources):
        at = pl.ds(pl.multiple_of(to, BLOCK), BLOCK)
        columns = (0, HW, 2 * HW) if n < 3 else (HW, 2 * HW)
        raw = [dot(rows_n, qkv_self[:, c : c + HW]) for c in columns]
        if n + 1 < len(sources):
            rows_n = normed(n + 1)
        if n < 3:
            queries.append(head_norm(raw[0], q_gain, ones))
        kv[at, :HW] = head_norm(raw[-2], k_gain, ones)
        kv[at, HW:] = raw[-1].astype(BF16)
    query[:BLOCK] = queries[0]
    query[BLOCK:] = queries[1]
    for k in range(1, held.shape[0]):
        hold(k)

    parts = [part_steps(n, queries[n], kv, part_out, part_sum, part_top) for n in range(2)]

    def meanwhile(steps):
        while steps and parts:
            if next(parts[0], parts) is parts:
                parts.pop(0)
            else:
                steps -= 1

    bias = window_bias(rows + HALF, 0)
    attended = []
    for cols in SLABS:
        scores = window_scores(queries[2][:, cols], kv[:, cols], bias)
        meanwhile(2)
        powers, _ = raised(scores)
        out, total = weighted(powers, kv[:, HW + cols.start : HW + cols.stop])
        attended.append((out / total).astype(BF16))
    f = first_of(early_rows[...], jnp.concatenate(attended, axis=1), out_self, mods(2))
    first[...] = f
    meanwhile(3)
    normed_f = modulated(f, mods(3), mods(4))
    meanwhile(3)
    raw = [dot(normed_f, qkv_cross[:, at : at + HW]) for at in range(0, 3 * HW, HW)]
    meanwhile(4)
    first_q[...] = head_norm(raw[0], wide_gain(gains_cross[0:1]), ones)
    first_k[...] = head_norm(raw[1], wide_gain(gains_cross[1:2]), ones)
    first_v[...] = raw[2].astype(BF16)
    meanwhile(4 * HW)


def far_keys(rows, held, qkv_self, gains):
    mods = mods_held(held, 0)
    normed = modulated(rows, mods(0), mods(1))
    keys = dot(normed, qkv_self[:, HW : 2 * HW])
    values = dot(normed, qkv_self[:, 2 * HW :]).astype(BF16)
    return head_norm(keys, wide_gain(gains[1:2]), head_ones()), values


def far_bias(rows, block_start, outermost):
    place = lax.axis_index("tm")
    below = -2 * BLOCK if outermost else -BLOCK
    start = jnp.where(lax.rem(place, 2) == 0, below, rows + (BLOCK if outermost else 0))
    total = rows * lax.axis_size("tm")
    return window_bias(BLOCK, start - block_start + HALF, place * rows + start, total)


def far_attend(block, bias, query, keys, values, part_out, part_sum, part_top, attended):
    to = slice(block * BLOCK, (block + 1) * BLOCK)
    scores = [window_scores(query[to, cols], keys[:, cols], bias) for cols in SLABS]
    powers = [raised(each) for each in scores]
    sums = [weighted(each, values[:, cols]) for (each, _), cols in zip(powers, SLABS)]
    for cols, (_, top), (out, summed) in zip(SLABS, powers, sums):
        top = by_head(jnp.broadcast_to(top, (2 * BLOCK, SLAB)))
        both = jnp.maximum(top, part_top[to, cols])
        here = jnp.exp(top - both)
        before = jnp.exp(part_top[to, cols] - both)
        out = out * here + part_out[to, cols] * before
        summed = summed * here + part_sum[to, cols] * before
        attended[:, cols] = (out / summed).astype(BF16)


def far_inner_kernel(rows, held, far, qkv_self, gains, query, *refs):
    *parts, attended, kv = refs
    keys, values = far_keys(far[...], held, qkv_self, gains)
    far_attend(1, far_bias(rows, rows - HALF, False), query, keys, values, *parts, attended)
    kv[:, :HW], kv[:, HW:] = keys, values


def far_outer_kernel(rows, early_values, held, far, qkv_self, gains, query, *refs):
    *parts, kv, attended, passed = refs
    passed[...] = early_values[...]
    keys, values = far_keys(far[...], held, qkv_self, gains)
    keys = jnp.concatenate([kv[:, :HW], keys], axis=0)
    values = jnp.concatenate([kv[:, HW:], values], axis=0)
    start = lax.rem(lax.axis_index("tm"), 2) * HALF
    bias = [far_bias(rows, start, outermost) for outermost in (False, True)]
    far_attend(0, jnp.concatenate(bias, axis=1), query, keys, values, *parts, attended)


def first_of(frames, attended, weight, gate):
    mixed = dot(attended, weight[...])
    return (frames.astype(F32) + gate * mixed).astype(BF16)


def projected_cross(first, mods, weight, gains, ones, with_query):
    normed = modulated(first, mods(3), mods(4))
    raw = [dot(normed, weight[:, at : at + HW]) for at in range(0 if with_query else HW, 3 * HW, HW)]
    query = head_norm(raw[0], wide_gain(gains[0:1]), ones) if with_query else None
    keys = head_norm(raw[-2], wide_gain(gains[1:2]), ones)
    return query, keys, raw[-1].astype(BF16)


def finished(first, attended, weight, gate):
    out = dot(attended, weight[...]).astype(BF16)
    return (first.astype(F32) + gate * out.astype(F32)).astype(BF16)


def own_kernel(held, frames, inner, outer, out_self, qkv_cross, gains, *refs):
    first, query, kv = refs[-3:]
    mods = mods_held(held, 0)
    ones = head_ones()
    parts = [slice(0, BLOCK), slice(BLOCK, HALF)]
    mixed = [dot(attended[...], out_self[...]) for attended in (outer, inner)]
    gains = [wide_gain(gains[i : i + 1]) for i in range(2)]

    def normed(n):
        f = (frames[parts[n]].astype(F32) + mods(2) * mixed[n]).astype(BF16)
        first[parts[n]] = f
        return modulated(f, mods(3), mods(4))

    rows = normed(0)
    for n, part in enumerate(parts):
        raw = [dot(rows, qkv_cross[:, at : at + HW]) for at in (2 * HW, 0, HW)]
        if n + 1 < len(parts):
            rows = normed(n + 1)
        kv[part, HW:] = raw[0].astype(BF16)
        query[part] = head_norm(raw[1], gains[0], ones)
        kv[part, :HW] = head_norm(raw[2], gains[1], ones)


def late_block(block, held, first, query, kv, others, their_frames, out_self, qkv_cross, gains, out_cross):
    ones = head_ones()
    part = slice(block * BLOCK, (block + 1) * BLOCK)
    keys, values = [kv[part, :HW]], [kv[part, HW:]]
    for n, (attended, source) in enumerate(zip(others, their_frames)):
        mods = mods_held(held, n + 1)
        g = first_of(source[part], attended[...], out_self, mods(2))
        _, k, v = projected_cross(g, mods, qkv_cross, gains, ones, False)
        keys.append(k)
        values.append(v)
    mixed = cross_sum(cross_weights(query[part], keys, ones), values)
    return finished(first[part], mixed, out_cross, mods_held(held, 0)(5))


def late_kernel(block, count, held, first, query, kv, *refs):
    others, their_frames = refs[: count - 1], refs[count - 1 : 2 * count - 2]
    *weights, out = refs[2 * count - 2 :]
    out[...] = late_block(block, held, first, query, kv, others, their_frames, *weights)


def weights_kernel(_, query, *refs):
    keys, out = refs[:-1], refs[-1]
    for n, each in enumerate(cross_weights(query[...], [k[...] for k in keys], head_ones())):
        out[n] = each


def early_kernel(count, held, inner_out, outer_out, out_cross, first, weights, *refs):
    values = refs[:count]
    out, early_out, sems = refs[count:]
    _, outer, inner, early = places(out.shape[1])
    copies = [
        pltpu.make_async_copy(source, out.at[0, pl.ds(at, BLOCK)], sems.at[n])
        for n, (source, at) in enumerate(((inner_out, inner), (outer_out, outer)))
    ]
    for n in range(2):
        to = out.at[0, pl.ds(early, BLOCK), pl.ds(n * HW, HW)]
        copies.append(pltpu.make_async_copy(early_out.at[n], to, sems.at[2 + n]))
    copies[0].start()
    copies[1].start()
    mixed = cross_sum([weights[n] for n in range(count)], [v[...] for v in values])
    gate = mods_held(held, 0)(5)
    for n in range(2):
        cols = slice(n * HW, (n + 1) * HW)
        early_out[n] = finished(first[:, cols], mixed, out_cross.at[:, cols], gate[:, cols])
        copies[2 + n].start()
    for copy in copies:
        copy.wait()


def on_device(
    frames,
    timestep,
    modulation,
    qkv_self,
    out_self,
    qk_gain_self,
    qkv_cross,
    out_cross,
    qk_gain_cross,
):
    stems = lax.axis_size("stem")
    count = lax.axis_size("tm")
    rows = frames.shape[1]
    assert count % 2 == 0 and rows == HALF + BLOCK
    modulation = jnp.transpose(modulation, (1, 0, 2))
    inside = [(i, i ^ 1) for i in range(count)]
    across = [(i, i + 2) for i in range(0, count - 2, 2)]
    across += [(i + 3, i + 1) for i in range(0, count - 2, 2)]
    across += [(count - 2, count - 1), (1, 0)]

    def to_stems(array):
        return [
            lax.ppermute(array, "stem", [(i, (i + k) % stems) for i in range(stems)])
            for k in range(1, stems)
        ]

    def call(kernel, name, us, outs, *args, scratch=(), in_specs=None, out_specs=None):
        out_specs = out_specs or jax.tree.map(lambda _: VMEM, outs)
        return pl.pallas_call(
            kernel,
            out_shape=outs,
            in_specs=in_specs or [VMEM] * len(args),
            out_specs=out_specs,
            scratch_shapes=list(scratch),
            compiler_params=params(),
            cost_estimate=cost(us),
            name=name,
        )(*args)

    half = shape(BLOCK, D)
    own_rows = pltpu.with_memory_space_constraint(frames, pltpu.HBM)
    late_rows = call(
        split_kernel, "split", 4, shape(HALF, D), own_rows,
        scratch=[pltpu.SemaphoreType.DMA((2,))], in_specs=[ANY], out_specs=ANY,
    )
    their_frames = to_stems(late_rows)
    near = lax.ppermute(frames, "tm", inside)
    mate_outer, mate_inner = call(mate_kernel, "mate", 0.1, (half, half), near)
    far = lax.ppermute(mate_outer, "tm", across)
    farther = lax.ppermute(mate_inner, "tm", across)

    late, block, part = shape(HALF, HW), shape(BLOCK, HW), shape(HALF, HW, dtype=F32)
    query, part_out, part_sum, part_top, first_early, q_early, k_early, v_early, held = call(
        near_kernel, "near", 0.12,
        (late, part, part, part, half, block, block, block, shape(stems, 8, D, dtype=F32)),
        timestep.reshape(1, -1), modulation, own_rows, late_rows, near, qkv_self, qk_gain_self, out_self, qkv_cross, qk_gain_cross,
        scratch=[pltpu.VMEM((rows + HALF, 2 * HW), BF16), pltpu.VMEM((BLOCK, D), BF16), pltpu.SemaphoreType.DMA],
        in_specs=[VMEM] * 2 + [ANY] + [VMEM] * 7,
    )
    their_keys = to_stems(k_early)
    parts = (part_out, part_sum, part_top)

    self_weights = (qkv_self, qk_gain_self)
    att_inner, far_kv = call(
        lambda *refs: far_inner_kernel(rows, *refs), "far_inner", 0.04, (block, half),
        held, far, *self_weights, query, *parts,
    )
    others_inner = to_stems(att_inner)
    att_outer, passed = call(
        lambda *refs: far_outer_kernel(rows, *refs), "far_outer", 0.006, (block, block),
        v_early, held, farther, *self_weights, query, *parts, far_kv,
    )
    others_outer = to_stems(att_outer)
    their_values = to_stems(passed)

    weights = (out_self, qkv_cross, qk_gain_cross)
    own = call(
        own_kernel, "own", 0.02, (shape(HALF, D), late, shape(HALF, D)),
        held, late_rows, att_inner, att_outer, *weights, *their_keys,
        in_specs=[VMEM] * 7 + [ANY] * (stems - 1),
    )
    inner_out = call(
        lambda *refs: late_kernel(1, stems, *refs), "inner", 0.04, half,
        held, *own, *others_inner, *their_frames, *weights, out_cross,
    )
    early_weights = call(
        weights_kernel, "weights", 0.02, shape(stems, BLOCK, HW),
        inner_out, q_early, k_early, *their_keys,
        in_specs=[ANY] + [VMEM] * (1 + stems),
    )
    outer_out = call(
        lambda _, *refs: late_kernel(0, stems, *refs), "outer", 0.04, half,
        early_weights, held, *own, *others_outer, *their_frames, *weights, out_cross,
        in_specs=[ANY] + [VMEM] * (6 + 2 * stems),
    )
    return call(
        lambda *refs: early_kernel(stems, *refs), "early", 2, shape(1, rows, D),
        held, inner_out, outer_out, out_cross, first_early, early_weights, v_early, *their_values,
        scratch=[pltpu.VMEM((2, BLOCK, HW), BF16), pltpu.SemaphoreType.DMA((4,))], out_specs=ANY,
    )


def solution(mesh):
    return jax.shard_map(
        on_device,
        mesh=mesh,
        in_specs=(P("stem", "tm", None), P(), P(), P(), P(), P(), P(), P(), P()),
        out_specs=P("stem", "tm", None),
        check_vma=False,
    )
```
